32 devices in a mesh: lat: 4 (over z), lon: 4 (over y, core), tm: 2 (over x).
Axes of the slice: x: 2, y: 2, z: 4, core: 2. Of those that a mesh axis runs over, the one named last changes fastest.
Arguments:
- gradient: float32 [56, 64, 1024], P('tm', 'lat', 'lon'), may hold values from -6 to 6
- control: float32 [56, 64, 1024], P('tm', 'lat', 'lon'), may hold values from -6 to 6
- diffusivity: float32 [64, 1024], P('lat', 'lon'), may hold values from 0.03 to 0.24
- land_mask: int32 [64, 1024], P('lat', 'lon'), may hold values 0 or 1
- time_corr: float32 [56, 56], replicated, may hold values from -0.35 to 1.35
- pair_steps: bfloat16 [8, 56, 64, 1024], P(None, 'tm', 'lat', 'lon'), may hold values from -12 to 12
- pair_grads: bfloat16 [8, 56, 64, 1024], P(None, 'tm', 'lat', 'lon'), may hold values from -24 to 24
Outputs:
- next_control: float32 [56, 64, 1024], P('tm', 'lat', 'lon')
The draws below stay inside these ranges and needn't reach their ends.
All inputs are finite; a program needn't handle non-finite values. No bound on the sum of `land_mask` on one device may be relied on, other than what follows from the above.
Results may differ from the reference program's by a relative error of at most 0.0003.
Values sent between devices are 32-bit elements; how exact they have to be, the bound alone decides.
No kernel may reach another device: no remote copies, remote signals or barrier semaphores. Data moves between devices by JAX's collectives and lax.ppermute only.
A program may use at most 64 MiB of HBM per device.

```python
import math
import jax
import jax.numpy as jnp
from jax import lax

NT = 56
PAIRS = 8
SWEEPS = 6
NLAT = 64
NLON = 1024


def base_noise(key, salt, shape):
    inner = jax.random.fold_in(key, salt)
    return jax.random.normal(inner, shape, jnp.float32)


def rough_noise(key, salt, shape):
    return jnp.clip(base_noise(key, salt, shape), -5.0, 5.0)


def box_three(values, axis):
    return jnp.roll(values, -1, axis=axis) + values + jnp.roll(values, 1, axis=axis)


def common_field(key):
    values = base_noise(key, 11, (NT, NLAT, NLON))
    values = box_three(values, 0)
    values = box_three(values, 1)
    values = box_three(values, 2)
    return jnp.clip(values * (1.0 / math.sqrt(27.0)), -5.0, 5.0)


def ramp_field():
    rows = 0.6 + 1.2 * jnp.arange(NLAT, dtype=jnp.float32)[:, None] / NLAT
    return rows * jnp.ones((1, NLON), jnp.float32)


def pair_base(key):
    common = common_field(key)
    own = rough_noise(key, 12, (PAIRS, NT, NLAT, NLON))
    return jnp.clip(ramp_field() * (0.6 * common[None] + 0.8 * own), -12.0, 12.0)


def draw_gradient(key, part):
    common = common_field(key)
    return jnp.clip(0.6 * common + 0.8 * rough_noise(key, 15, (NT, NLAT, NLON)), -6.0, 6.0)


def draw_time_corr(key, part):
    return jnp.eye(NT, dtype=jnp.float32) + 0.07 * rough_noise(key, 16, (NT, NT))


def draw_pair_steps(key, part):
    return pair_base(key).astype(jnp.bfloat16)


def draw_pair_grads(key, part):
    steps = pair_base(key)
    shape = (PAIRS, NT, NLAT, NLON)
    factor = jnp.exp(jax.random.uniform(jax.random.fold_in(key, 13), shape, jnp.float32, -0.916, 0.916))
    grads = factor * steps + 0.5 * rough_noise(key, 14, shape)
    return jnp.clip(grads, -24.0, 24.0).astype(jnp.bfloat16)


def touch_ends(drawn, rng, low, top_value):
    place = [jax.random.randint(jax.random.fold_in(rng, axis), (), 0, length) for axis, length in enumerate(drawn.shape)]
    widest = drawn.shape.index(max(drawn.shape))
    beside = place[:widest] + [(place[widest] + 1) % drawn.shape[widest]] + place[widest + 1:]
    return drawn.at[tuple(place)].set(low).at[tuple(beside)].set(top_value)


def block_levels(rng, shape, split, least, high):
    loudness = 1.0
    for dim, blocks in split:
        heights = jax.random.uniform(jax.random.fold_in(jax.random.fold_in(rng, 6), dim), (blocks,), jnp.float32, least / len(split), high / len(split))
        loudness = loudness * jnp.repeat(jnp.exp(heights), shape[dim] // blocks).reshape((-1,) + (1,) * (len(shape) - 1 - dim))
    return loudness


def gaussian(key, shape, scale, limit, cuts=(), kind=jnp.bfloat16):
    drawn = jax.random.normal(key, shape, jnp.float32) * scale
    if len(cuts) > 0:
        drawn = block_levels(key, shape, cuts, -0.22, 0.18) * drawn
    return jnp.clip(drawn, min=-limit, max=limit).astype(kind)


def setup_inputs(seed: int = 0) -> dict:
    key_list = jax.random.split(jax.random.key(seed), 8)
    gradient = draw_gradient(jax.random.fold_in(key_list[7], 71), 0)
    control = gaussian(key_list[1], (NT, NLAT, NLON), 1.0, 6.0, ((0, 2), (1, 4), (2, 4)), jnp.float32)
    diffusivity = jnp.clip(jnp.exp(math.log(0.24) - 2.0794415 * jax.random.uniform(key_list[2], (NLAT, NLON), jnp.float32) ** block_levels(key_list[2], (NLAT, NLON), ((0, 4), (1, 4)), -0.2, 0.2)), 0.03, 0.24)
    land_mask = touch_ends((jax.random.randint(key_list[3], (NLAT, NLON), 0, 4) < 3).astype(jnp.int32), jax.random.fold_in(key_list[3], 1), 0, 1)
    time_corr = draw_time_corr(jax.random.fold_in(key_list[7], 71), 0)
    pair_steps = draw_pair_steps(jax.random.fold_in(key_list[7], 71), 0)
    pair_grads = draw_pair_grads(jax.random.fold_in(key_list[7], 71), 0)
    return {"gradient": gradient, "control": control, "diffusivity": diffusivity, "land_mask": land_mask, "time_corr": time_corr, "pair_steps": pair_steps, "pair_grads": pair_grads}


def pad_grid(values):
    widths = [(0, 0)] * (values.ndim - 2) + [(1, 1), (0, 0)]
    padded = jnp.pad(values, widths)
    return jnp.concatenate([padded[..., -1:], padded, padded[..., :1]], axis=-1)


def stencil(padded, kappa_pad):
    centre = padded[..., 1:-1, 1:-1]
    kc = kappa_pad[1:-1, 1:-1]
    north = 0.5 * (kc + kappa_pad[:-2, 1:-1]) * (padded[..., :-2, 1:-1] - centre)
    south = 0.5 * (kc + kappa_pad[2:, 1:-1]) * (padded[..., 2:, 1:-1] - centre)
    west = 0.5 * (kc + kappa_pad[1:-1, :-2]) * (padded[..., 1:-1, :-2] - centre)
    east = 0.5 * (kc + kappa_pad[1:-1, 2:]) * (padded[..., 1:-1, 2:] - centre)
    return centre + north + south + west + east


def solve_upper(upper, target):
    result = jnp.zeros_like(target)
    for position in reversed(range(PAIRS)):
        remainder = target[position] - jnp.sum(upper[position] * result)
        result = result.at[position].set(remainder / upper[position, position])
    return result


def solve_upper_transposed(upper, target):
    result = jnp.zeros_like(target)
    for position in range(PAIRS):
        remainder = target[position] - jnp.sum(upper[:, position] * result)
        result = result.at[position].set(remainder / upper[position, position])
    return result


def compact(cross, square, proj_s, proj_y, count):
    index = jnp.arange(PAIRS, dtype=jnp.int32)
    valid = (index < count).astype(jnp.float32)
    last = (index == count - 1).astype(jnp.float32)
    curve = jnp.diagonal(cross)
    gamma = jnp.sum(last * curve) / jnp.sum(last * jnp.diagonal(square))
    pair_mask = valid[:, None] * valid[None, :]
    upper = jnp.triu(cross) * pair_mask + jnp.diag(1.0 - valid)
    first = solve_upper(upper, proj_s * valid)
    middle = jnp.diag(curve * valid) + gamma * square * pair_mask
    target = jnp.dot(middle, first, precision=lax.Precision.HIGHEST) - gamma * proj_y * valid
    second = solve_upper_transposed(upper, target)
    return gamma, first, second


def reference(gradient, control, diffusivity, land_mask, time_corr, pair_steps, pair_grads):
    field = gradient * land_mask.astype(jnp.float32)[None]
    kappa_pad = pad_grid(diffusivity)
    for sweep in range(SWEEPS):
        field = stencil(pad_grid(field), kappa_pad)
    control_grad = jnp.einsum("st,sab->tab", time_corr, field, precision=lax.Precision.HIGHEST)
    grad_half = control_grad.astype(jnp.bfloat16)

    def accumulate(step, carry):
        cross, square, proj_s, proj_y = carry
        steps_t = lax.dynamic_index_in_dim(pair_steps, step, 1, keepdims=False).reshape(PAIRS, -1)
        grads_t = lax.dynamic_index_in_dim(pair_grads, step, 1, keepdims=False).reshape(PAIRS, -1)
        grad_t = lax.dynamic_index_in_dim(grad_half, step, 0, keepdims=False).reshape(-1)
        dims = (((1,), (1,)), ((), ()))
        cross = cross + lax.dot_general(steps_t, grads_t, dims, preferred_element_type=jnp.float32)
        square = square + lax.dot_general(grads_t, grads_t, dims, preferred_element_type=jnp.float32)
        proj_s = proj_s + jnp.dot(steps_t, grad_t, preferred_element_type=jnp.float32)
        proj_y = proj_y + jnp.dot(grads_t, grad_t, preferred_element_type=jnp.float32)
        return cross, square, proj_s, proj_y

    start = (jnp.zeros((PAIRS, PAIRS), jnp.float32), jnp.zeros((PAIRS, PAIRS), jnp.float32),
             jnp.zeros((PAIRS,), jnp.float32), jnp.zeros((PAIRS,), jnp.float32))
    cross, square, proj_s, proj_y = lax.fori_loop(0, NT, accumulate, start)
    gamma, first, second = compact(cross, square, proj_s, proj_y, PAIRS)
    update = gamma * control_grad
    for index in range(PAIRS):
        update = update + second[index] * pair_steps[index].astype(jnp.float32)
        update = update - gamma * first[index] * pair_grads[index].astype(jnp.float32)
    return control - update
```

```python
import jax
import jax.numpy as jnp
from jax import lax
from jax.experimental import pallas as pl
from jax.experimental.pallas import tpu as pltpu
from jax.sharding import PartitionSpec as P

PAIRS = 8
SWEEPS = 6
SUB = 8
LANE = 128
GROUP = 8
PER = LANE // GROUP
CROSS = [(i, j) for i in range(PAIRS) for j in range(i, PAIRS)]
NSYM = len(CROSS)
WHERE = {pair: k for k, pair in enumerate(CROSS)}
NGRAM = 2 * NSYM
NPROJ = 2 * PAIRS
NROW = NGRAM + NPROJ
CHUNKS = 2

VMEM = pl.BlockSpec(memory_space=pltpu.VMEM)
SMEM = pl.BlockSpec(memory_space=pltpu.SMEM)
PARAMS = pltpu.CompilerParams(vmem_limit_bytes=48 * 1024 * 1024)


def f32(*shape):
    return jax.ShapeDtypeStruct(shape, jnp.float32)


def call(kernel, outs, args, specs=None, scratch=(), name=None):
    single = not isinstance(outs, (tuple, list))
    return pl.pallas_call(
        kernel,
        out_shape=outs,
        in_specs=specs or [VMEM] * len(args),
        out_specs=VMEM if single else [VMEM] * len(outs),
        scratch_shapes=list(scratch),
        compiler_params=PARAMS,
        name=name,
    )(*args)


def lane_index():
    return lax.broadcasted_iota(jnp.int32, (SUB, LANE), 1)


def row_index():
    return lax.broadcasted_iota(jnp.int32, (SUB, LANE), 0)


def pack_kernel(grad_ref, mask_ref, diff_ref, masked_ref, first_ref, last_ref, west_ref, east_ref):
    steps, rows, cols = grad_ref.shape
    mask = mask_ref[...].astype(jnp.float32)
    lane = lane_index()
    zero = jnp.zeros((SUB, LANE), jnp.float32)
    tiles = rows // SUB
    for base in range(0, steps + 1, PER):
        west = [zero] * tiles
        east = [zero] * tiles
        for step in range(base, min(base + PER, steps + 1)):
            value = grad_ref[step] * mask if step < steps else diff_ref[...]
            if step < steps:
                masked_ref[step] = value
            first_ref[step] = value[:SUB]
            last_ref[step] = value[rows - SUB:]
            start = (step - base) * GROUP
            here = (lane >= start) & (lane < start + GROUP)
            for r in range(tiles):
                left = value[r * SUB:(r + 1) * SUB, :LANE]
                right = value[r * SUB:(r + 1) * SUB, cols - LANE:]
                west[r] = jnp.where(here, pltpu.roll(left, start, 1) if start else left, west[r])
                turn = (start + GROUP) % LANE
                east[r] = jnp.where(here, pltpu.roll(right, turn, 1) if turn else right, east[r])
        place = base // PER * LANE
        for r in range(tiles):
            west_ref[r * SUB:(r + 1) * SUB, place:place + LANE] = west[r]
            east_ref[r * SUB:(r + 1) * SUB, place:place + LANE] = east[r]


def load_tiles(step, slot, own, above, below, left_ref, right_ref, up_ref, down_ref, lane):
    rows, cols = own.shape
    tiles = [above, *(own[r * SUB:(r + 1) * SUB] for r in range(rows // SUB)), below]
    group = lax.rem(step, PER) if not isinstance(step, int) else step % PER
    block = lax.div(step, PER) if not isinstance(step, int) else step // PER
    place = pl.multiple_of(block * LANE, LANE) if not isinstance(step, int) else block * LANE
    to_left = lax.rem(LANE - group * GROUP, LANE) if not isinstance(step, int) else (LANE - group * GROUP) % LANE
    to_right = lax.rem(2 * LANE - GROUP - group * GROUP, LANE) if not isinstance(step, int) else (2 * LANE - GROUP - group * GROUP) % LANE
    sides = [(up_ref, 0, up_ref, SUB)]
    sides += [(left_ref, r * SUB, right_ref, r * SUB) for r in range(rows // SUB)]
    sides += [(down_ref, 0, down_ref, SUB)]
    result = []
    for tile, (lref, lrow, rref, rrow) in zip(tiles, sides):
        west = pltpu.roll(lref[lrow:lrow + SUB, pl.ds(place, LANE)], to_right, 1)
        east = pltpu.roll(rref[rrow:rrow + SUB, pl.ds(place, LANE)], to_left, 1)
        extra = jnp.where(lane < LANE // 2, east, west)
        result.append([tile[:, c * LANE:(c + 1) * LANE] for c in range(cols // LANE)] + [extra])
    return result


def shifted(tiles, r, c, kind, masks):
    height, width = len(tiles), len(tiles[0])
    if kind == "w":
        return jnp.where(masks[0], pltpu.roll(tiles[r][(c - 1) % width], 1, 1), pltpu.roll(tiles[r][c], 1, 1))
    if kind == "e":
        return jnp.where(masks[1], pltpu.roll(tiles[r][(c + 1) % width], LANE - 1, 1), pltpu.roll(tiles[r][c], LANE - 1, 1))
    if kind == "n":
        return jnp.where(masks[2], pltpu.roll(tiles[(r - 1) % height][c], 1, 0), pltpu.roll(tiles[r][c], 1, 0))
    return jnp.where(masks[3], pltpu.roll(tiles[(r + 1) % height][c], SUB - 1, 0), pltpu.roll(tiles[r][c], SUB - 1, 0))


def make_sweep_kernel(begin, count):
    def kernel(masked_ref, diff_ref, above_ref, below_ref, left_ref, right_ref, up_ref, down_ref, out_ref, coef_ref):
        steps, rows, cols = masked_ref.shape
        lane, row = lane_index(), row_index()
        masks = (lane == 0, lane == LANE - 1, row == 0, row == SUB - 1)
        height, width = rows // SUB + 2, cols // LANE + 1
        packed = (left_ref, right_ref, up_ref, down_ref, lane)
        kappa = load_tiles(steps, 0, diff_ref[...], above_ref[steps], below_ref[steps], *packed)
        for r in range(height):
            for c in range(width):
                centre = kappa[r][c]
                inside = centre > 0.0
                total = jnp.ones((SUB, LANE), jnp.float32)
                for n, kind in enumerate("nswe"):
                    part = jnp.where(inside, 0.5 * (centre + shifted(kappa, r, c, kind, masks)), 0.0)
                    total = total - part
                    coef_ref[(r * width + c) * 5 + 1 + n] = part
                coef_ref[(r * width + c) * 5] = total

        def body(offset, carry):
            step = begin + offset
            tiles = load_tiles(step, 0, masked_ref[step], above_ref[step], below_ref[step], *packed)
            for sweep in range(SWEEPS):
                fresh = [list(line) for line in tiles]
                for r in range(height):
                    for c in range(width):
                        if sweep == SWEEPS - 1 and (r in (0, height - 1) or c == width - 1):
                            continue
                        at = (r * width + c) * 5
                        total = coef_ref[at] * tiles[r][c]
                        for n, kind in enumerate("nswe"):
                            total = total + coef_ref[at + 1 + n] * shifted(tiles, r, c, kind, masks)
                        fresh[r][c] = total
                tiles = fresh
            for r in range(1, height - 1):
                for c in range(width - 1):
                    out_ref[offset, (r - 1) * SUB:r * SUB, c * LANE:(c + 1) * LANE] = tiles[r][c]
            return carry

        lax.fori_loop(0, count, body, 0)

    return kernel


def gram_kernel(steps_ref, grads_ref, out_ref):
    _, steps, rows, cols = steps_ref.shape
    for half, left_ref in enumerate((steps_ref, grads_ref)):
        def body(step, sums):
            sums = list(sums)
            for c in range(0, cols, LANE):
                for r in range(0, rows, 2 * SUB):
                    where = (step, pl.ds(r, 2 * SUB), pl.ds(c, LANE))
                    right = [grads_ref[(i, *where)].astype(jnp.float32) for i in range(PAIRS)]
                    left = right if half else [left_ref[(i, *where)].astype(jnp.float32) for i in range(PAIRS)]
                    for part in range(2):
                        cut = slice(part * SUB, (part + 1) * SUB)
                        for k, (i, j) in enumerate(CROSS):
                            sums[k] = sums[k] + left[i][cut] * right[j][cut]
            return tuple(sums)

        zero = jnp.zeros((SUB, LANE), jnp.float32)
        sums = lax.fori_loop(0, steps, body, (zero,) * NSYM)
        for k in range(NSYM):
            out_ref[half * NSYM + k:half * NSYM + k + 1, :] = jnp.sum(sums[k], axis=0, keepdims=True)


def mix_into(corr_ref, row0, col0, field_ref, acc_ref, fresh):
    count, rows, cols = field_ref.shape
    steps = acc_ref.shape[0]
    block = 7
    for begin in range(0, steps, block):
        size = min(block, steps - begin)
        for c in range(0, cols, 2 * LANE):
            for r in range(0, rows, 2 * SUB):
                where = (pl.ds(r, 2 * SUB), pl.ds(c, 2 * LANE))

                def body(s, sums):
                    value = field_ref[(s, *where)]
                    return tuple(
                        sums[k] + corr_ref[row0 + s, col0 + begin + k] * value for k in range(size)
                    )

                start = tuple(
                    jnp.zeros((2 * SUB, 2 * LANE), jnp.float32) if fresh else acc_ref[(begin + k, *where)]
                    for k in range(size)
                )
                sums = lax.fori_loop(0, count, body, start, unroll=2)
                for k in range(size):
                    acc_ref[(begin + k, *where)] = sums[k]


def make_mix_own(parts):
    def kernel(corr_ref, base_ref, *refs):
        out_ref = refs[-1]
        row = base_ref[0]
        for n in range(parts):
            mix_into(corr_ref, row, base_ref[0], refs[n], out_ref, n == 0)
            row = row + refs[n].shape[0]

    return kernel


def make_mix_rest(sources, final):
    parts = len(sources)

    def kernel(corr_ref, base_ref, origin_ref, acc_ref, *refs):
        field_refs = refs[:parts]
        if final:
            gram_ref, steps_ref, grads_ref, out_ref, message_ref, rows_ref = refs[parts:]
        else:
            (out_ref,) = refs[parts:]
        out_ref[...] = acc_ref[...]
        for (shift, offset), field_ref in zip(sources, field_refs):
            mix_into(corr_ref, origin_ref[shift] + offset, base_ref[0], field_ref, out_ref, False)
        if not final:
            return
        _, steps, rows, cols = steps_ref.shape

        def body(step, sums):
            sums = list(sums)
            for c in range(0, cols, LANE):
                for r in range(0, rows, 2 * SUB):
                    where = (step, pl.ds(r, 2 * SUB), pl.ds(c, LANE))
                    half = out_ref[where].astype(jnp.bfloat16).astype(jnp.float32)
                    for n in range(NPROJ):
                        source = steps_ref if n < PAIRS else grads_ref
                        product = source[(n % PAIRS, *where)].astype(jnp.float32) * half
                        sums[n] = sums[n] + (product[:SUB] + product[SUB:])
            return tuple(sums)

        zero = jnp.zeros((SUB, LANE), jnp.float32)
        sums = lax.fori_loop(0, steps, body, (zero,) * NPROJ)
        rows_ref[0:NGRAM, :] = gram_ref[...]
        for n in range(NPROJ):
            rows_ref[NGRAM + n:NGRAM + n + 1, :] = jnp.sum(sums[n], axis=0, keepdims=True)
        lane, row = lane_index(), row_index()
        total = zero
        for first in range(0, NROW, SUB):
            summed = jnp.sum(rows_ref[first:first + SUB, :], axis=1, keepdims=True)
            total = total + jnp.where(lane == row + first, summed, 0.0)
        message = jnp.sum(total, axis=0, keepdims=True)
        message_ref[...] = jnp.broadcast_to(message[None], message_ref.shape)

    return kernel


def final_kernel(inbox_ref, mixed_ref, control_ref, steps_ref, grads_ref, out_ref, rows_ref):
    totals = jnp.sum(inbox_ref[...], axis=0)
    lane, row = lane_index(), row_index()
    spread = jnp.broadcast_to(totals, (SUB, LANE))
    for first in range(0, NROW, SUB):
        picked = jnp.where(lane == row + first, spread, 0.0)
        rows_ref[first:first + SUB, :] = jnp.broadcast_to(jnp.sum(picked, axis=1, keepdims=True), (SUB, LANE))

    def entry(k):
        return jnp.broadcast_to(rows_ref[k:k + 1, :], (SUB, LANE))

    cross = {pair: entry(k) for pair, k in WHERE.items()}

    def square(i, j):
        return entry(NSYM + WHERE[(min(i, j), max(i, j))])

    gamma = cross[(PAIRS - 1, PAIRS - 1)] / square(PAIRS - 1, PAIRS - 1)
    first = [None] * PAIRS
    for i in reversed(range(PAIRS)):
        rest = entry(NGRAM + i)
        for j in reversed(range(i + 1, PAIRS)):
            rest = rest - cross[(i, j)] * first[j]
        first[i] = rest / cross[(i, i)]
    second = [None] * PAIRS
    for i in range(PAIRS):
        inner = -entry(NGRAM + PAIRS + i)
        for j in range(PAIRS):
            inner = inner + square(i, j) * first[j]
        rest = cross[(i, i)] * first[i] + gamma * inner
        for j in range(i):
            rest = rest - cross[(j, i)] * second[j]
        second[i] = rest / cross[(i, i)]
    scaled = [gamma * value for value in first]

    _, steps, rows, cols = steps_ref.shape

    def body(step, carry):
        for c in range(0, cols, LANE):
            for r in range(0, rows, 2 * SUB):
                where = (step, pl.ds(r, 2 * SUB), pl.ds(c, LANE))
                mixed = mixed_ref[where]
                control = control_ref[where]
                update = [gamma * mixed[:SUB], gamma * mixed[SUB:]]
                for i in range(PAIRS):
                    s = steps_ref[(i, *where)].astype(jnp.float32)
                    y = grads_ref[(i, *where)].astype(jnp.float32)
                    for part, cut in enumerate((slice(0, SUB), slice(SUB, 2 * SUB))):
                        update[part] = update[part] + (second[i] * s[cut] - scaled[i] * y[cut])
                out_ref[step, pl.ds(r, SUB), pl.ds(c, LANE)] = control[:SUB] - update[0]
                out_ref[step, pl.ds(r + SUB, SUB), pl.ds(c, LANE)] = control[SUB:] - update[1]
        return carry

    lax.fori_loop(0, steps, body, 0)


def local(gradient, control, diffusivity, land_mask, time_corr, pair_steps, pair_grads):
    steps, rows, cols = gradient.shape
    height, breadth, groups = (lax.axis_size(axis) for axis in ("lat", "lon", "tm"))
    mine = lax.axis_index("tm")
    base = (mine * steps).reshape(1).astype(jnp.int32)
    origin = (lax.rem(mine - jnp.arange(groups, dtype=jnp.int32) + groups, groups) * steps).astype(jnp.int32)
    down = [(i, i + 1) for i in range(height - 1)]
    up = [(i + 1, i) for i in range(height - 1)]
    right = [(i, (i + 1) % breadth) for i in range(breadth)]
    left = [(j, i) for i, j in right]

    packed_width = -(-(steps + 1) // PER) * LANE
    masked, first, last, west, east = call(
        pack_kernel,
        (f32(steps, rows, cols), f32(steps + 1, SUB, cols), f32(steps + 1, SUB, cols), f32(rows, packed_width), f32(rows, packed_width)),
        (gradient, land_mask, diffusivity),
        name="pack",
    )
    from_left = lax.ppermute(east, "lon", right)
    from_right = lax.ppermute(west, "lon", left)
    above = lax.ppermute(last, "lat", down)
    below = lax.ppermute(first, "lat", up)
    corners_up = jnp.concatenate([from_left[:SUB], from_right[:SUB]], axis=0)
    corners_down = jnp.concatenate([from_left[rows - SUB:], from_right[rows - SUB:]], axis=0)
    above_sides = lax.ppermute(corners_down, "lat", down)
    below_sides = lax.ppermute(corners_up, "lat", up)

    gram = call(gram_kernel, f32(NGRAM, LANE), (pair_steps, pair_grads), name="gram")

    chunk = steps // CHUNKS
    own, other = [], []
    for n in range(CHUNKS):
        width = cols // LANE + 1
        field = call(
            make_sweep_kernel(n * chunk, chunk),
            f32(chunk, rows, cols),
            (masked, diffusivity, above, below, from_left, from_right, above_sides, below_sides),
            scratch=[pltpu.VMEM(((rows // SUB + 2) * width * 5, SUB, LANE), jnp.float32)],
            name="sweeps",
        )
        own.append(field)
        for shift in range(1, groups):
            pairs = [(i, (i + shift) % groups) for i in range(groups)]
            other.append((shift, n * chunk, lax.ppermute(field, "tm", pairs)))
    mixed = call(
        make_mix_own(CHUNKS), f32(steps, rows, cols), (time_corr, base, *own),
        specs=[SMEM, SMEM] + [VMEM] * CHUNKS, name="mix_own",
    )
    early, late = other[:-1], other[-1:]
    if early:
        mixed = call(
            make_mix_rest([(s, o) for s, o, _ in early], False), f32(steps, rows, cols),
            (time_corr, base, origin, mixed, *(v for _, _, v in early)),
            specs=[SMEM, SMEM, SMEM] + [VMEM] * (1 + len(early)), name="mix_early",
        )
    devices = height * breadth * groups
    mixed, message = call(
        make_mix_rest([(s, o) for s, o, _ in late], True), (f32(steps, rows, cols), f32(devices, 1, LANE)),
        (time_corr, base, origin, mixed, *(v for _, _, v in late), gram, pair_steps, pair_grads),
        specs=[SMEM, SMEM, SMEM] + [VMEM] * (4 + len(late)),
        scratch=[pltpu.VMEM((NROW, LANE), jnp.float32)], name="mix_late",
    )
    inbox = lax.all_to_all(message, ("lat", "lon", "tm"), split_axis=0, concat_axis=0, tiled=True)
    return call(
        final_kernel, f32(steps, rows, cols), (inbox, mixed, control, pair_steps, pair_grads),
        scratch=[pltpu.VMEM((NROW, LANE), jnp.float32)], name="final",
    )


def solution(mesh):
    placed = (
        P("tm", "lat", "lon"),
        P("tm", "lat", "lon"),
        P("lat", "lon"),
        P("lat", "lon"),
        P(),
        P(None, "tm", "lat", "lon"),
        P(None, "tm", "lat", "lon"),
    )
    return jax.shard_map(
        local, mesh=mesh, in_specs=placed, out_specs=P("tm", "lat", "lon"), check_vma=False
    )
```

```python
import functools
import jax
import jax.numpy as jnp
from jax import lax
from jax.experimental import pallas as pl
from jax.experimental.pallas import tpu as pltpu
from jax.sharding import PartitionSpec as P

PAIRS = 8
SWEEPS = 6
SUB = 8
LANE = 128
HALO = SWEEPS
GROUP = 8
PER = LANE // GROUP
CROSS = [(i, j) for i in range(PAIRS) for j in range(i, PAIRS)]
NSYM = len(CROSS)
WHERE = {pair: k for k, pair in enumerate(CROSS)}
NGRAM = 2 * NSYM
NPROJ = 2 * PAIRS
NROW = NGRAM + NPROJ

VMEM = pl.BlockSpec(memory_space=pltpu.VMEM)
HBM = pl.BlockSpec(memory_space=pl.ANY)
PARAMS = pltpu.CompilerParams(vmem_limit_bytes=48 * 1024 * 1024)


def f32(*shape):
    return jax.ShapeDtypeStruct(shape, jnp.float32)


def call(kernel, outs, args, specs=None, scratch=(), name=None):
    single = not isinstance(outs, (tuple, list))
    return pl.pallas_call(
        kernel,
        out_shape=outs,
        in_specs=specs or [VMEM] * len(args),
        out_specs=VMEM if single else [VMEM] * len(outs),
        scratch_shapes=list(scratch),
        compiler_params=PARAMS,
        name=name,
    )(*args)


def lane_index():
    return lax.broadcasted_iota(jnp.int32, (SUB, LANE), 1)


def row_index():
    return lax.broadcasted_iota(jnp.int32, (SUB, LANE), 0)


def gram_kernel(steps_ref, grads_ref, out_ref):
    _, steps, rows, cols = steps_ref.shape
    for half, left_ref in enumerate((steps_ref, grads_ref)):
        def body(step, sums):
            sums = list(sums)
            for c in range(0, cols, LANE):
                for r in range(0, rows, 2 * SUB):
                    where = (step, pl.ds(r, 2 * SUB), pl.ds(c, LANE))
                    right = [grads_ref[(i, *where)].astype(jnp.float32) for i in range(PAIRS)]
                    left = right if half else [left_ref[(i, *where)].astype(jnp.float32) for i in range(PAIRS)]
                    for part in range(2):
                        cut = slice(part * SUB, (part + 1) * SUB)
                        for k, (i, j) in enumerate(CROSS):
                            sums[k] = sums[k] + left[i][cut] * right[j][cut]
            return tuple(sums)

        zero = jnp.zeros((SUB, LANE), jnp.float32)
        sums = lax.fori_loop(0, steps, body, (zero,) * NSYM)
        for k in range(NSYM):
            out_ref[half * NSYM + k:half * NSYM + k + 1, :] = jnp.sum(sums[k], axis=0, keepdims=True)


def groups_of(steps):
    return [(begin, min(SUB, steps - begin)) for begin in range(0, steps, SUB)]


def slots_of(steps):
    return -(-(steps + 1) // SUB) * SUB


def pack_kernel(grad_hbm, mask_hbm, diff_hbm, field_ref, first_ref, last_ref, grad_ref, mask_ref, diff_ref, turn_ref, sems):
    steps, rows, cols = grad_ref.shape
    slots = field_ref.shape[1]
    copies = [
        pltpu.make_async_copy(mask_hbm, mask_ref, sems.at[0]),
        pltpu.make_async_copy(diff_hbm, diff_ref, sems.at[1]),
        pltpu.make_async_copy(grad_hbm, grad_ref, sems.at[2]),
    ]
    for copy in copies:
        copy.start()
    for copy in copies:
        copy.wait()
    zero = jnp.zeros((SUB, LANE), jnp.float32)
    for c in range(cols // LANE):
        across = slice(c * LANE, (c + 1) * LANE)
        for r in range(rows // SUB):
            down = slice(r * SUB, (r + 1) * SUB)
            base = (c * (rows // SUB) + r) * slots * SUB
            mask = mask_ref[down, across].astype(jnp.float32)
            for slot in range(slots):
                if slot < steps:
                    value = grad_ref[slot, down, across] * mask
                else:
                    value = diff_ref[down, across] if slot == steps else zero
                turn_ref[base + slot * SUB:base + (slot + 1) * SUB, :] = value
    for c in range(cols // LANE):
        across = slice(c * LANE, (c + 1) * LANE)
        for row in range(rows):
            base = (c * (rows // SUB) + row // SUB) * slots * SUB + row % SUB
            for slot in range(0, slots, SUB):
                value = turn_ref[pl.ds(base + slot * SUB, SUB, stride=SUB), :]
                field_ref[row, slot:slot + SUB, across] = value
                if row < HALO:
                    first_ref[row, slot:slot + SUB, across] = value
                if row >= rows - HALO:
                    last_ref[row - (rows - HALO), slot:slot + SUB, across] = value


def extended(row, above_ref, field_ref, below_ref):
    rows = field_ref.shape[0]
    if row < HALO:
        return above_ref, row
    if row < HALO + rows:
        return field_ref, row - HALO
    return below_ref, row - HALO - rows


def side_kernel(above_ref, field_ref, below_ref, order_ref, west_ref, east_ref):
    rows, slots, cols = field_ref.shape
    lane = lane_index()
    for slot in range(0, slots, SUB):
        down = slice(slot, slot + SUB)
        for base in range(0, rows + 2 * HALO, PER):
            west = east = jnp.zeros((SUB, LANE), jnp.float32)
            for row in range(base, min(base + PER, rows + 2 * HALO)):
                ref, at = extended(row, above_ref, field_ref, below_ref)
                begin = (row - base) * GROUP
                here = (lane >= begin) & (lane < begin + GROUP)
                left = ref[at, down, 0:LANE]
                right = ref[at, down, cols - LANE:cols]
                west = jnp.where(here, pltpu.roll(left, begin, 1) if begin else left, west)
                turn = (begin + GROUP) % LANE
                east = jnp.where(here, pltpu.roll(right, turn, 1) if turn else right, east)
            place = slice(base // PER * LANE, (base // PER + 1) * LANE)
            west_ref[down, place] = west
            east_ref[down, place] = east


def make_row_loader(above_ref, field_ref, below_ref, left_ref, right_ref):
    cols = field_ref.shape[2]
    lane = lane_index()

    def load(row, down, size):
        ref, at = extended(row, above_ref, field_ref, below_ref)
        place = slice(row // PER * LANE, (row // PER + 1) * LANE)
        begin = row % PER * GROUP
        tiles = [ref[at, down, c * LANE:(c + 1) * LANE] for c in range(cols // LANE)]
        east, west = right_ref[down, place], left_ref[down, place]
        if size == 1:
            tiles = [jnp.broadcast_to(tile, (SUB, LANE)) for tile in tiles]
            east, west = (jnp.broadcast_to(tile, (SUB, LANE)) for tile in (east, west))
        east = pltpu.roll(east, LANE - begin, 1) if begin else east
        turn = (2 * LANE - GROUP - begin) % LANE
        west = pltpu.roll(west, turn, 1) if turn else west
        return tiles + [jnp.where(lane < LANE // 2, east, west)]

    return load


def from_east(tiles, at_end):
    turned = [pltpu.roll(tile, LANE - 1, 1) for tile in tiles]
    return [jnp.where(at_end, turned[(c + 1) % len(tiles)], turned[c]) for c in range(len(tiles))]


def from_west(tiles, at_start):
    turned = [pltpu.roll(tile, 1, 1) for tile in tiles]
    return [jnp.where(at_start, turned[c - 1], turned[c]) for c in range(len(tiles))]


def weight_kernel(above_ref, field_ref, below_ref, left_ref, right_ref, south_ref, east_ref, *, steps):
    rows, _, cols = field_ref.shape
    load = make_row_loader(above_ref, field_ref, below_ref, left_ref, right_ref)
    at_end = lane_index() == LANE - 1
    height = rows + 2 * HALO
    above = None
    for row in range(height):
        kappa = load(row, slice(steps, steps + 1), 1)
        beside = from_east(kappa, at_end)
        for c in range(len(kappa)):
            east_ref[row, :, c * LANE:(c + 1) * LANE] = 0.5 * (kappa[c] + beside[c])
            if above is not None:
                south_ref[row - 1, :, c * LANE:(c + 1) * LANE] = 0.5 * (above[c] + kappa[c])
        above = kappa
    for side, row in enumerate((HALO - 1, HALO + rows)):
        kappa = load(row, slice(steps, steps + 1), 1)
        for c in range(len(kappa)):
            south_ref[height - 1 + side, :, c * LANE:(c + 1) * LANE] = jnp.where(kappa[c] > 0.0, 1.0, 0.0)


def sweep_kernel(above_ref, field_ref, below_ref, left_ref, right_ref, south_ref, east_ref, out_ref, *, begin):
    rows, _, cols = field_ref.shape
    height, width = rows + 2 * HALO, cols // LANE + 1
    count = out_ref.shape[1]
    lane = lane_index()
    at_start, at_end = lane == 0, lane == LANE - 1
    load = make_row_loader(above_ref, field_ref, below_ref, left_ref, right_ref)
    state = [None] * (SWEEPS + 1)

    def at(ref, row, c):
        return ref[row, :, c * LANE:(c + 1) * LANE]

    def feed(sweep, row, tiles):
        if sweep > SWEEPS:
            for c in range(width - 1):
                out_ref[row - HALO, :, c * LANE:(c + 1) * LANE] = tiles[c][:count]
            return
        before = state[sweep]
        if before is None:
            state[sweep] = (tiles, None)
            return
        centre, north = before
        south = [at(south_ref, row - 1, c) * (tiles[c] - centre[c]) for c in range(width)]
        state[sweep] = (tiles, south)
        if north is None:
            return
        ahead = from_east(centre, at_end)
        flux = [at(east_ref, row - 1, c) * (ahead[c] - centre[c]) for c in range(width)]
        behind = from_west(flux, at_start)
        fresh = []
        for c in range(width):
            change = (south[c] - north[c]) + (flux[c] - behind[c])
            if row - 1 < HALO:
                change = change * at(south_ref, height - 1, c)
            if row - 1 >= HALO + rows:
                change = change * at(south_ref, height, c)
            fresh.append(centre[c] + change)
        feed(sweep + 1, row - 1, fresh)

    for row in range(height):
        feed(1, row, load(row, slice(begin, begin + SUB), SUB))


def split_stack(value):
    high = value.astype(jnp.bfloat16).astype(jnp.float32)
    rest = value - high
    middle = rest.astype(jnp.bfloat16).astype(jnp.float32)
    low = rest - middle
    return jnp.concatenate([high, middle, high, low, middle, high], axis=0).astype(jnp.bfloat16)


def corr_stack(time_corr, source, target, count, steps):
    block = lax.dynamic_slice(time_corr, (source, target), (count, steps))
    block = jnp.pad(block, ((0, -count % SUB), (0, 0))).T
    high = lax.reduce_precision(block, 8, 7)
    rest = block - high
    middle = lax.reduce_precision(rest, 8, 7)
    low = rest - middle
    return jnp.concatenate([high, high, middle, high, middle, low], axis=1).astype(jnp.bfloat16)


def mixed_row(row, corr_ref, field_refs):
    parts = []
    for ref in field_refs:
        part = ref[row]
        parts.append(part)
        if -part.shape[0] % SUB:
            parts.append(jnp.zeros((-part.shape[0] % SUB, part.shape[1]), jnp.float32))
    stacked = split_stack(jnp.concatenate(parts, axis=0) if len(parts) > 1 else parts[0])
    return jnp.dot(corr_ref[...], stacked, preferred_element_type=jnp.float32)


def make_mix(first):
    def kernel(*refs):
        *refs, out_ref = refs
        if first:
            corr_ref, *field_refs = refs
        else:
            acc_ref, corr_ref, *field_refs = refs
        for row in range(out_ref.shape[0]):
            total = mixed_row(row, corr_ref, field_refs)
            out_ref[row] = total if first else acc_ref[row] + total

    return kernel


def last_mix_kernel(acc_ref, corr_ref, field_ref, gram_ref, steps_ref, grads_ref, out_ref, message_ref, turn_ref, rows_ref):
    _, steps, rows, cols = steps_ref.shape
    slots = turn_ref.shape[0] // (rows * (cols // LANE))
    for row in range(rows):
        total = acc_ref[row] + mixed_row(row, corr_ref, [field_ref])
        for c in range(cols // LANE):
            base = (c * (rows // SUB) + row // SUB) * slots * SUB + row % SUB
            for begin, count in groups_of(steps):
                turn_ref[pl.ds(base + begin * SUB, count, stride=SUB), :] = total[begin:begin + count, c * LANE:(c + 1) * LANE]

    zero = jnp.zeros((SUB, LANE), jnp.float32)

    def body(step, sums):
        sums = list(sums)
        for c in range(cols // LANE):
            for r in range(0, rows, 2 * SUB):
                where = (step, pl.ds(r, 2 * SUB), pl.ds(c * LANE, LANE))
                halves = []
                for part in range(2):
                    base = (c * (rows // SUB) + r // SUB + part) * slots * SUB
                    halves.append(turn_ref[pl.ds(pl.multiple_of(base + step * SUB, SUB), SUB), :])
                mixed = jnp.concatenate(halves, axis=0)
                out_ref[where] = mixed
                half = mixed.astype(jnp.bfloat16).astype(jnp.float32)
                for n in range(NPROJ):
                    source = steps_ref if n < PAIRS else grads_ref
                    product = source[(n % PAIRS, *where)].astype(jnp.float32) * half
                    sums[n] = sums[n] + (product[:SUB] + product[SUB:])
        return tuple(sums)

    sums = lax.fori_loop(0, steps, body, (zero,) * NPROJ)
    rows_ref[0:NGRAM, :] = gram_ref[...]
    for n in range(NPROJ):
        rows_ref[NGRAM + n:NGRAM + n + 1, :] = jnp.sum(sums[n], axis=0, keepdims=True)
    lane, row = lane_index(), row_index()
    total = zero
    for first in range(0, NROW, SUB):
        summed = jnp.sum(rows_ref[first:first + SUB, :], axis=1, keepdims=True)
        total = total + jnp.where(lane == row + first, summed, 0.0)
    message = jnp.sum(total, axis=0, keepdims=True)
    message_ref[...] = jnp.broadcast_to(message[None], message_ref.shape)


def final_kernel(inbox_ref, mixed_ref, control_ref, steps_ref, grads_ref, out_ref, rows_ref):
    totals = jnp.sum(inbox_ref[...], axis=0)
    lane, row = lane_index(), row_index()
    spread = jnp.broadcast_to(totals, (SUB, LANE))
    for first in range(0, NROW, SUB):
        picked = jnp.where(lane == row + first, spread, 0.0)
        rows_ref[first:first + SUB, :] = jnp.broadcast_to(jnp.sum(picked, axis=1, keepdims=True), (SUB, LANE))

    def entry(k):
        return jnp.broadcast_to(rows_ref[k:k + 1, :], (SUB, LANE))

    cross = {pair: entry(k) for pair, k in WHERE.items()}

    def square(i, j):
        return entry(NSYM + WHERE[(min(i, j), max(i, j))])

    gamma = cross[(PAIRS - 1, PAIRS - 1)] / square(PAIRS - 1, PAIRS - 1)
    first = [None] * PAIRS
    for i in reversed(range(PAIRS)):
        rest = entry(NGRAM + i)
        for j in reversed(range(i + 1, PAIRS)):
            rest = rest - cross[(i, j)] * first[j]
        first[i] = rest / cross[(i, i)]
    second = [None] * PAIRS
    for i in range(PAIRS):
        inner = -entry(NGRAM + PAIRS + i)
        for j in range(PAIRS):
            inner = inner + square(i, j) * first[j]
        rest = cross[(i, i)] * first[i] + gamma * inner
        for j in range(i):
            rest = rest - cross[(j, i)] * second[j]
        second[i] = rest / cross[(i, i)]
    scaled = [gamma * value for value in first]

    _, steps, rows, cols = steps_ref.shape

    def body(step, carry):
        for c in range(0, cols, LANE):
            for r in range(0, rows, 2 * SUB):
                where = (step, pl.ds(r, 2 * SUB), pl.ds(c, LANE))
                mixed = mixed_ref[where]
                control = control_ref[where]
                update = [gamma * mixed[:SUB], gamma * mixed[SUB:]]
                for i in range(PAIRS):
                    s = steps_ref[(i, *where)].astype(jnp.float32)
                    y = grads_ref[(i, *where)].astype(jnp.float32)
                    for part, cut in enumerate((slice(0, SUB), slice(SUB, 2 * SUB))):
                        update[part] = update[part] + (second[i] * s[cut] - scaled[i] * y[cut])
                out_ref[step, pl.ds(r, SUB), pl.ds(c, LANE)] = control[:SUB] - update[0]
                out_ref[step, pl.ds(r + SUB, SUB), pl.ds(c, LANE)] = control[SUB:] - update[1]
        return carry

    lax.fori_loop(0, steps, body, 0)


def local(gradient, control, diffusivity, land_mask, time_corr, pair_steps, pair_grads):
    steps, rows, cols = gradient.shape
    height, breadth, groups = (lax.axis_size(axis) for axis in ("lat", "lon", "tm"))
    mine = lax.axis_index("tm")
    down = [(i, i + 1) for i in range(height - 1)]
    up = [(i + 1, i) for i in range(height - 1)]
    right = [(i, (i + 1) % breadth) for i in range(breadth)]
    left = [(j, i) for i, j in right]
    slots = slots_of(steps)
    turn = pltpu.VMEM((rows * (cols // LANE) * slots, LANE), jnp.float32)

    field, first, last = call(
        pack_kernel,
        (f32(rows, slots, cols), f32(HALO, slots, cols), f32(HALO, slots, cols)),
        (gradient, land_mask, diffusivity),
        specs=[HBM] * 3,
        scratch=[
            pltpu.VMEM((steps, rows, cols), jnp.float32), pltpu.VMEM((rows, cols), jnp.int32),
            pltpu.VMEM((rows, cols), jnp.float32), turn, pltpu.SemaphoreType.DMA((3,)),
        ],
        name="pack",
    )
    above = lax.ppermute(last, "lat", down)
    below = lax.ppermute(first, "lat", up)
    gram = call(gram_kernel, f32(NGRAM, LANE), (pair_steps, pair_grads), name="gram")
    side_shape = f32(slots, -(-(rows + 2 * HALO) // PER) * LANE)
    west, east = call(side_kernel, (side_shape, side_shape), (above, field, below, gram), name="sides")
    from_left = lax.ppermute(east, "lon", right)
    from_right = lax.ppermute(west, "lon", left)
    whole = (above, field, below, from_left, from_right)
    tall, wide = rows + 2 * HALO, cols + LANE
    south, beside = call(
        functools.partial(weight_kernel, steps=steps), (f32(tall + 1, SUB, wide), f32(tall, SUB, wide)), whole, name="weights"
    )
    own, other = [], []
    for begin, count in groups_of(steps):
        part = call(
            functools.partial(sweep_kernel, begin=begin), f32(rows, count, cols), (*whole, south, beside), name="sweeps"
        )
        own.append(part)
        for shift in range(1, groups):
            pairs = [(i, (i + shift) % groups) for i in range(groups)]
            source = lax.rem(mine - shift + groups, groups) * steps + begin
            other.append((corr_stack(time_corr, source, mine * steps, count, steps), lax.ppermute(part, "tm", pairs)))
    mixed = call(
        make_mix(True), f32(rows, steps, cols),
        (corr_stack(time_corr, mine * steps, mine * steps, steps, steps), *own), name="mix_own",
    )
    for corr, part in other[:-1]:
        mixed = call(make_mix(False), f32(rows, steps, cols), (mixed, corr, part), name="mix_more")
    devices = height * breadth * groups
    mixed, message = call(
        last_mix_kernel, (f32(steps, rows, cols), f32(devices, 1, LANE)),
        (mixed, *other[-1], gram, pair_steps, pair_grads),
        scratch=[turn, pltpu.VMEM((NROW, LANE), jnp.float32)], name="mix_last",
    )
    inbox = lax.all_to_all(message, ("lat", "lon", "tm"), split_axis=0, concat_axis=0, tiled=True)
    return call(
        final_kernel, f32(steps, rows, cols), (inbox, mixed, control, pair_steps, pair_grads),
        scratch=[pltpu.VMEM((NROW, LANE), jnp.float32)], name="final",
    )


def solution(mesh):
    placed = (
        P("tm", "lat", "lon"),
        P("tm", "lat", "lon"),
        P("lat", "lon"),
        P("lat", "lon"),
        P(),
        P(None, "tm", "lat", "lon"),
        P(None, "tm", "lat", "lon"),
    )
    return jax.shard_map(
        local, mesh=mesh, in_specs=placed, out_specs=P("tm", "lat", "lon"), check_vma=False
    )
```

```python
import functools
import jax
import jax.numpy as jnp
from jax import lax
from jax.experimental import pallas as pl
from jax.experimental.pallas import tpu as pltpu
from jax.sharding import PartitionSpec as P

PAIRS = 8
SWEEPS = 6
SUB = 8
LANE = 128
HALO = SWEEPS
GROUP = 8
PER = LANE // GROUP
CROSS = [(i, j) for i in range(PAIRS) for j in range(i, PAIRS)]
NSYM = len(CROSS)
WHERE = {pair: k for k, pair in enumerate(CROSS)}
NGRAM = 2 * NSYM
NPROJ = 2 * PAIRS
NROW = NGRAM + NPROJ

VMEM = pl.BlockSpec(memory_space=pltpu.VMEM)
HBM = pl.BlockSpec(memory_space=pltpu.HBM)
PARAMS = pltpu.CompilerParams(vmem_limit_bytes=48 * 1024 * 1024)


def f32(*shape):
    return jax.ShapeDtypeStruct(shape, jnp.float32)


def call(kernel, outs, args, specs=None, scratch=(), name=None):
    single = not isinstance(outs, (tuple, list))
    return pl.pallas_call(
        kernel,
        out_shape=outs,
        in_specs=specs or [VMEM] * len(args),
        out_specs=VMEM if single else [VMEM] * len(outs),
        scratch_shapes=list(scratch),
        compiler_params=PARAMS,
        name=name,
    )(*args)


def lane_index():
    return lax.broadcasted_iota(jnp.int32, (SUB, LANE), 1)


def row_index():
    return lax.broadcasted_iota(jnp.int32, (SUB, LANE), 0)


def gram_kernel(steps_hbm, grads_hbm, out_ref, steps_ref, grads_ref, sems):
    _, steps, rows, cols = steps_ref.shape
    pieces = 4
    while steps % pieces:
        pieces -= 1
    count = steps // pieces
    copies = []
    for n in range(pieces):
        part = (slice(None), pl.ds(n * count, count))
        copies.append((
            pltpu.make_async_copy(steps_hbm.at[part], steps_ref.at[part], sems.at[0, n]),
            pltpu.make_async_copy(grads_hbm.at[part], grads_ref.at[part], sems.at[1, n]),
        ))
    for pair in copies:
        for copy in pair:
            copy.start()

    def make_body(half):
        def body(step, sums):
            sums = list(sums)
            for c in range(0, cols, LANE):
                for r in range(0, rows, 2 * SUB):
                    where = (step, pl.ds(r, 2 * SUB), pl.ds(c, LANE))
                    right = [grads_ref[(i, *where)].astype(jnp.float32) for i in range(PAIRS)]
                    left = right if half else [steps_ref[(i, *where)].astype(jnp.float32) for i in range(PAIRS)]
                    for part in range(2):
                        cut = slice(part * SUB, (part + 1) * SUB)
                        for k, (i, j) in enumerate(CROSS):
                            sums[k] = sums[k] + left[i][cut] * right[j][cut]
            return tuple(sums)

        return body

    zero = jnp.zeros((SUB, LANE), jnp.float32)
    sums = (zero,) * NSYM
    for n in range(pieces):
        for copy in copies[n]:
            copy.wait()
        sums = lax.fori_loop(n * count, (n + 1) * count, make_body(0), sums)
    for k in range(NSYM):
        out_ref[k:k + 1, :] = jnp.sum(sums[k], axis=0, keepdims=True)
    sums = lax.fori_loop(0, steps, make_body(1), (zero,) * NSYM)
    for k in range(NSYM):
        out_ref[NSYM + k:NSYM + k + 1, :] = jnp.sum(sums[k], axis=0, keepdims=True)


def groups_of(steps):
    return [(begin, min(SUB, steps - begin)) for begin in range(0, steps, SUB)]


def slots_of(steps):
    return -(-(steps + 1) // SUB) * SUB


def pack_kernel(grad_hbm, mask_hbm, diff_hbm, field_ref, first_ref, last_ref, grad_ref, mask_ref, diff_ref, turn_ref, sems):
    steps, rows, cols = grad_ref.shape
    slots = field_ref.shape[1]
    pieces = [(begin, min(SUB, steps - begin)) for begin in range(0, steps, SUB)]
    copies = [pltpu.make_async_copy(mask_hbm, mask_ref, sems.at[0]), pltpu.make_async_copy(diff_hbm, diff_ref, sems.at[1])]
    for n, (begin, count) in enumerate(pieces):
        part = pl.ds(begin, count)
        copies.append(pltpu.make_async_copy(grad_hbm.at[part], grad_ref.at[part], sems.at[2 + n]))
    for copy in copies:
        copy.start()
    copies[0].wait()
    copies[1].wait()
    zero = jnp.zeros((SUB, LANE), jnp.float32)
    tiles = [
        (slice(r * SUB, (r + 1) * SUB), slice(c * LANE, (c + 1) * LANE), (c * (rows // SUB) + r) * slots * SUB)
        for c in range(cols // LANE) for r in range(rows // SUB)
    ]
    mask = [mask_ref[down, across].astype(jnp.float32) for down, across, _ in tiles]
    for slot in range(steps, slots):
        for down, across, base in tiles:
            value = diff_ref[down, across] if slot == steps else zero
            turn_ref[base + slot * SUB:base + (slot + 1) * SUB, :] = value
    for n, (begin, count) in enumerate(pieces):
        copies[2 + n].wait()
        for slot in range(begin, begin + count):
            for (down, across, base), keep in zip(tiles, mask):
                turn_ref[base + slot * SUB:base + (slot + 1) * SUB, :] = grad_ref[slot, down, across] * keep
    for c in range(cols // LANE):
        across = slice(c * LANE, (c + 1) * LANE)
        for row in range(rows):
            base = (c * (rows // SUB) + row // SUB) * slots * SUB + row % SUB
            for slot in range(0, slots, SUB):
                value = turn_ref[pl.ds(base + slot * SUB, SUB, stride=SUB), :]
                field_ref[row, slot:slot + SUB, across] = value
                if row < HALO:
                    first_ref[row, slot:slot + SUB, across] = value
                if row >= rows - HALO:
                    last_ref[row - (rows - HALO), slot:slot + SUB, across] = value


def extended(row, above_ref, field_ref, below_ref):
    rows = field_ref.shape[0]
    if row < HALO:
        return above_ref, row
    if row < HALO + rows:
        return field_ref, row - HALO
    return below_ref, row - HALO - rows


def side_kernel(above_ref, field_ref, below_ref, order_ref, west_ref, east_ref):
    rows, slots, cols = field_ref.shape
    lane = lane_index()
    for slot in range(0, slots, SUB):
        down = slice(slot, slot + SUB)
        for base in range(0, rows + 2 * HALO, PER):
            west = east = jnp.zeros((SUB, LANE), jnp.float32)
            for row in range(base, min(base + PER, rows + 2 * HALO)):
                ref, at = extended(row, above_ref, field_ref, below_ref)
                begin = (row - base) * GROUP
                here = (lane >= begin) & (lane < begin + GROUP)
                left = ref[at, down, 0:LANE]
                right = ref[at, down, cols - LANE:cols]
                west = jnp.where(here, pltpu.roll(left, begin, 1) if begin else left, west)
                turn = (begin + GROUP) % LANE
                east = jnp.where(here, pltpu.roll(right, turn, 1) if turn else right, east)
            place = slice(base // PER * LANE, (base // PER + 1) * LANE)
            west_ref[down, place] = west
            east_ref[down, place] = east


def make_row_loader(above_ref, field_ref, below_ref, left_ref, right_ref):
    cols = field_ref.shape[2]
    lane = lane_index()

    def load(row, down, size):
        ref, at = extended(row, above_ref, field_ref, below_ref)
        place = slice(row // PER * LANE, (row // PER + 1) * LANE)
        begin = row % PER * GROUP
        tiles = [ref[at, down, c * LANE:(c + 1) * LANE] for c in range(cols // LANE)]
        east, west = right_ref[down, place], left_ref[down, place]
        if size == 1:
            tiles = [jnp.broadcast_to(tile, (SUB, LANE)) for tile in tiles]
            east, west = (jnp.broadcast_to(tile, (SUB, LANE)) for tile in (east, west))
        east = pltpu.roll(east, LANE - begin, 1) if begin else east
        turn = (2 * LANE - GROUP - begin) % LANE
        west = pltpu.roll(west, turn, 1) if turn else west
        return tiles + [jnp.where(lane < LANE // 2, east, west)]

    return load


def from_east(tiles, at_end):
    turned = [pltpu.roll(tile, LANE - 1, 1) for tile in tiles]
    return [jnp.where(at_end, turned[(c + 1) % len(tiles)], turned[c]) for c in range(len(tiles))]


def from_west(tiles, at_start):
    turned = [pltpu.roll(tile, 1, 1) for tile in tiles]
    return [jnp.where(at_start, turned[c - 1], turned[c]) for c in range(len(tiles))]


def weight_kernel(above_ref, field_ref, below_ref, left_ref, right_ref, south_ref, east_ref, west_ref, keep_ref, *, steps):
    rows, _, cols = field_ref.shape
    load = make_row_loader(above_ref, field_ref, below_ref, left_ref, right_ref)
    lane = lane_index()
    at_start, at_end = lane == 0, lane == LANE - 1
    height = rows + 2 * HALO
    above = None
    for row in range(height):
        kappa = load(row, slice(steps, steps + 1), 1)
        beside = from_east(kappa, at_end)
        east = [0.5 * (kappa[c] + beside[c]) for c in range(len(kappa))]
        west = from_west(east, at_start)
        for c in range(len(kappa)):
            across = slice(c * LANE, (c + 1) * LANE)
            east_ref[row, :, across] = east[c]
            west_ref[row, :, across] = west[c]
            keep_ref[row, :, across] = 1.0 - east[c] - west[c]
            if above is not None:
                south_ref[row - 1, :, across] = 0.5 * (above[c] + kappa[c])
            if row in (HALO - 1, HALO + rows):
                south_ref[height - 1 + (row >= HALO), :, across] = jnp.where(kappa[c] > 0.0, 1.0, 0.0)
        above = kappa


def sweep_kernel(
    above_ref, field_ref, below_ref, left_ref, right_ref, south_ref, east_ref, west_ref, keep_ref, out_ref, *, begin
):
    rows, _, cols = field_ref.shape
    height, width = rows + 2 * HALO, cols // LANE + 1
    count = out_ref.shape[1]
    lane = lane_index()
    at_start, at_end = lane == 0, lane == LANE - 1
    load = make_row_loader(above_ref, field_ref, below_ref, left_ref, right_ref)
    state = [None] * SWEEPS

    def at(ref, row, c):
        return ref[row, :, c * LANE:(c + 1) * LANE]

    def advance(sweep, row, tiles):
        before = state[sweep]
        if before is None:
            state[sweep] = (tiles, None)
            return None
        centre, north = before
        south = [at(south_ref, row - 1, c) * (tiles[c] - centre[c]) for c in range(width)]
        state[sweep] = (tiles, south)
        if north is None:
            return None
        ahead, behind = from_east(centre, at_end), from_west(centre, at_start)
        fresh = []
        for c in range(width):
            change = south[c] - north[c]
            if row - 1 < HALO:
                change = change * at(south_ref, height - 1, c)
            if row - 1 >= HALO + rows:
                change = change * at(south_ref, height, c)
            across = at(east_ref, row - 1, c) * ahead[c] + at(west_ref, row - 1, c) * behind[c]
            fresh.append(at(keep_ref, row - 1, c) * centre[c] + across + change)
        return fresh

    waiting = [None] * (SWEEPS + 1)
    for tick in range(height + SWEEPS + 1):
        if waiting[SWEEPS] is not None:
            row, tiles = waiting[SWEEPS]
            for c in range(width - 1):
                out_ref[row - HALO, :, c * LANE:(c + 1) * LANE] = tiles[c][:count]
        for sweep in reversed(range(SWEEPS)):
            if sweep == 0:
                entry = (tick, load(tick, slice(begin, begin + SUB), SUB)) if tick < height else None
            else:
                entry = waiting[sweep]
            waiting[sweep + 1] = None
            if entry is not None:
                fresh = advance(sweep, *entry)
                if fresh is not None:
                    waiting[sweep + 1] = (entry[0] - 1, fresh)


def split_stack(value):
    high = value.astype(jnp.bfloat16).astype(jnp.float32)
    rest = value - high
    middle = rest.astype(jnp.bfloat16).astype(jnp.float32)
    low = rest - middle
    return jnp.concatenate([high, middle, high, low, middle, high], axis=0).astype(jnp.bfloat16)


def corr_stack(time_corr, source, target, count, steps):
    block = lax.dynamic_slice(time_corr, (source, target), (count, steps))
    block = jnp.pad(block, ((0, -count % SUB), (0, 0))).T
    high = lax.reduce_precision(block, 8, 7)
    rest = block - high
    middle = lax.reduce_precision(rest, 8, 7)
    low = rest - middle
    return jnp.concatenate([high, high, middle, high, middle, low], axis=1).astype(jnp.bfloat16)


def mixed_row(row, corr_ref, field_refs):
    parts = []
    for ref in field_refs:
        part = ref[row]
        parts.append(part)
        if -part.shape[0] % SUB:
            parts.append(jnp.zeros((-part.shape[0] % SUB, part.shape[1]), jnp.float32))
    stacked = split_stack(jnp.concatenate(parts, axis=0) if len(parts) > 1 else parts[0])
    return jnp.dot(corr_ref[...], stacked, preferred_element_type=jnp.float32)


def make_mix(first):
    def kernel(*refs):
        *refs, out_ref = refs
        if first:
            corr_ref, *field_refs = refs
        else:
            acc_ref, corr_ref, *field_refs = refs
        for row in range(out_ref.shape[0]):
            total = mixed_row(row, corr_ref, field_refs)
            out_ref[row] = total if first else acc_ref[row] + total

    return kernel


def last_mix_kernel(acc_ref, corr_ref, field_ref, gram_ref, steps_ref, grads_ref, out_ref, message_ref, turn_ref, rows_ref):
    _, steps, rows, cols = steps_ref.shape
    slots = turn_ref.shape[0] // (rows * (cols // LANE))
    for row in range(rows):
        total = acc_ref[row] + mixed_row(row, corr_ref, [field_ref])
        for c in range(cols // LANE):
            base = (c * (rows // SUB) + row // SUB) * slots * SUB + row % SUB
            for begin, count in groups_of(steps):
                turn_ref[pl.ds(base + begin * SUB, count, stride=SUB), :] = total[begin:begin + count, c * LANE:(c + 1) * LANE]

    zero = jnp.zeros((SUB, LANE), jnp.float32)

    def body(step, sums):
        sums = list(sums)
        for c in range(cols // LANE):
            for r in range(0, rows, 2 * SUB):
                where = (step, pl.ds(r, 2 * SUB), pl.ds(c * LANE, LANE))
                halves = []
                for part in range(2):
                    base = (c * (rows // SUB) + r // SUB + part) * slots * SUB
                    halves.append(turn_ref[pl.ds(pl.multiple_of(base + step * SUB, SUB), SUB), :])
                mixed = jnp.concatenate(halves, axis=0)
                out_ref[where] = mixed
                half = mixed.astype(jnp.bfloat16).astype(jnp.float32)
                for n in range(NPROJ):
                    source = steps_ref if n < PAIRS else grads_ref
                    product = source[(n % PAIRS, *where)].astype(jnp.float32) * half
                    sums[n] = sums[n] + (product[:SUB] + product[SUB:])
        return tuple(sums)

    sums = lax.fori_loop(0, steps, body, (zero,) * NPROJ)
    rows_ref[0:NGRAM, :] = gram_ref[...]
    for n in range(NPROJ):
        rows_ref[NGRAM + n:NGRAM + n + 1, :] = jnp.sum(sums[n], axis=0, keepdims=True)
    lane, row = lane_index(), row_index()
    total = zero
    for first in range(0, NROW, SUB):
        summed = jnp.sum(rows_ref[first:first + SUB, :], axis=1, keepdims=True)
        total = total + jnp.where(lane == row + first, summed, 0.0)
    message = jnp.sum(total, axis=0, keepdims=True)
    message_ref[...] = jnp.broadcast_to(message[None], message_ref.shape)


def final_kernel(inbox_ref, mixed_ref, control_ref, steps_ref, grads_ref, out_ref, rows_ref):
    totals = jnp.sum(inbox_ref[...], axis=0)
    lane, row = lane_index(), row_index()
    spread = jnp.broadcast_to(totals, (SUB, LANE))
    for first in range(0, NROW, SUB):
        picked = jnp.where(lane == row + first, spread, 0.0)
        rows_ref[first:first + SUB, :] = jnp.broadcast_to(jnp.sum(picked, axis=1, keepdims=True), (SUB, LANE))

    def entry(k):
        return jnp.broadcast_to(rows_ref[k:k + 1, :], (SUB, LANE))

    cross = {pair: entry(k) for pair, k in WHERE.items()}

    def square(i, j):
        return entry(NSYM + WHERE[(min(i, j), max(i, j))])

    gamma = cross[(PAIRS - 1, PAIRS - 1)] / square(PAIRS - 1, PAIRS - 1)
    first = [None] * PAIRS
    for i in reversed(range(PAIRS)):
        rest = entry(NGRAM + i)
        for j in reversed(range(i + 1, PAIRS)):
            rest = rest - cross[(i, j)] * first[j]
        first[i] = rest / cross[(i, i)]
    second = [None] * PAIRS
    for i in range(PAIRS):
        inner = -entry(NGRAM + PAIRS + i)
        for j in range(PAIRS):
            inner = inner + square(i, j) * first[j]
        rest = cross[(i, i)] * first[i] + gamma * inner
        for j in range(i):
            rest = rest - cross[(j, i)] * second[j]
        second[i] = rest / cross[(i, i)]
    scaled = [gamma * value for value in first]

    _, steps, rows, cols = steps_ref.shape

    def body(step, carry):
        for c in range(0, cols, LANE):
            for r in range(0, rows, 2 * SUB):
                where = (step, pl.ds(r, 2 * SUB), pl.ds(c, LANE))
                mixed = mixed_ref[where]
                control = control_ref[where]
                update = [gamma * mixed[:SUB], gamma * mixed[SUB:]]
                for i in range(PAIRS):
                    s = steps_ref[(i, *where)].astype(jnp.float32)
                    y = grads_ref[(i, *where)].astype(jnp.float32)
                    for part, cut in enumerate((slice(0, SUB), slice(SUB, 2 * SUB))):
                        update[part] = update[part] + (second[i] * s[cut] - scaled[i] * y[cut])
                out_ref[step, pl.ds(r, SUB), pl.ds(c, LANE)] = control[:SUB] - update[0]
                out_ref[step, pl.ds(r + SUB, SUB), pl.ds(c, LANE)] = control[SUB:] - update[1]
        return carry

    lax.fori_loop(0, steps, body, 0)


def local(gradient, control, diffusivity, land_mask, time_corr, pair_steps, pair_grads):
    steps, rows, cols = gradient.shape
    height, breadth, groups = (lax.axis_size(axis) for axis in ("lat", "lon", "tm"))
    mine = lax.axis_index("tm")
    down = [(i, i + 1) for i in range(height - 1)]
    up = [(i + 1, i) for i in range(height - 1)]
    right = [(i, (i + 1) % breadth) for i in range(breadth)]
    left = [(j, i) for i, j in right]
    slots = slots_of(steps)
    turn = pltpu.VMEM((rows * (cols // LANE) * slots, LANE), jnp.float32)

    field, first, last = call(
        pack_kernel,
        (f32(rows, slots, cols), f32(HALO, slots, cols), f32(HALO, slots, cols)),
        (gradient, land_mask, diffusivity),
        specs=[HBM] * 3,
        scratch=[
            pltpu.VMEM((steps, rows, cols), jnp.float32), pltpu.VMEM((rows, cols), jnp.int32),
            pltpu.VMEM((rows, cols), jnp.float32), turn, pltpu.SemaphoreType.DMA((2 + len(groups_of(steps)),)),
        ],
        name="pack",
    )
    above = lax.ppermute(last, "lat", down)
    below = lax.ppermute(first, "lat", up)
    gram = call(
        gram_kernel, f32(NGRAM, LANE), (pair_steps, pair_grads), specs=[HBM] * 2,
        scratch=[
            pltpu.VMEM(pair_steps.shape, jnp.bfloat16), pltpu.VMEM(pair_grads.shape, jnp.bfloat16),
            pltpu.SemaphoreType.DMA((2, 4)),
        ],
        name="gram",
    )
    side_shape = f32(slots, -(-(rows + 2 * HALO) // PER) * LANE)
    west, east = call(side_kernel, (side_shape, side_shape), (above, field, below, gram), name="sides")
    from_left = lax.ppermute(east, "lon", right)
    from_right = lax.ppermute(west, "lon", left)
    whole = (above, field, below, from_left, from_right)
    tall, wide = rows + 2 * HALO, cols + LANE
    weights = call(
        functools.partial(weight_kernel, steps=steps),
        (f32(tall + 1, SUB, wide), f32(tall, SUB, wide), f32(tall, SUB, wide), f32(tall, SUB, wide)), whole, name="weights",
    )
    own, other = [], []
    for begin, count in groups_of(steps):
        part = call(
            functools.partial(sweep_kernel, begin=begin), f32(rows, count, cols), (*whole, *weights), name="sweeps"
        )
        if not own:
            time_corr, part = lax.optimization_barrier((time_corr, part))
        own.append(part)
        for shift in range(1, groups):
            pairs = [(i, (i + shift) % groups) for i in range(groups)]
            source = lax.rem(mine - shift + groups, groups) * steps + begin
            other.append((corr_stack(time_corr, source, mine * steps, count, steps), lax.ppermute(part, "tm", pairs)))
    mixed = call(
        make_mix(True), f32(rows, steps, cols),
        (corr_stack(time_corr, mine * steps, mine * steps, steps, steps), *own), name="mix_own",
    )
    for corr, part in other[:-1]:
        mixed = call(make_mix(False), f32(rows, steps, cols), (mixed, corr, part), name="mix_more")
    devices = height * breadth * groups
    mixed, message = call(
        last_mix_kernel, (f32(steps, rows, cols), f32(devices, 1, LANE)),
        (mixed, *other[-1], gram, pair_steps, pair_grads),
        scratch=[turn, pltpu.VMEM((NROW, LANE), jnp.float32)], name="mix_last",
    )
    inbox = lax.all_to_all(message, ("lat", "lon", "tm"), split_axis=0, concat_axis=0, tiled=True)
    return call(
        final_kernel, f32(steps, rows, cols), (inbox, mixed, control, pair_steps, pair_grads),
        scratch=[pltpu.VMEM((NROW, LANE), jnp.float32)], name="final",
    )


def solution(mesh):
    placed = (
        P("tm", "lat", "lon"),
        P("tm", "lat", "lon"),
        P("lat", "lon"),
        P("lat", "lon"),
        P(),
        P(None, "tm", "lat", "lon"),
        P(None, "tm", "lat", "lon"),
    )
    return jax.shard_map(
        local, mesh=mesh, in_specs=placed, out_specs=P("tm", "lat", "lon"), check_vma=False
    )
```

```python
import functools
import jax
import jax.numpy as jnp
from jax import lax
from jax.experimental import pallas as pl
from jax.experimental.pallas import tpu as pltpu
from jax.sharding import PartitionSpec as P

PAIRS = 8
SWEEPS = 6
SUB = 8
LANE = 128
HALO = SWEEPS
GROUP = 8
PER = LANE // GROUP
CROSS = [(i, j) for i in range(PAIRS) for j in range(i, PAIRS)]
NSYM = len(CROSS)
WHERE = {pair: k for k, pair in enumerate(CROSS)}
NGRAM = 2 * NSYM
NPROJ = 2 * PAIRS
NROW = NGRAM + NPROJ

VMEM = pl.BlockSpec(memory_space=pltpu.VMEM)
HBM = pl.BlockSpec(memory_space=pltpu.HBM)
PARAMS = pltpu.CompilerParams(vmem_limit_bytes=48 * 1024 * 1024)


def f32(*shape):
    return jax.ShapeDtypeStruct(shape, jnp.float32)


def call(kernel, outs, args, specs=None, scratch=(), name=None):
    single = not isinstance(outs, (tuple, list))
    return pl.pallas_call(
        kernel,
        out_shape=outs,
        in_specs=specs or [VMEM] * len(args),
        out_specs=VMEM if single else [VMEM] * len(outs),
        scratch_shapes=list(scratch),
        compiler_params=PARAMS,
        name=name,
    )(*args)


def lane_index():
    return lax.broadcasted_iota(jnp.int32, (SUB, LANE), 1)


def row_index():
    return lax.broadcasted_iota(jnp.int32, (SUB, LANE), 0)


def gram_kernel(steps_hbm, grads_hbm, out_ref, steps_ref, grads_ref, sems):
    _, steps, rows, cols = steps_ref.shape
    pieces = 4
    while steps % pieces:
        pieces -= 1
    count = steps // pieces
    copies = []
    for n in range(pieces):
        part = (slice(None), pl.ds(n * count, count))
        copies.append((
            pltpu.make_async_copy(steps_hbm.at[part], steps_ref.at[part], sems.at[0, n]),
            pltpu.make_async_copy(grads_hbm.at[part], grads_ref.at[part], sems.at[1, n]),
        ))
    for pair in copies:
        for copy in pair:
            copy.start()

    def make_body(half):
        def body(step, sums):
            sums = list(sums)
            for c in range(0, cols, LANE):
                for r in range(0, rows, 2 * SUB):
                    where = (step, pl.ds(r, 2 * SUB), pl.ds(c, LANE))
                    right = [grads_ref[(i, *where)].astype(jnp.float32) for i in range(PAIRS)]
                    left = right if half else [steps_ref[(i, *where)].astype(jnp.float32) for i in range(PAIRS)]
                    for part in range(2):
                        cut = slice(part * SUB, (part + 1) * SUB)
                        for k, (i, j) in enumerate(CROSS):
                            sums[k] = sums[k] + left[i][cut] * right[j][cut]
            return tuple(sums)

        return body

    zero = jnp.zeros((SUB, LANE), jnp.float32)
    sums = (zero,) * NSYM
    for n in range(pieces):
        for copy in copies[n]:
            copy.wait()
        sums = lax.fori_loop(n * count, (n + 1) * count, make_body(0), sums)
    for k in range(NSYM):
        out_ref[k:k + 1, :] = jnp.sum(sums[k], axis=0, keepdims=True)
    sums = lax.fori_loop(0, steps, make_body(1), (zero,) * NSYM)
    for k in range(NSYM):
        out_ref[NSYM + k:NSYM + k + 1, :] = jnp.sum(sums[k], axis=0, keepdims=True)


def groups_of(steps):
    return [(begin, min(SUB, steps - begin)) for begin in range(0, steps, SUB)]


def slots_of(steps):
    return -(-(steps + 1) // SUB) * SUB


def pack_kernel(grad_hbm, mask_hbm, diff_hbm, field_ref, first_ref, last_ref, grad_ref, mask_ref, diff_ref, turn_ref, sems):
    steps, rows, cols = grad_ref.shape
    slots = field_ref.shape[1]
    pieces = [(begin, min(SUB, steps - begin)) for begin in range(0, steps, SUB)]
    copies = [pltpu.make_async_copy(mask_hbm, mask_ref, sems.at[0]), pltpu.make_async_copy(diff_hbm, diff_ref, sems.at[1])]
    for n, (begin, count) in enumerate(pieces):
        part = pl.ds(begin, count)
        copies.append(pltpu.make_async_copy(grad_hbm.at[part], grad_ref.at[part], sems.at[2 + n]))
    for copy in copies:
        copy.start()
    copies[0].wait()
    copies[1].wait()
    zero = jnp.zeros((SUB, LANE), jnp.float32)
    tiles = [
        (slice(r * SUB, (r + 1) * SUB), slice(c * LANE, (c + 1) * LANE), (c * (rows // SUB) + r) * slots * SUB)
        for c in range(cols // LANE) for r in range(rows // SUB)
    ]
    mask = [mask_ref[down, across].astype(jnp.float32) for down, across, _ in tiles]
    for slot in range(steps, slots):
        for down, across, base in tiles:
            value = diff_ref[down, across] if slot == steps else zero
            turn_ref[base + slot * SUB:base + (slot + 1) * SUB, :] = value
    for n, (begin, count) in enumerate(pieces):
        copies[2 + n].wait()
        for slot in range(begin, begin + count):
            for (down, across, base), keep in zip(tiles, mask):
                turn_ref[base + slot * SUB:base + (slot + 1) * SUB, :] = grad_ref[slot, down, across] * keep
    for c in range(cols // LANE):
        across = slice(c * LANE, (c + 1) * LANE)
        for row in range(rows):
            base = (c * (rows // SUB) + row // SUB) * slots * SUB + row % SUB
            for slot in range(0, slots, SUB):
                value = turn_ref[pl.ds(base + slot * SUB, SUB, stride=SUB), :]
                field_ref[row, slot:slot + SUB, across] = value
                if row < HALO:
                    first_ref[row, slot:slot + SUB, across] = value
                if row >= rows - HALO:
                    last_ref[row - (rows - HALO), slot:slot + SUB, across] = value


def extended(row, above_ref, field_ref, below_ref):
    rows = field_ref.shape[0]
    if row < HALO:
        return above_ref, row
    if row < HALO + rows:
        return field_ref, row - HALO
    return below_ref, row - HALO - rows


def side_kernel(above_ref, field_ref, below_ref, order_ref, west_ref, east_ref):
    rows, slots, cols = field_ref.shape
    lane = lane_index()
    for slot in range(0, slots, SUB):
        down = slice(slot, slot + SUB)
        for base in range(0, rows + 2 * HALO, PER):
            west = east = jnp.zeros((SUB, LANE), jnp.float32)
            for row in range(base, min(base + PER, rows + 2 * HALO)):
                ref, at = extended(row, above_ref, field_ref, below_ref)
                begin = (row - base) * GROUP
                here = (lane >= begin) & (lane < begin + GROUP)
                left = ref[at, down, 0:LANE]
                right = ref[at, down, cols - LANE:cols]
                west = jnp.where(here, pltpu.roll(left, begin, 1) if begin else left, west)
                turn = (begin + GROUP) % LANE
                east = jnp.where(here, pltpu.roll(right, turn, 1) if turn else right, east)
            place = slice(base // PER * LANE, (base // PER + 1) * LANE)
            west_ref[down, place] = west
            east_ref[down, place] = east


def make_row_loader(above_ref, field_ref, below_ref, left_ref, right_ref):
    cols = field_ref.shape[2]
    lane = lane_index()

    def load(row, down, size):
        ref, at = extended(row, above_ref, field_ref, below_ref)
        place = slice(row // PER * LANE, (row // PER + 1) * LANE)
        begin = row % PER * GROUP
        tiles = [ref[at, down, c * LANE:(c + 1) * LANE] for c in range(cols // LANE)]
        east, west = right_ref[down, place], left_ref[down, place]
        if size == 1:
            tiles = [jnp.broadcast_to(tile, (SUB, LANE)) for tile in tiles]
            east, west = (jnp.broadcast_to(tile, (SUB, LANE)) for tile in (east, west))
        east = pltpu.roll(east, LANE - begin, 1) if begin else east
        turn = (2 * LANE - GROUP - begin) % LANE
        west = pltpu.roll(west, turn, 1) if turn else west
        return tiles + [jnp.where(lane < LANE // 2, east, west)]

    return load


def from_east(tiles, at_end):
    turned = [pltpu.roll(tile, LANE - 1, 1) for tile in tiles]
    return [jnp.where(at_end, turned[(c + 1) % len(tiles)], turned[c]) for c in range(len(tiles))]


def from_west(tiles, at_start):
    turned = [pltpu.roll(tile, 1, 1) for tile in tiles]
    return [jnp.where(at_start, turned[c - 1], turned[c]) for c in range(len(tiles))]


def weight_kernel(above_ref, field_ref, below_ref, left_ref, right_ref, south_ref, east_ref, west_ref, keep_ref, *, steps):
    rows, _, cols = field_ref.shape
    load = make_row_loader(above_ref, field_ref, below_ref, left_ref, right_ref)
    lane = lane_index()
    at_start, at_end = lane == 0, lane == LANE - 1
    height = rows + 2 * HALO
    above = None
    for row in range(height):
        kappa = load(row, slice(steps, steps + 1), 1)
        beside = from_east(kappa, at_end)
        east = [0.5 * (kappa[c] + beside[c]) for c in range(len(kappa))]
        west = from_west(east, at_start)
        for c in range(len(kappa)):
            across = slice(c * LANE, (c + 1) * LANE)
            east_ref[row, :, across] = east[c]
            west_ref[row, :, across] = west[c]
            keep_ref[row, :, across] = 1.0 - east[c] - west[c]
            if above is not None:
                south_ref[row - 1, :, across] = 0.5 * (above[c] + kappa[c])
            if row in (HALO - 1, HALO + rows):
                south_ref[height - 1 + (row >= HALO), :, across] = jnp.where(kappa[c] > 0.0, 1.0, 0.0)
        above = kappa


def sweep_kernel(
    above_ref, field_ref, below_ref, left_ref, right_ref, south_ref, east_ref, west_ref, keep_ref, out_ref, *, begin
):
    rows, _, cols = field_ref.shape
    height, width = rows + 2 * HALO, cols // LANE + 1
    count = out_ref.shape[1]
    lane = lane_index()
    at_start, at_end = lane == 0, lane == LANE - 1
    load = make_row_loader(above_ref, field_ref, below_ref, left_ref, right_ref)
    state = [None] * SWEEPS

    def at(ref, row, c):
        return ref[row, :, c * LANE:(c + 1) * LANE]

    def advance(sweep, row, tiles):
        before = state[sweep]
        if before is None:
            state[sweep] = (tiles, None)
            return None
        centre, north = before
        south = [at(south_ref, row - 1, c) * (tiles[c] - centre[c]) for c in range(width)]
        state[sweep] = (tiles, south)
        if north is None:
            return None
        ahead, behind = from_east(centre, at_end), from_west(centre, at_start)
        fresh = []
        for c in range(width):
            change = south[c] - north[c]
            if row - 1 < HALO:
                change = change * at(south_ref, height - 1, c)
            if row - 1 >= HALO + rows:
                change = change * at(south_ref, height, c)
            across = at(east_ref, row - 1, c) * ahead[c] + at(west_ref, row - 1, c) * behind[c]
            fresh.append(at(keep_ref, row - 1, c) * centre[c] + across + change)
        return fresh

    waiting = [None] * (SWEEPS + 1)
    for tick in range(height + SWEEPS + 1):
        if waiting[SWEEPS] is not None:
            row, tiles = waiting[SWEEPS]
            for c in range(width - 1):
                out_ref[row - HALO, :, c * LANE:(c + 1) * LANE] = tiles[c][:count]
        for sweep in reversed(range(SWEEPS)):
            if sweep == 0:
                entry = (tick, load(tick, slice(begin, begin + SUB), SUB)) if tick < height else None
            else:
                entry = waiting[sweep]
            waiting[sweep + 1] = None
            if entry is not None:
                fresh = advance(sweep, *entry)
                if fresh is not None:
                    waiting[sweep + 1] = (entry[0] - 1, fresh)


def split_stack(value):
    high = value.astype(jnp.bfloat16).astype(jnp.float32)
    rest = value - high
    middle = rest.astype(jnp.bfloat16).astype(jnp.float32)
    low = rest - middle
    return jnp.concatenate([high, middle, high, low, middle, high], axis=0).astype(jnp.bfloat16)


def corr_stack(time_corr, source, target, count, steps):
    block = lax.dynamic_slice(time_corr, (source, target), (count, steps))
    block = jnp.pad(block, ((0, -count % SUB), (0, 0))).T
    high = lax.reduce_precision(block, 8, 7)
    rest = block - high
    middle = lax.reduce_precision(rest, 8, 7)
    low = rest - middle
    return jnp.concatenate([high, high, middle, high, middle, low], axis=1).astype(jnp.bfloat16)


def mixed_row(row, corr_ref, field_refs):
    parts = []
    for ref in field_refs:
        part = ref[row]
        parts.append(part)
        if -part.shape[0] % SUB:
            parts.append(jnp.zeros((-part.shape[0] % SUB, part.shape[1]), jnp.float32))
    stacked = split_stack(jnp.concatenate(parts, axis=0) if len(parts) > 1 else parts[0])
    return jnp.dot(corr_ref[...], stacked, preferred_element_type=jnp.float32)


def make_mix(first):
    def kernel(*refs):
        *refs, out_ref = refs
        if first:
            corr_ref, *field_refs = refs
        else:
            acc_ref, corr_ref, *field_refs = refs
        for row in range(out_ref.shape[0]):
            total = mixed_row(row, corr_ref, field_refs)
            out_ref[row] = total if first else acc_ref[row] + total

    return kernel


def last_mix_kernel(acc_ref, corr_ref, field_ref, gram_ref, steps_ref, grads_ref, out_ref, message_ref, turn_ref, rows_ref):
    _, steps, rows, cols = steps_ref.shape
    slots = turn_ref.shape[0] // (rows * (cols // LANE))
    for row in range(rows):
        total = acc_ref[row] + mixed_row(row, corr_ref, [field_ref])
        for c in range(cols // LANE):
            base = (c * (rows // SUB) + row // SUB) * slots * SUB + row % SUB
            for begin, count in groups_of(steps):
                turn_ref[pl.ds(base + begin * SUB, count, stride=SUB), :] = total[begin:begin + count, c * LANE:(c + 1) * LANE]

    zero = jnp.zeros((SUB, LANE), jnp.float32)

    def body(step, sums):
        sums = list(sums)
        for c in range(cols // LANE):
            for r in range(0, rows, 2 * SUB):
                where = (step, pl.ds(r, 2 * SUB), pl.ds(c * LANE, LANE))
                halves = []
                for part in range(2):
                    base = (c * (rows // SUB) + r // SUB + part) * slots * SUB
                    halves.append(turn_ref[pl.ds(pl.multiple_of(base + step * SUB, SUB), SUB), :])
                mixed = jnp.concatenate(halves, axis=0)
                out_ref[where] = mixed
                half = mixed.astype(jnp.bfloat16).astype(jnp.float32)
                for n in range(NPROJ):
                    source = steps_ref if n < PAIRS else grads_ref
                    product = source[(n % PAIRS, *where)].astype(jnp.float32) * half
                    sums[n] = sums[n] + (product[:SUB] + product[SUB:])
        return tuple(sums)

    sums = lax.fori_loop(0, steps, body, (zero,) * NPROJ)
    rows_ref[0:NGRAM, :] = gram_ref[...]
    for n in range(NPROJ):
        rows_ref[NGRAM + n:NGRAM + n + 1, :] = jnp.sum(sums[n], axis=0, keepdims=True)
    lane, row = lane_index(), row_index()
    total = zero
    for first in range(0, NROW, SUB):
        summed = jnp.sum(rows_ref[first:first + SUB, :], axis=1, keepdims=True)
        total = total + jnp.where(lane == row + first, summed, 0.0)
    message = jnp.sum(total, axis=0, keepdims=True)
    message_ref[...] = jnp.broadcast_to(message[None], message_ref.shape)


def final_kernel(inbox_ref, mixed_ref, control_ref, steps_ref, grads_ref, out_ref, rows_ref):
    totals = jnp.sum(inbox_ref[...], axis=0)
    lane, row = lane_index(), row_index()
    spread = jnp.broadcast_to(totals, (SUB, LANE))
    for first in range(0, NROW, SUB):
        picked = jnp.where(lane == row + first, spread, 0.0)
        rows_ref[first:first + SUB, :] = jnp.broadcast_to(jnp.sum(picked, axis=1, keepdims=True), (SUB, LANE))

    def entry(k):
        return jnp.broadcast_to(rows_ref[k:k + 1, :], (SUB, LANE))

    cross = {pair: entry(k) for pair, k in WHERE.items()}

    def square(i, j):
        return entry(NSYM + WHERE[(min(i, j), max(i, j))])

    gamma = cross[(PAIRS - 1, PAIRS - 1)] / square(PAIRS - 1, PAIRS - 1)
    first = [None] * PAIRS
    for i in reversed(range(PAIRS)):
        rest = entry(NGRAM + i)
        for j in reversed(range(i + 1, PAIRS)):
            rest = rest - cross[(i, j)] * first[j]
        first[i] = rest / cross[(i, i)]
    second = [None] * PAIRS
    for i in range(PAIRS):
        inner = -entry(NGRAM + PAIRS + i)
        for j in range(PAIRS):
            inner = inner + square(i, j) * first[j]
        rest = cross[(i, i)] * first[i] + gamma * inner
        for j in range(i):
            rest = rest - cross[(j, i)] * second[j]
        second[i] = rest / cross[(i, i)]
    scaled = [gamma * value for value in first]

    _, steps, rows, cols = steps_ref.shape

    def body(step, carry):
        for c in range(0, cols, LANE):
            for r in range(0, rows, 2 * SUB):
                where = (step, pl.ds(r, 2 * SUB), pl.ds(c, LANE))
                mixed = mixed_ref[where]
                control = control_ref[where]
                update = [gamma * mixed[:SUB], gamma * mixed[SUB:]]
                for i in range(PAIRS):
                    s = steps_ref[(i, *where)].astype(jnp.float32)
                    y = grads_ref[(i, *where)].astype(jnp.float32)
                    for part, cut in enumerate((slice(0, SUB), slice(SUB, 2 * SUB))):
                        update[part] = update[part] + (second[i] * s[cut] - scaled[i] * y[cut])
                out_ref[step, pl.ds(r, SUB), pl.ds(c, LANE)] = control[:SUB] - update[0]
                out_ref[step, pl.ds(r + SUB, SUB), pl.ds(c, LANE)] = control[SUB:] - update[1]
        return carry

    lax.fori_loop(0, steps, body, 0)


def local(gradient, control, diffusivity, land_mask, time_corr, pair_steps, pair_grads):
    steps, rows, cols = gradient.shape
    height, breadth, groups = (lax.axis_size(axis) for axis in ("lat", "lon", "tm"))
    mine = lax.axis_index("tm")
    down = [(i, i + 1) for i in range(height - 1)]
    up = [(i + 1, i) for i in range(height - 1)]
    right = [(i, (i + 1) % breadth) for i in range(breadth)]
    left = [(j, i) for i, j in right]
    slots = slots_of(steps)
    turn = pltpu.VMEM((rows * (cols // LANE) * slots, LANE), jnp.float32)

    field, first, last = call(
        pack_kernel,
        (f32(rows, slots, cols), f32(HALO, slots, cols), f32(HALO, slots, cols)),
        [pltpu.with_memory_space_constraint(v, pltpu.HBM) for v in (gradient, land_mask, diffusivity)],
        specs=[HBM] * 3,
        scratch=[
            pltpu.VMEM((steps, rows, cols), jnp.float32), pltpu.VMEM((rows, cols), jnp.int32),
            pltpu.VMEM((rows, cols), jnp.float32), turn, pltpu.SemaphoreType.DMA((2 + len(groups_of(steps)),)),
        ],
        name="pack",
    )
    above = lax.ppermute(last, "lat", down)
    below = lax.ppermute(first, "lat", up)
    pair_shape = jax.ShapeDtypeStruct(pair_steps.shape, jnp.bfloat16)
    gram, pair_steps, pair_grads = call(
        gram_kernel, (f32(NGRAM, LANE), pair_shape, pair_shape),
        [pltpu.with_memory_space_constraint(v, pltpu.HBM) for v in (pair_steps, pair_grads)], specs=[HBM] * 2,
        scratch=[pltpu.SemaphoreType.DMA((2, 4))],
        name="gram",
    )
    side_shape = f32(slots, -(-(rows + 2 * HALO) // PER) * LANE)
    west, east = call(side_kernel, (side_shape, side_shape), (above, field, below, gram), name="sides")
    from_left = lax.ppermute(east, "lon", right)
    from_right = lax.ppermute(west, "lon", left)
    whole = (above, field, below, from_left, from_right)
    tall, wide = rows + 2 * HALO, cols + LANE
    weights = call(
        functools.partial(weight_kernel, steps=steps),
        (f32(tall + 1, SUB, wide), f32(tall, SUB, wide), f32(tall, SUB, wide), f32(tall, SUB, wide)), whole, name="weights",
    )
    own, other = [], []
    for begin, count in groups_of(steps):
        part = call(
            functools.partial(sweep_kernel, begin=begin), f32(rows, count, cols), (*whole, *weights), name="sweeps"
        )
        if not own:
            time_corr, part = lax.optimization_barrier((time_corr, part))
        own.append(part)
        for shift in range(1, groups):
            pairs = [(i, (i + shift) % groups) for i in range(groups)]
            source = lax.rem(mine - shift + groups, groups) * steps + begin
            other.append((corr_stack(time_corr, source, mine * steps, count, steps), lax.ppermute(part, "tm", pairs)))
    mixed = call(
        make_mix(True), f32(rows, steps, cols),
        (corr_stack(time_corr, mine * steps, mine * steps, steps, steps), *own), name="mix_own",
    )
    for corr, part in other[:-1]:
        mixed = call(make_mix(False), f32(rows, steps, cols), (mixed, corr, part), name="mix_more")
    mixed, message = call(
        last_mix_kernel, (f32(steps, rows, cols), f32(1, 1, LANE)),
        (mixed, *other[-1], gram, pair_steps, pair_grads),
        scratch=[turn, pltpu.VMEM((NROW, LANE), jnp.float32)], name="mix_last",
    )
    inbox = lax.all_gather(message, ("lat", "lon", "tm"), axis=0, tiled=True)
    return call(
        final_kernel, f32(steps, rows, cols), (inbox, mixed, control, pair_steps, pair_grads),
        scratch=[pltpu.VMEM((NROW, LANE), jnp.float32)], name="final",
    )


def solution(mesh):
    placed = (
        P("tm", "lat", "lon"),
        P("tm", "lat", "lon"),
        P("lat", "lon"),
        P("lat", "lon"),
        P(),
        P(None, "tm", "lat", "lon"),
        P(None, "tm", "lat", "lon"),
    )
    return jax.shard_map(
        local, mesh=mesh, in_specs=placed, out_specs=P("tm", "lat", "lon"), check_vma=False
    )
```

```python
import functools
import jax
import jax.numpy as jnp
from jax import lax
from jax.experimental import pallas as pl
from jax.experimental.pallas import tpu as pltpu
from jax.sharding import PartitionSpec as P

PAIRS = 8
SWEEPS = 6
SUB = 8
LANE = 128
HALO = SWEEPS
GROUP = 8
PER = LANE // GROUP
CROSS = [(i, j) for i in range(PAIRS) for j in range(i, PAIRS)]
NSYM = len(CROSS)
WHERE = {pair: k for k, pair in enumerate(CROSS)}
NGRAM = 2 * NSYM
NPROJ = 2 * PAIRS
NROW = NGRAM + NPROJ

VMEM = pl.BlockSpec(memory_space=pltpu.VMEM)
HBM = pl.BlockSpec(memory_space=pltpu.HBM)
PARAMS = pltpu.CompilerParams(vmem_limit_bytes=12 * 1024 * 1024)


def f32(*shape):
    return jax.ShapeDtypeStruct(shape, jnp.float32)


def call(kernel, outs, args, specs=None, scratch=(), name=None):
    single = not isinstance(outs, (tuple, list))
    return pl.pallas_call(
        kernel,
        out_shape=outs,
        in_specs=specs or [VMEM] * len(args),
        out_specs=VMEM if single else [VMEM] * len(outs),
        scratch_shapes=list(scratch),
        compiler_params=PARAMS,
        name=name,
    )(*args)


def lane_index():
    return lax.broadcasted_iota(jnp.int32, (SUB, LANE), 1)


def row_index():
    return lax.broadcasted_iota(jnp.int32, (SUB, LANE), 0)


def gram_kernel(steps_hbm, grads_hbm, out_ref, steps_ref, grads_ref, sems):
    _, steps, rows, cols = steps_ref.shape
    pieces = 4
    while steps % pieces:
        pieces -= 1
    count = steps // pieces
    copies = []
    for n in range(pieces):
        part = (slice(None), pl.ds(n * count, count))
        copies.append((
            pltpu.make_async_copy(steps_hbm.at[part], steps_ref.at[part], sems.at[0, n]),
            pltpu.make_async_copy(grads_hbm.at[part], grads_ref.at[part], sems.at[1, n]),
        ))
    for pair in copies:
        for copy in pair:
            copy.start()

    def make_body(half):
        def body(step, sums):
            sums = list(sums)
            for c in range(0, cols, LANE):
                for r in range(0, rows, 2 * SUB):
                    where = (step, pl.ds(r, 2 * SUB), pl.ds(c, LANE))
                    right = [grads_ref[(i, *where)].astype(jnp.float32) for i in range(PAIRS)]
                    left = right if half else [steps_ref[(i, *where)].astype(jnp.float32) for i in range(PAIRS)]
                    for part in range(2):
                        cut = slice(part * SUB, (part + 1) * SUB)
                        for k, (i, j) in enumerate(CROSS):
                            sums[k] = sums[k] + left[i][cut] * right[j][cut]
            return tuple(sums)

        return body

    zero = jnp.zeros((SUB, LANE), jnp.float32)
    sums = (zero,) * NSYM
    for n in range(pieces):
        for copy in copies[n]:
            copy.wait()
        sums = lax.fori_loop(n * count, (n + 1) * count, make_body(0), sums)
    for k in range(NSYM):
        out_ref[k:k + 1, :] = jnp.sum(sums[k], axis=0, keepdims=True)
    sums = lax.fori_loop(0, steps, make_body(1), (zero,) * NSYM)
    for k in range(NSYM):
        out_ref[NSYM + k:NSYM + k + 1, :] = jnp.sum(sums[k], axis=0, keepdims=True)


def groups_of(steps):
    return [(begin, min(SUB, steps - begin)) for begin in range(0, steps, SUB)]


def slots_of(steps):
    return -(-(steps + 1) // SUB) * SUB


def pack_kernel(grad_hbm, mask_hbm, diff_hbm, field_ref, first_ref, last_ref, grad_ref, mask_ref, diff_ref, turn_ref, sems):
    steps, rows, cols = grad_ref.shape
    slots = field_ref.shape[1]
    pieces = [(begin, min(SUB, steps - begin)) for begin in range(0, steps, SUB)]
    copies = [pltpu.make_async_copy(mask_hbm, mask_ref, sems.at[0]), pltpu.make_async_copy(diff_hbm, diff_ref, sems.at[1])]
    for n, (begin, count) in enumerate(pieces):
        part = pl.ds(begin, count)
        copies.append(pltpu.make_async_copy(grad_hbm.at[part], grad_ref.at[part], sems.at[2 + n]))
    for copy in copies:
        copy.start()
    copies[0].wait()
    copies[1].wait()
    zero = jnp.zeros((SUB, LANE), jnp.float32)
    tiles = [
        (slice(r * SUB, (r + 1) * SUB), slice(c * LANE, (c + 1) * LANE), (c * (rows // SUB) + r) * slots * SUB)
        for c in range(cols // LANE) for r in range(rows // SUB)
    ]
    mask = [mask_ref[down, across].astype(jnp.float32) for down, across, _ in tiles]
    for slot in range(steps, slots):
        for down, across, base in tiles:
            value = diff_ref[down, across] if slot == steps else zero
            turn_ref[base + slot * SUB:base + (slot + 1) * SUB, :] = value
    for n, (begin, count) in enumerate(pieces):
        copies[2 + n].wait()
        for slot in range(begin, begin + count):
            for (down, across, base), keep in zip(tiles, mask):
                turn_ref[base + slot * SUB:base + (slot + 1) * SUB, :] = grad_ref[slot, down, across] * keep
    for c in range(cols // LANE):
        across = slice(c * LANE, (c + 1) * LANE)
        for row in range(rows):
            base = (c * (rows // SUB) + row // SUB) * slots * SUB + row % SUB
            for slot in range(0, slots, SUB):
                value = turn_ref[pl.ds(base + slot * SUB, SUB, stride=SUB), :]
                field_ref[row, slot:slot + SUB, across] = value
                if row < HALO:
                    first_ref[row, slot:slot + SUB, across] = value
                if row >= rows - HALO:
                    last_ref[row - (rows - HALO), slot:slot + SUB, across] = value


def extended(row, above_ref, field_ref, below_ref):
    rows = field_ref.shape[0]
    if row < HALO:
        return above_ref, row
    if row < HALO + rows:
        return field_ref, row - HALO
    return below_ref, row - HALO - rows


def side_kernel(above_ref, field_ref, below_ref, order_ref, west_ref, east_ref):
    rows, slots, cols = field_ref.shape
    lane = lane_index()
    for slot in range(0, slots, SUB):
        down = slice(slot, slot + SUB)
        for base in range(0, rows + 2 * HALO, PER):
            west = east = jnp.zeros((SUB, LANE), jnp.float32)
            for row in range(base, min(base + PER, rows + 2 * HALO)):
                ref, at = extended(row, above_ref, field_ref, below_ref)
                begin = (row - base) * GROUP
                here = (lane >= begin) & (lane < begin + GROUP)
                left = ref[at, down, 0:LANE]
                right = ref[at, down, cols - LANE:cols]
                west = jnp.where(here, pltpu.roll(left, begin, 1) if begin else left, west)
                turn = (begin + GROUP) % LANE
                east = jnp.where(here, pltpu.roll(right, turn, 1) if turn else right, east)
            place = slice(base // PER * LANE, (base // PER + 1) * LANE)
            west_ref[down, place] = west
            east_ref[down, place] = east


def make_row_loader(above_ref, field_ref, below_ref, left_ref, right_ref):
    cols = field_ref.shape[2]
    lane = lane_index()

    def load(row, down, size):
        ref, at = extended(row, above_ref, field_ref, below_ref)
        place = slice(row // PER * LANE, (row // PER + 1) * LANE)
        begin = row % PER * GROUP
        tiles = [ref[at, down, c * LANE:(c + 1) * LANE] for c in range(cols // LANE)]
        east, west = right_ref[down, place], left_ref[down, place]
        if size == 1:
            tiles = [jnp.broadcast_to(tile, (SUB, LANE)) for tile in tiles]
            east, west = (jnp.broadcast_to(tile, (SUB, LANE)) for tile in (east, west))
        east = pltpu.roll(east, LANE - begin, 1) if begin else east
        turn = (2 * LANE - GROUP - begin) % LANE
        west = pltpu.roll(west, turn, 1) if turn else west
        return tiles + [jnp.where(lane < LANE // 2, east, west)]

    return load


def from_east(tiles, at_end):
    turned = [pltpu.roll(tile, LANE - 1, 1) for tile in tiles]
    return [jnp.where(at_end, turned[(c + 1) % len(tiles)], turned[c]) for c in range(len(tiles))]


def from_west(tiles, at_start):
    turned = [pltpu.roll(tile, 1, 1) for tile in tiles]
    return [jnp.where(at_start, turned[c - 1], turned[c]) for c in range(len(tiles))]


def weight_kernel(above_ref, field_ref, below_ref, left_ref, right_ref, south_ref, east_ref, west_ref, keep_ref, *, steps):
    rows, _, cols = field_ref.shape
    load = make_row_loader(above_ref, field_ref, below_ref, left_ref, right_ref)
    lane = lane_index()
    at_start, at_end = lane == 0, lane == LANE - 1
    height = rows + 2 * HALO
    above = None
    for row in range(height):
        kappa = load(row, slice(steps, steps + 1), 1)
        beside = from_east(kappa, at_end)
        east = [0.5 * (kappa[c] + beside[c]) for c in range(len(kappa))]
        west = from_west(east, at_start)
        for c in range(len(kappa)):
            across = slice(c * LANE, (c + 1) * LANE)
            east_ref[row, :, across] = east[c]
            west_ref[row, :, across] = west[c]
            keep_ref[row, :, across] = 1.0 - east[c] - west[c]
            if above is not None:
                south_ref[row - 1, :, across] = 0.5 * (above[c] + kappa[c])
            if row in (HALO - 1, HALO + rows):
                south_ref[height - 1 + (row >= HALO), :, across] = jnp.where(kappa[c] > 0.0, 1.0, 0.0)
        above = kappa


def sweep_kernel(
    above_ref, field_ref, below_ref, left_ref, right_ref, south_ref, east_ref, west_ref, keep_ref, out_ref, *, begin
):
    rows, _, cols = field_ref.shape
    height, width = rows + 2 * HALO, cols // LANE + 1
    count = out_ref.shape[1]
    lane = lane_index()
    at_start, at_end = lane == 0, lane == LANE - 1
    load = make_row_loader(above_ref, field_ref, below_ref, left_ref, right_ref)
    state = [None] * SWEEPS

    def at(ref, row, c):
        return ref[row, :, c * LANE:(c + 1) * LANE]

    def advance(sweep, row, tiles):
        before = state[sweep]
        if before is None:
            state[sweep] = (tiles, None)
            return None
        centre, north = before
        south = [at(south_ref, row - 1, c) * (tiles[c] - centre[c]) for c in range(width)]
        state[sweep] = (tiles, south)
        if north is None:
            return None
        ahead, behind = from_east(centre, at_end), from_west(centre, at_start)
        fresh = []
        for c in range(width):
            change = south[c] - north[c]
            if row - 1 < HALO:
                change = change * at(south_ref, height - 1, c)
            if row - 1 >= HALO + rows:
                change = change * at(south_ref, height, c)
            across = at(east_ref, row - 1, c) * ahead[c] + at(west_ref, row - 1, c) * behind[c]
            fresh.append(at(keep_ref, row - 1, c) * centre[c] + across + change)
        return fresh

    waiting = [None] * (SWEEPS + 1)
    for tick in range(height + SWEEPS + 1):
        if waiting[SWEEPS] is not None:
            row, tiles = waiting[SWEEPS]
            for c in range(width - 1):
                out_ref[row - HALO, :, c * LANE:(c + 1) * LANE] = tiles[c][:count]
        for sweep in reversed(range(SWEEPS)):
            if sweep == 0:
                entry = (tick, load(tick, slice(begin, begin + SUB), SUB)) if tick < height else None
            else:
                entry = waiting[sweep]
            waiting[sweep + 1] = None
            if entry is not None:
                fresh = advance(sweep, *entry)
                if fresh is not None:
                    waiting[sweep + 1] = (entry[0] - 1, fresh)


def split_stack(value):
    high = value.astype(jnp.bfloat16).astype(jnp.float32)
    rest = value - high
    middle = rest.astype(jnp.bfloat16).astype(jnp.float32)
    low = rest - middle
    return jnp.concatenate([high, middle, high, low, middle, high], axis=0).astype(jnp.bfloat16)


def corr_stack(time_corr, source, target, count, steps):
    block = lax.dynamic_slice(time_corr, (source, target), (count, steps))
    block = jnp.pad(block, ((0, -count % SUB), (0, 0))).T
    high = lax.reduce_precision(block, 8, 7)
    rest = block - high
    middle = lax.reduce_precision(rest, 8, 7)
    low = rest - middle
    return jnp.concatenate([high, high, middle, high, middle, low], axis=1).astype(jnp.bfloat16)


def mixed_row(row, corr_ref, field_refs):
    parts = []
    for ref in field_refs:
        part = ref[row]
        parts.append(part)
        if -part.shape[0] % SUB:
            parts.append(jnp.zeros((-part.shape[0] % SUB, part.shape[1]), jnp.float32))
    stacked = split_stack(jnp.concatenate(parts, axis=0) if len(parts) > 1 else parts[0])
    return jnp.dot(corr_ref[...], stacked, preferred_element_type=jnp.float32)


def make_mix(first):
    def kernel(*refs):
        *refs, out_ref = refs
        if first:
            corr_ref, *field_refs = refs
        else:
            acc_ref, corr_ref, *field_refs = refs
        for row in range(out_ref.shape[0]):
            total = mixed_row(row, corr_ref, field_refs)
            out_ref[row] = total if first else acc_ref[row] + total

    return kernel


def last_mix_kernel(acc_ref, corr_ref, field_ref, gram_ref, steps_ref, grads_ref, out_ref, message_ref, turn_ref, rows_ref):
    _, steps, rows, cols = steps_ref.shape
    slots = turn_ref.shape[0] // (rows * (cols // LANE))
    for row in range(rows):
        total = acc_ref[row] + mixed_row(row, corr_ref, [field_ref])
        for c in range(cols // LANE):
            base = (c * (rows // SUB) + row // SUB) * slots * SUB + row % SUB
            for begin, count in groups_of(steps):
                turn_ref[pl.ds(base + begin * SUB, count, stride=SUB), :] = total[begin:begin + count, c * LANE:(c + 1) * LANE]

    zero = jnp.zeros((SUB, LANE), jnp.float32)

    def body(step, sums):
        sums = list(sums)
        for c in range(cols // LANE):
            for r in range(0, rows, 2 * SUB):
                where = (step, pl.ds(r, 2 * SUB), pl.ds(c * LANE, LANE))
                halves = []
                for part in range(2):
                    base = (c * (rows // SUB) + r // SUB + part) * slots * SUB
                    halves.append(turn_ref[pl.ds(pl.multiple_of(base + step * SUB, SUB), SUB), :])
                mixed = jnp.concatenate(halves, axis=0)
                out_ref[where] = mixed
                half = mixed.astype(jnp.bfloat16).astype(jnp.float32)
                for n in range(NPROJ):
                    source = steps_ref if n < PAIRS else grads_ref
                    product = source[(n % PAIRS, *where)].astype(jnp.float32) * half
                    sums[n] = sums[n] + (product[:SUB] + product[SUB:])
        return tuple(sums)

    sums = lax.fori_loop(0, steps, body, (zero,) * NPROJ)
    rows_ref[0:NGRAM, :] = gram_ref[...]
    for n in range(NPROJ):
        rows_ref[NGRAM + n:NGRAM + n + 1, :] = jnp.sum(sums[n], axis=0, keepdims=True)
    lane, row = lane_index(), row_index()
    total = zero
    for first in range(0, NROW, SUB):
        summed = jnp.sum(rows_ref[first:first + SUB, :], axis=1, keepdims=True)
        total = total + jnp.where(lane == row + first, summed, 0.0)
    message = jnp.sum(total, axis=0, keepdims=True)
    message_ref[...] = jnp.broadcast_to(message[None], message_ref.shape)


def final_kernel(inbox_ref, mixed_ref, control_ref, steps_ref, grads_ref, out_ref, rows_ref):
    totals = jnp.sum(inbox_ref[...], axis=0)
    lane, row = lane_index(), row_index()
    spread = jnp.broadcast_to(totals, (SUB, LANE))
    for first in range(0, NROW, SUB):
        picked = jnp.where(lane == row + first, spread, 0.0)
        rows_ref[first:first + SUB, :] = jnp.broadcast_to(jnp.sum(picked, axis=1, keepdims=True), (SUB, LANE))

    def entry(k):
        return jnp.broadcast_to(rows_ref[k:k + 1, :], (SUB, LANE))

    cross = {pair: entry(k) for pair, k in WHERE.items()}

    def square(i, j):
        return entry(NSYM + WHERE[(min(i, j), max(i, j))])

    gamma = cross[(PAIRS - 1, PAIRS - 1)] / square(PAIRS - 1, PAIRS - 1)
    first = [None] * PAIRS
    for i in reversed(range(PAIRS)):
        rest = entry(NGRAM + i)
        for j in reversed(range(i + 1, PAIRS)):
            rest = rest - cross[(i, j)] * first[j]
        first[i] = rest / cross[(i, i)]
    second = [None] * PAIRS
    for i in range(PAIRS):
        inner = -entry(NGRAM + PAIRS + i)
        for j in range(PAIRS):
            inner = inner + square(i, j) * first[j]
        rest = cross[(i, i)] * first[i] + gamma * inner
        for j in range(i):
            rest = rest - cross[(j, i)] * second[j]
        second[i] = rest / cross[(i, i)]
    scaled = [gamma * value for value in first]

    _, steps, rows, cols = steps_ref.shape

    def body(step, carry):
        for c in range(0, cols, LANE):
            for r in range(0, rows, 2 * SUB):
                where = (step, pl.ds(r, 2 * SUB), pl.ds(c, LANE))
                mixed = mixed_ref[where]
                control = control_ref[where]
                update = [gamma * mixed[:SUB], gamma * mixed[SUB:]]
                for i in range(PAIRS):
                    s = steps_ref[(i, *where)].astype(jnp.float32)
                    y = grads_ref[(i, *where)].astype(jnp.float32)
                    for part, cut in enumerate((slice(0, SUB), slice(SUB, 2 * SUB))):
                        update[part] = update[part] + (second[i] * s[cut] - scaled[i] * y[cut])
                out_ref[step, pl.ds(r, SUB), pl.ds(c, LANE)] = control[:SUB] - update[0]
                out_ref[step, pl.ds(r + SUB, SUB), pl.ds(c, LANE)] = control[SUB:] - update[1]
        return carry

    lax.fori_loop(0, steps, body, 0)


def local(gradient, control, diffusivity, land_mask, time_corr, pair_steps, pair_grads):
    steps, rows, cols = gradient.shape
    height, breadth, groups = (lax.axis_size(axis) for axis in ("lat", "lon", "tm"))
    mine = lax.axis_index("tm")
    down = [(i, i + 1) for i in range(height - 1)]
    up = [(i + 1, i) for i in range(height - 1)]
    right = [(i, (i + 1) % breadth) for i in range(breadth)]
    left = [(j, i) for i, j in right]
    slots = slots_of(steps)
    turn = pltpu.VMEM((rows * (cols // LANE) * slots, LANE), jnp.float32)

    field, first, last = call(
        pack_kernel,
        (f32(rows, slots, cols), f32(HALO, slots, cols), f32(HALO, slots, cols)),
        [pltpu.with_memory_space_constraint(v, pltpu.HBM) for v in (gradient, land_mask, diffusivity)],
        specs=[HBM] * 3,
        scratch=[
            pltpu.VMEM((steps, rows, cols), jnp.float32), pltpu.VMEM((rows, cols), jnp.int32),
            pltpu.VMEM((rows, cols), jnp.float32), turn, pltpu.SemaphoreType.DMA((2 + len(groups_of(steps)),)),
        ],
        name="pack",
    )
    above = lax.ppermute(last, "lat", down)
    below = lax.ppermute(first, "lat", up)
    pair_shape = jax.ShapeDtypeStruct(pair_steps.shape, jnp.bfloat16)
    gram, pair_steps, pair_grads = call(
        gram_kernel, (f32(NGRAM, LANE), pair_shape, pair_shape),
        [pltpu.with_memory_space_constraint(v, pltpu.HBM) for v in (pair_steps, pair_grads)], specs=[HBM] * 2,
        scratch=[pltpu.SemaphoreType.DMA((2, 4))],
        name="gram",
    )
    side_shape = f32(slots, -(-(rows + 2 * HALO) // PER) * LANE)
    west, east = call(side_kernel, (side_shape, side_shape), (above, field, below, gram), name="sides")
    from_left = lax.ppermute(east, "lon", right)
    from_right = lax.ppermute(west, "lon", left)
    whole = (above, field, below, from_left, from_right)
    tall, wide = rows + 2 * HALO, cols + LANE
    weights = call(
        functools.partial(weight_kernel, steps=steps),
        (f32(tall + 1, SUB, wide), f32(tall, SUB, wide), f32(tall, SUB, wide), f32(tall, SUB, wide)), whole, name="weights",
    )
    own, other = [], []
    for begin, count in groups_of(steps):
        part = call(
            functools.partial(sweep_kernel, begin=begin), f32(rows, count, cols), (*whole, *weights), name="sweeps"
        )
        if not own:
            time_corr, part = lax.optimization_barrier((time_corr, part))
        own.append(part)
        for shift in range(1, groups):
            pairs = [(i, (i + shift) % groups) for i in range(groups)]
            source = lax.rem(mine - shift + groups, groups) * steps + begin
            other.append((corr_stack(time_corr, source, mine * steps, count, steps), lax.ppermute(part, "tm", pairs)))
    mixed = call(
        make_mix(True), f32(rows, steps, cols),
        (corr_stack(time_corr, mine * steps, mine * steps, steps, steps), *own), name="mix_own",
    )
    for corr, part in other[:-1]:
        mixed = call(make_mix(False), f32(rows, steps, cols), (mixed, corr, part), name="mix_more")
    devices = height * breadth * groups
    mixed, message = call(
        last_mix_kernel, (f32(steps, rows, cols), f32(devices, 1, LANE)),
        (mixed, *other[-1], gram, pair_steps, pair_grads),
        scratch=[turn, pltpu.VMEM((NROW, LANE), jnp.float32)], name="mix_last",
    )
    inbox = lax.all_to_all(message, ("lat", "lon", "tm"), split_axis=0, concat_axis=0, tiled=True)
    return call(
        final_kernel, f32(steps, rows, cols), (inbox, mixed, control, pair_steps, pair_grads),
        scratch=[pltpu.VMEM((NROW, LANE), jnp.float32)], name="final",
    )


def solution(mesh):
    placed = (
        P("tm", "lat", "lon"),
        P("tm", "lat", "lon"),
        P("lat", "lon"),
        P("lat", "lon"),
        P(),
        P(None, "tm", "lat", "lon"),
        P(None, "tm", "lat", "lon"),
    )
    return jax.shard_map(
        local, mesh=mesh, in_specs=placed, out_specs=P("tm", "lat", "lon"), check_vma=False
    )
```

```python
import functools
import jax
import jax.numpy as jnp
from jax import lax
from jax.experimental import pallas as pl
from jax.experimental.pallas import tpu as pltpu
from jax.sharding import PartitionSpec as P

PAIRS = 8
SWEEPS = 6
SUB = 8
LANE = 128
HALO = SWEEPS
GROUP = 8
PER = LANE // GROUP
CROSS = [(i, j) for i in range(PAIRS) for j in range(i, PAIRS)]
NSYM = len(CROSS)
WHERE = {pair: k for k, pair in enumerate(CROSS)}
NGRAM = 2 * NSYM
NPROJ = 2 * PAIRS
NROW = NGRAM + NPROJ

VMEM = pl.BlockSpec(memory_space=pltpu.VMEM)
HBM = pl.BlockSpec(memory_space=pltpu.HBM)
PARAMS = pltpu.CompilerParams(vmem_limit_bytes=12 * 1024 * 1024)


def f32(*shape):
    return jax.ShapeDtypeStruct(shape, jnp.float32)


def call(kernel, outs, args, specs=None, scratch=(), name=None):
    single = not isinstance(outs, (tuple, list))
    return pl.pallas_call(
        kernel,
        out_shape=outs,
        in_specs=specs or [VMEM] * len(args),
        out_specs=VMEM if single else [VMEM] * len(outs),
        scratch_shapes=list(scratch),
        compiler_params=PARAMS,
        name=name,
    )(*args)


def lane_index():
    return lax.broadcasted_iota(jnp.int32, (SUB, LANE), 1)


def row_index():
    return lax.broadcasted_iota(jnp.int32, (SUB, LANE), 0)


def gram_kernel(steps_hbm, grads_hbm, out_ref, steps_ref, grads_ref, sems):
    _, steps, rows, cols = steps_ref.shape
    pieces = 4
    while steps % pieces:
        pieces -= 1
    count = steps // pieces
    copies = []
    for n in range(pieces):
        part = (slice(None), pl.ds(n * count, count))
        copies.append((
            pltpu.make_async_copy(steps_hbm.at[part], steps_ref.at[part], sems.at[0, n]),
            pltpu.make_async_copy(grads_hbm.at[part], grads_ref.at[part], sems.at[1, n]),
        ))
    for pair in copies:
        for copy in pair:
            copy.start()

    def make_body(half):
        def body(step, sums):
            sums = list(sums)
            for c in range(0, cols, LANE):
                for r in range(0, rows, 2 * SUB):
                    where = (step, pl.ds(r, 2 * SUB), pl.ds(c, LANE))
                    right = [grads_ref[(i, *where)].astype(jnp.float32) for i in range(PAIRS)]
                    left = right if half else [steps_ref[(i, *where)].astype(jnp.float32) for i in range(PAIRS)]
                    for part in range(2):
                        cut = slice(part * SUB, (part + 1) * SUB)
                        for k, (i, j) in enumerate(CROSS):
                            sums[k] = sums[k] + left[i][cut] * right[j][cut]
            return tuple(sums)

        return body

    zero = jnp.zeros((SUB, LANE), jnp.float32)
    sums = (zero,) * NSYM
    for n in range(pieces):
        for copy in copies[n]:
            copy.wait()
        sums = lax.fori_loop(n * count, (n + 1) * count, make_body(0), sums)
    for k in range(NSYM):
        out_ref[k:k + 1, :] = jnp.sum(sums[k], axis=0, keepdims=True)
    sums = lax.fori_loop(0, steps, make_body(1), (zero,) * NSYM)
    for k in range(NSYM):
        out_ref[NSYM + k:NSYM + k + 1, :] = jnp.sum(sums[k], axis=0, keepdims=True)


def groups_of(steps):
    return [(begin, min(SUB, steps - begin)) for begin in range(0, steps, SUB)]


def slots_of(steps):
    return -(-(steps + 1) // SUB) * SUB


def pack_kernel(grad_hbm, mask_hbm, diff_hbm, field_ref, swap_ref, next_ref, grad_ref, mask_ref, diff_ref, turn_ref, sems):
    steps, rows, cols = grad_ref.shape
    slots = field_ref.shape[1]
    pieces = [(begin, min(SUB, steps - begin)) for begin in range(0, steps, SUB)]
    copies = [pltpu.make_async_copy(mask_hbm, mask_ref, sems.at[0]), pltpu.make_async_copy(diff_hbm, diff_ref, sems.at[1])]
    for n, (begin, count) in enumerate(pieces):
        part = pl.ds(begin, count)
        copies.append(pltpu.make_async_copy(grad_hbm.at[part], grad_ref.at[part], sems.at[2 + n]))
    for copy in copies:
        copy.start()
    copies[0].wait()
    copies[1].wait()
    zero = jnp.zeros((SUB, LANE), jnp.float32)
    tiles = [
        (slice(r * SUB, (r + 1) * SUB), slice(c * LANE, (c + 1) * LANE), (c * (rows // SUB) + r) * slots * SUB)
        for c in range(cols // LANE) for r in range(rows // SUB)
    ]
    mask = [mask_ref[down, across].astype(jnp.float32) for down, across, _ in tiles]
    for slot in range(steps, slots):
        for down, across, base in tiles:
            value = diff_ref[down, across] if slot == steps else zero
            turn_ref[base + slot * SUB:base + (slot + 1) * SUB, :] = value
    for n, (begin, count) in enumerate(pieces):
        copies[2 + n].wait()
        for slot in range(begin, begin + count):
            for (down, across, base), keep in zip(tiles, mask):
                turn_ref[base + slot * SUB:base + (slot + 1) * SUB, :] = grad_ref[slot, down, across] * keep
    for c in range(cols // LANE):
        across = slice(c * LANE, (c + 1) * LANE)
        for row in range(rows):
            base = (c * (rows // SUB) + row // SUB) * slots * SUB + row % SUB
            for slot in range(0, slots, SUB):
                value = turn_ref[pl.ds(base + slot * SUB, SUB, stride=SUB), :]
                field_ref[row, slot:slot + SUB, across] = value
    odd = lax.rem(lax.axis_index("lat"), 2)
    near, far = (1 - odd) * (rows - HALO), odd * (rows - HALO)
    for row in range(HALO):
        swap_ref[row] = field_ref[near + row]
        next_ref[row] = field_ref[far + row]


def side_kernel(swap_ref, field_ref, next_ref, order_ref, whole_ref, west_ref, east_ref):
    rows, slots, cols = field_ref.shape
    odd = lax.rem(lax.axis_index("lat"), 2)
    near, far = (1 - odd) * (HALO + rows), odd * (HALO + rows)
    for row in range(HALO):
        whole_ref[near + row] = swap_ref[row]
        whole_ref[far + row] = next_ref[row]
    for row in range(rows):
        whole_ref[HALO + row] = field_ref[row]
    lane = lane_index()
    for slot in range(0, slots, SUB):
        down = slice(slot, slot + SUB)
        for base in range(0, rows + 2 * HALO, PER):
            west = east = jnp.zeros((SUB, LANE), jnp.float32)
            for row in range(base, min(base + PER, rows + 2 * HALO)):
                begin = (row - base) * GROUP
                here = (lane >= begin) & (lane < begin + GROUP)
                left = whole_ref[row, down, 0:LANE]
                right = whole_ref[row, down, cols - LANE:cols]
                west = jnp.where(here, pltpu.roll(left, begin, 1) if begin else left, west)
                turn = (begin + GROUP) % LANE
                east = jnp.where(here, pltpu.roll(right, turn, 1) if turn else right, east)
            place = slice(base // PER * LANE, (base // PER + 1) * LANE)
            west_ref[down, place] = west
            east_ref[down, place] = east


def make_row_loader(whole_ref, left_ref, right_ref):
    cols = whole_ref.shape[2]
    lane = lax.broadcasted_iota(jnp.int32, (1, LANE), 1)

    def load(row, down):
        place = slice(row // PER * LANE, (row // PER + 1) * LANE)
        begin = row % PER * GROUP
        tiles = [whole_ref[row, down, c * LANE:(c + 1) * LANE] for c in range(cols // LANE)]
        east, west = right_ref[down, place], left_ref[down, place]
        east = pltpu.roll(east, LANE - begin, 1) if begin else east
        turn = (2 * LANE - GROUP - begin) % LANE
        west = pltpu.roll(west, turn, 1) if turn else west
        return tiles + [jnp.where(lane < LANE // 2, east, west)]

    return load


def from_east(tiles, at_end):
    turned = [pltpu.roll(tile, LANE - 1, 1) for tile in tiles]
    return [jnp.where(at_end, turned[(c + 1) % len(tiles)], turned[c]) for c in range(len(tiles))]


def from_west(tiles, at_start):
    turned = [pltpu.roll(tile, 1, 1) for tile in tiles]
    return [jnp.where(at_start, turned[c - 1], turned[c]) for c in range(len(tiles))]


def weight_kernel(
    whole_ref, left_ref, right_ref, south_ref, east_ref, west_ref, keep_ref, kappa_ref, packed_ref, *, steps
):
    height, _, cols = whole_ref.shape
    width = cols // LANE + 1
    load = make_row_loader(whole_ref, left_ref, right_ref)
    lane = lane_index()
    at_start, at_end = lane == 0, lane == LANE - 1
    for row in range(height):
        for c, tile in enumerate(load(row, slice(steps, steps + 1))):
            kappa_ref[row:row + 1, c * LANE:(c + 1) * LANE] = tile
    for first in range(0, height, SUB):
        down = slice(first, first + SUB)
        kappa = [kappa_ref[down, c * LANE:(c + 1) * LANE] for c in range(width)]
        below = [kappa_ref[first + 1:first + 1 + SUB, c * LANE:(c + 1) * LANE] for c in range(width)]
        beside = from_east(kappa, at_end)
        east = [0.5 * (kappa[c] + beside[c]) for c in range(width)]
        west = from_west(east, at_start)
        for c in range(width):
            across = slice(c * LANE, (c + 1) * LANE)
            packed_ref[0, down, across] = 0.5 * (kappa[c] + below[c])
            packed_ref[1, down, across] = east[c]
            packed_ref[2, down, across] = west[c]
            packed_ref[3, down, across] = 1.0 - east[c] - west[c]
    for n, ref in enumerate((south_ref, east_ref, west_ref, keep_ref)):
        for row in range(height - 1):
            ref[row] = jnp.broadcast_to(packed_ref[n, row:row + 1, :], ref.shape[1:])
    for side, row in enumerate((HALO - 1, height - HALO)):
        inside = jnp.where(kappa_ref[row:row + 1, :] > 0.0, 1.0, 0.0)
        south_ref[height - 1 + side] = jnp.broadcast_to(inside, south_ref.shape[1:])


def sweep_kernel(whole_ref, left_ref, right_ref, south_ref, east_ref, west_ref, keep_ref, out_ref, *, begin):
    height, _, cols = whole_ref.shape
    rows, width = height - 2 * HALO, cols // LANE + 1
    count = out_ref.shape[1]
    lane = lane_index()
    at_start, at_end = lane == 0, lane == LANE - 1
    load = make_row_loader(whole_ref, left_ref, right_ref)
    state = [None] * SWEEPS

    def at(ref, row, c):
        return ref[row, :, c * LANE:(c + 1) * LANE]

    def advance(sweep, row, tiles):
        before = state[sweep]
        if before is None:
            state[sweep] = (tiles, None)
            return None
        centre, north = before
        south = [at(south_ref, row - 1, c) * (tiles[c] - centre[c]) for c in range(width)]
        state[sweep] = (tiles, south)
        if north is None:
            return None
        ahead, behind = from_east(centre, at_end), from_west(centre, at_start)
        fresh = []
        for c in range(width):
            change = south[c] - north[c]
            if row - 1 < HALO:
                change = change * at(south_ref, height - 1, c)
            if row - 1 >= HALO + rows:
                change = change * at(south_ref, height, c)
            across = at(east_ref, row - 1, c) * ahead[c] + at(west_ref, row - 1, c) * behind[c]
            fresh.append(at(keep_ref, row - 1, c) * centre[c] + across + change)
        return fresh

    waiting = [None] * (SWEEPS + 1)
    for tick in range(height + SWEEPS + 1):
        if waiting[SWEEPS] is not None:
            row, tiles = waiting[SWEEPS]
            for c in range(width - 1):
                out_ref[row - HALO, :, c * LANE:(c + 1) * LANE] = tiles[c][:count]
        for sweep in reversed(range(SWEEPS)):
            if sweep == 0:
                entry = (tick, load(tick, slice(begin, begin + SUB))) if tick < height else None
            else:
                entry = waiting[sweep]
            waiting[sweep + 1] = None
            if entry is not None:
                fresh = advance(sweep, *entry)
                if fresh is not None:
                    waiting[sweep + 1] = (entry[0] - 1, fresh)


def split_stack(value):
    high = value.astype(jnp.bfloat16).astype(jnp.float32)
    rest = value - high
    middle = rest.astype(jnp.bfloat16).astype(jnp.float32)
    low = rest - middle
    return jnp.concatenate([high, middle, high, low, middle, high], axis=0).astype(jnp.bfloat16)


def corr_kernel(corr_ref, *out_refs, groups, steps, sources):
    mine = lax.axis_index("tm")
    for at in range(groups):
        @pl.when(mine == at)
        def _(at=at):
            for (shift, begin, count), out_ref in zip(sources, out_refs):
                source = (at - shift) % groups * steps + begin
                block = corr_ref[source:source + count, at * steps:(at + 1) * steps]
                high = block.astype(jnp.bfloat16).astype(jnp.float32)
                rest = block - high
                middle = rest.astype(jnp.bfloat16).astype(jnp.float32)
                low = rest - middle
                depth = out_ref.shape[1] // 6
                pad = [jnp.zeros((depth - count, steps), jnp.float32)] if depth > count else []
                stack = []
                for part in (high, high, middle, high, middle, low):
                    stack += [part, *pad]
                out_ref[...] = jnp.concatenate(stack, axis=0).T.astype(jnp.bfloat16)


def mixed_row(row, corr_ref, field_refs):
    parts = []
    for ref in field_refs:
        part = ref[row]
        parts.append(part)
        if -part.shape[0] % SUB:
            parts.append(jnp.zeros((-part.shape[0] % SUB, part.shape[1]), jnp.float32))
    stacked = split_stack(jnp.concatenate(parts, axis=0) if len(parts) > 1 else parts[0])
    return jnp.dot(corr_ref[...], stacked, preferred_element_type=jnp.float32)


def make_mix(first):
    def kernel(*refs):
        *refs, out_ref = refs
        if first:
            corr_ref, *field_refs = refs
        else:
            acc_ref, corr_ref, *field_refs = refs
        for row in range(out_ref.shape[0]):
            total = mixed_row(row, corr_ref, field_refs)
            out_ref[row] = total if first else acc_ref[row] + total

    return kernel


def last_mix_kernel(acc_ref, corr_ref, field_ref, gram_ref, steps_ref, grads_ref, out_ref, message_ref, turn_ref, rows_ref):
    _, steps, rows, cols = steps_ref.shape
    slots = turn_ref.shape[0] // (rows * (cols // LANE))
    for row in range(rows):
        total = acc_ref[row] + mixed_row(row, corr_ref, [field_ref])
        for c in range(cols // LANE):
            base = (c * (rows // SUB) + row // SUB) * slots * SUB + row % SUB
            for begin, count in groups_of(steps):
                turn_ref[pl.ds(base + begin * SUB, count, stride=SUB), :] = total[begin:begin + count, c * LANE:(c + 1) * LANE]

    zero = jnp.zeros((SUB, LANE), jnp.float32)

    def body(step, sums):
        sums = list(sums)
        for c in range(cols // LANE):
            for r in range(0, rows, 2 * SUB):
                where = (step, pl.ds(r, 2 * SUB), pl.ds(c * LANE, LANE))
                halves = []
                for part in range(2):
                    base = (c * (rows // SUB) + r // SUB + part) * slots * SUB
                    halves.append(turn_ref[pl.ds(pl.multiple_of(base + step * SUB, SUB), SUB), :])
                mixed = jnp.concatenate(halves, axis=0)
                out_ref[where] = mixed
                half = mixed.astype(jnp.bfloat16).astype(jnp.float32)
                for n in range(NPROJ):
                    source = steps_ref if n < PAIRS else grads_ref
                    product = source[(n % PAIRS, *where)].astype(jnp.float32) * half
                    sums[n] = sums[n] + (product[:SUB] + product[SUB:])
        return tuple(sums)

    sums = lax.fori_loop(0, steps, body, (zero,) * NPROJ)
    rows_ref[0:NGRAM, :] = gram_ref[...]
    for n in range(NPROJ):
        rows_ref[NGRAM + n:NGRAM + n + 1, :] = jnp.sum(sums[n], axis=0, keepdims=True)
    lane, row = lane_index(), row_index()
    total = zero
    for first in range(0, NROW, SUB):
        summed = jnp.sum(rows_ref[first:first + SUB, :], axis=1, keepdims=True)
        total = total + jnp.where(lane == row + first, summed, 0.0)
    message = jnp.sum(total, axis=0, keepdims=True)
    message_ref[...] = jnp.broadcast_to(message[None], message_ref.shape)


def final_kernel(inbox_ref, mixed_ref, control_ref, steps_ref, grads_ref, out_ref, rows_ref):
    totals = jnp.sum(inbox_ref[...], axis=0)
    lane, row = lane_index(), row_index()
    spread = jnp.broadcast_to(totals, (SUB, LANE))
    for first in range(0, NROW, SUB):
        picked = jnp.where(lane == row + first, spread, 0.0)
        rows_ref[first:first + SUB, :] = jnp.broadcast_to(jnp.sum(picked, axis=1, keepdims=True), (SUB, LANE))

    def entry(k):
        return jnp.broadcast_to(rows_ref[k:k + 1, :], (SUB, LANE))

    cross = {pair: entry(k) for pair, k in WHERE.items()}

    def square(i, j):
        return entry(NSYM + WHERE[(min(i, j), max(i, j))])

    gamma = cross[(PAIRS - 1, PAIRS - 1)] / square(PAIRS - 1, PAIRS - 1)
    first = [None] * PAIRS
    for i in reversed(range(PAIRS)):
        rest = entry(NGRAM + i)
        for j in reversed(range(i + 1, PAIRS)):
            rest = rest - cross[(i, j)] * first[j]
        first[i] = rest / cross[(i, i)]
    second = [None] * PAIRS
    for i in range(PAIRS):
        inner = -entry(NGRAM + PAIRS + i)
        for j in range(PAIRS):
            inner = inner + square(i, j) * first[j]
        rest = cross[(i, i)] * first[i] + gamma * inner
        for j in range(i):
            rest = rest - cross[(j, i)] * second[j]
        second[i] = rest / cross[(i, i)]
    scaled = [gamma * value for value in first]

    _, steps, rows, cols = steps_ref.shape

    def body(step, carry):
        for c in range(0, cols, LANE):
            for r in range(0, rows, 2 * SUB):
                where = (step, pl.ds(r, 2 * SUB), pl.ds(c, LANE))
                mixed = mixed_ref[where]
                control = control_ref[where]
                update = [gamma * mixed[:SUB], gamma * mixed[SUB:]]
                for i in range(PAIRS):
                    s = steps_ref[(i, *where)].astype(jnp.float32)
                    y = grads_ref[(i, *where)].astype(jnp.float32)
                    for part, cut in enumerate((slice(0, SUB), slice(SUB, 2 * SUB))):
                        update[part] = update[part] + (second[i] * s[cut] - scaled[i] * y[cut])
                out_ref[step, pl.ds(r, SUB), pl.ds(c, LANE)] = control[:SUB] - update[0]
                out_ref[step, pl.ds(r + SUB, SUB), pl.ds(c, LANE)] = control[SUB:] - update[1]
        return carry

    lax.fori_loop(0, steps, body, 0)


def local(gradient, control, diffusivity, land_mask, time_corr, pair_steps, pair_grads):
    steps, rows, cols = gradient.shape
    height, breadth, groups = (lax.axis_size(axis) for axis in ("lat", "lon", "tm"))
    even = [(i, j) for k in range(0, height - 1, 2) for i, j in ((k, k + 1), (k + 1, k))]
    odd = [(i, j) for k in range(1, height - 1, 2) for i, j in ((k, k + 1), (k + 1, k))]
    right = [(i, (i + 1) % breadth) for i in range(breadth)]
    left = [(j, i) for i, j in right]
    slots = slots_of(steps)
    turn = pltpu.VMEM((rows * (cols // LANE) * slots, LANE), jnp.float32)

    field, to_swap, to_next = call(
        pack_kernel,
        (f32(rows, slots, cols), f32(HALO, slots, cols), f32(HALO, slots, cols)),
        [pltpu.with_memory_space_constraint(v, pltpu.HBM) for v in (gradient, land_mask, diffusivity)],
        specs=[HBM] * 3,
        scratch=[
            pltpu.VMEM((steps, rows, cols), jnp.float32), pltpu.VMEM((rows, cols), jnp.int32),
            pltpu.VMEM((rows, cols), jnp.float32), turn, pltpu.SemaphoreType.DMA((2 + len(groups_of(steps)),)),
        ],
        name="pack",
    )
    from_swap = lax.ppermute(to_swap, "lat", even)
    from_next = lax.ppermute(to_next, "lat", odd)
    pair_shape = jax.ShapeDtypeStruct(pair_steps.shape, jnp.bfloat16)
    gram, pair_steps, pair_grads = call(
        gram_kernel, (f32(NGRAM, LANE), pair_shape, pair_shape),
        [pltpu.with_memory_space_constraint(v, pltpu.HBM) for v in (pair_steps, pair_grads)], specs=[HBM] * 2,
        scratch=[pltpu.SemaphoreType.DMA((2, 4))],
        name="gram",
    )
    tall, wide = rows + 2 * HALO, cols + LANE
    parts = groups_of(steps)
    sources = [(0, 0, steps)] + [(shift, *part) for part in parts for shift in range(1, groups)]
    own_corr, *corrs = call(
        functools.partial(corr_kernel, groups=groups, steps=steps, sources=sources),
        [jax.ShapeDtypeStruct((steps, 6 * (count + -count % SUB)), jnp.bfloat16) for _, _, count in sources],
        (time_corr,), name="corr",
    )
    side_shape = f32(slots, -(-tall // PER) * LANE)
    whole, west, east = call(
        side_kernel, (f32(tall, slots, cols), side_shape, side_shape), (from_swap, field, from_next, gram), name="sides"
    )
    from_left = lax.ppermute(east, "lon", right)
    from_right = lax.ppermute(west, "lon", left)
    extended = (whole, from_left, from_right)
    weights = call(
        functools.partial(weight_kernel, steps=steps),
        (f32(tall + 1, SUB, wide), f32(tall, SUB, wide), f32(tall, SUB, wide), f32(tall, SUB, wide)), extended,
        scratch=[pltpu.VMEM((-(-tall // SUB) * SUB + SUB, wide), jnp.float32), pltpu.VMEM((4, -(-tall // SUB) * SUB, wide), jnp.float32)],
        name="weights",
    )
    own, other = [], []
    for begin, count in parts:
        part = call(
            functools.partial(sweep_kernel, begin=begin), f32(rows, count, cols), (*extended, *weights), name="sweeps"
        )
        own.append(part)
        for shift in range(1, groups):
            pairs = [(i, (i + shift) % groups) for i in range(groups)]
            other.append(lax.ppermute(part, "tm", pairs))
    mixed = call(make_mix(True), f32(rows, steps, cols), (own_corr, *own), name="mix_own")
    for corr, part in zip(corrs[:-1], other[:-1]):
        mixed = call(make_mix(False), f32(rows, steps, cols), (mixed, corr, part), name="mix_more")
    devices = height * breadth * groups
    mixed, message = call(
        last_mix_kernel, (f32(steps, rows, cols), f32(devices, 1, LANE)),
        (mixed, corrs[-1], other[-1], gram, pair_steps, pair_grads),
        scratch=[turn, pltpu.VMEM((NROW, LANE), jnp.float32)], name="mix_last",
    )
    inbox = lax.all_to_all(message, ("lat", "lon", "tm"), split_axis=0, concat_axis=0, tiled=True)
    return call(
        final_kernel, f32(steps, rows, cols), (inbox, mixed, control, pair_steps, pair_grads),
        scratch=[pltpu.VMEM((NROW, LANE), jnp.float32)], name="final",
    )


def solution(mesh):
    placed = (
        P("tm", "lat", "lon"),
        P("tm", "lat", "lon"),
        P("lat", "lon"),
        P("lat", "lon"),
        P(),
        P(None, "tm", "lat", "lon"),
        P(None, "tm", "lat", "lon"),
    )
    return jax.shard_map(
        local, mesh=mesh, in_specs=placed, out_specs=P("tm", "lat", "lon"), check_vma=False
    )
```

```python
import functools
import jax
import jax.numpy as jnp
from jax import lax
from jax.experimental import pallas as pl
from jax.experimental.pallas import tpu as pltpu
from jax.sharding import PartitionSpec as P

PAIRS = 8
SWEEPS = 6
SUB = 8
LANE = 128
HALO = SWEEPS
GROUP = 8
PER = LANE // GROUP
CROSS = [(i, j) for i in range(PAIRS) for j in range(i, PAIRS)]
NSYM = len(CROSS)
WHERE = {pair: k for k, pair in enumerate(CROSS)}
NGRAM = 2 * NSYM
NPROJ = 2 * PAIRS
NROW = NGRAM + NPROJ

VMEM = pl.BlockSpec(memory_space=pltpu.VMEM)
HBM = pl.BlockSpec(memory_space=pltpu.HBM)
PARAMS = pltpu.CompilerParams(vmem_limit_bytes=12 * 1024 * 1024)


def f32(*shape):
    return jax.ShapeDtypeStruct(shape, jnp.float32)


def call(kernel, outs, args, specs=None, scratch=(), outs_at=VMEM, name=None):
    single = not isinstance(outs, (tuple, list))
    return pl.pallas_call(
        kernel,
        out_shape=outs,
        in_specs=specs or [VMEM] * len(args),
        out_specs=outs_at if single else [outs_at] * len(outs),
        scratch_shapes=list(scratch),
        compiler_params=PARAMS,
        name=name,
    )(*args)


def lane_index():
    return lax.broadcasted_iota(jnp.int32, (SUB, LANE), 1)


def row_index():
    return lax.broadcasted_iota(jnp.int32, (SUB, LANE), 0)


def gram_kernel(steps_hbm, grads_hbm, out_ref, steps_ref, grads_ref, sems):
    _, steps, rows, cols = steps_ref.shape
    pieces = 4
    while steps % pieces:
        pieces -= 1
    count = steps // pieces
    copies = []
    for n in range(pieces):
        part = (slice(None), pl.ds(n * count, count))
        copies.append((
            pltpu.make_async_copy(steps_hbm.at[part], steps_ref.at[part], sems.at[0, n]),
            pltpu.make_async_copy(grads_hbm.at[part], grads_ref.at[part], sems.at[1, n]),
        ))
    for pair in copies:
        for copy in pair:
            copy.start()

    def make_body(half):
        def body(step, sums):
            sums = list(sums)
            for c in range(0, cols, LANE):
                for r in range(0, rows, 2 * SUB):
                    where = (step, pl.ds(r, 2 * SUB), pl.ds(c, LANE))
                    right = [grads_ref[(i, *where)].astype(jnp.float32) for i in range(PAIRS)]
                    left = right if half else [steps_ref[(i, *where)].astype(jnp.float32) for i in range(PAIRS)]
                    for part in range(2):
                        cut = slice(part * SUB, (part + 1) * SUB)
                        for k, (i, j) in enumerate(CROSS):
                            sums[k] = sums[k] + left[i][cut] * right[j][cut]
            return tuple(sums)

        return body

    zero = jnp.zeros((SUB, LANE), jnp.float32)
    sums = (zero,) * NSYM
    for n in range(pieces):
        for copy in copies[n]:
            copy.wait()
        sums = lax.fori_loop(n * count, (n + 1) * count, make_body(0), sums)
    for k in range(NSYM):
        out_ref[k:k + 1, :] = jnp.sum(sums[k], axis=0, keepdims=True)
    sums = lax.fori_loop(0, steps, make_body(1), (zero,) * NSYM)
    for k in range(NSYM):
        out_ref[NSYM + k:NSYM + k + 1, :] = jnp.sum(sums[k], axis=0, keepdims=True)


def groups_of(steps):
    return [(begin, min(SUB, steps - begin)) for begin in range(0, steps, SUB)]


def slots_of(steps):
    return -(-(steps + 1) // SUB) * SUB


def pack_kernel(grad_hbm, mask_hbm, diff_hbm, field_ref, swap_ref, next_ref, grad_ref, mask_ref, diff_ref, turn_ref, sems):
    steps, rows, cols = grad_ref.shape
    slots = field_ref.shape[1]
    pieces = [(begin, min(SUB, steps - begin)) for begin in range(0, steps, SUB)]
    copies = [pltpu.make_async_copy(mask_hbm, mask_ref, sems.at[0]), pltpu.make_async_copy(diff_hbm, diff_ref, sems.at[1])]
    for n, (begin, count) in enumerate(pieces):
        part = pl.ds(begin, count)
        copies.append(pltpu.make_async_copy(grad_hbm.at[part], grad_ref.at[part], sems.at[2 + n]))
    for copy in copies:
        copy.start()
    copies[0].wait()
    copies[1].wait()
    zero = jnp.zeros((SUB, LANE), jnp.float32)
    tiles = [
        (slice(r * SUB, (r + 1) * SUB), slice(c * LANE, (c + 1) * LANE), (c * (rows // SUB) + r) * slots * SUB)
        for c in range(cols // LANE) for r in range(rows // SUB)
    ]
    mask = [mask_ref[down, across].astype(jnp.float32) for down, across, _ in tiles]
    for slot in range(steps, slots):
        for down, across, base in tiles:
            value = diff_ref[down, across] if slot == steps else zero
            turn_ref[base + slot * SUB:base + (slot + 1) * SUB, :] = value
    for n, (begin, count) in enumerate(pieces):
        copies[2 + n].wait()
        for slot in range(begin, begin + count):
            for (down, across, base), keep in zip(tiles, mask):
                turn_ref[base + slot * SUB:base + (slot + 1) * SUB, :] = grad_ref[slot, down, across] * keep
    for c in range(cols // LANE):
        across = slice(c * LANE, (c + 1) * LANE)
        for row in range(rows):
            base = (c * (rows // SUB) + row // SUB) * slots * SUB + row % SUB
            for slot in range(0, slots, SUB):
                value = turn_ref[pl.ds(base + slot * SUB, SUB, stride=SUB), :]
                field_ref[row, slot:slot + SUB, across] = value
    odd = lax.rem(lax.axis_index("lat"), 2)
    near, far = (1 - odd) * (rows - HALO), odd * (rows - HALO)
    for row in range(HALO):
        swap_ref[row] = field_ref[near + row]
        next_ref[row] = field_ref[far + row]


def side_kernel(swap_ref, field_ref, next_ref, order_ref, whole_ref, west_ref, east_ref):
    rows, slots, cols = field_ref.shape
    odd = lax.rem(lax.axis_index("lat"), 2)
    near, far = (1 - odd) * (HALO + rows), odd * (HALO + rows)
    for row in range(HALO):
        whole_ref[near + row] = swap_ref[row]
        whole_ref[far + row] = next_ref[row]
    for row in range(rows):
        whole_ref[HALO + row] = field_ref[row]
    lane = lane_index()
    for slot in range(0, slots, SUB):
        down = slice(slot, slot + SUB)
        for base in range(0, rows + 2 * HALO, PER):
            west = east = jnp.zeros((SUB, LANE), jnp.float32)
            for row in range(base, min(base + PER, rows + 2 * HALO)):
                begin = (row - base) * GROUP
                here = (lane >= begin) & (lane < begin + GROUP)
                left = whole_ref[row, down, 0:LANE]
                right = whole_ref[row, down, cols - LANE:cols]
                west = jnp.where(here, pltpu.roll(left, begin, 1) if begin else left, west)
                turn = (begin + GROUP) % LANE
                east = jnp.where(here, pltpu.roll(right, turn, 1) if turn else right, east)
            place = slice(base // PER * LANE, (base // PER + 1) * LANE)
            west_ref[down, place] = west
            east_ref[down, place] = east


def make_row_loader(whole_ref, left_ref, right_ref):
    cols = whole_ref.shape[2]
    lane = lax.broadcasted_iota(jnp.int32, (1, LANE), 1)

    def load(row, down):
        place = slice(row // PER * LANE, (row // PER + 1) * LANE)
        begin = row % PER * GROUP
        tiles = [whole_ref[row, down, c * LANE:(c + 1) * LANE] for c in range(cols // LANE)]
        east, west = right_ref[down, place], left_ref[down, place]
        east = pltpu.roll(east, LANE - begin, 1) if begin else east
        turn = (2 * LANE - GROUP - begin) % LANE
        west = pltpu.roll(west, turn, 1) if turn else west
        return tiles + [jnp.where(lane < LANE // 2, east, west)]

    return load


def from_east(tiles, at_end):
    turned = [pltpu.roll(tile, LANE - 1, 1) for tile in tiles]
    return [jnp.where(at_end, turned[(c + 1) % len(tiles)], turned[c]) for c in range(len(tiles))]


def from_west(tiles, at_start):
    turned = [pltpu.roll(tile, 1, 1) for tile in tiles]
    return [jnp.where(at_start, turned[c - 1], turned[c]) for c in range(len(tiles))]


def weight_kernel(
    whole_ref, left_ref, right_ref, south_ref, east_ref, west_ref, keep_ref, kappa_ref, packed_ref, *, steps
):
    height, _, cols = whole_ref.shape
    width = cols // LANE + 1
    load = make_row_loader(whole_ref, left_ref, right_ref)
    lane = lane_index()
    at_start, at_end = lane == 0, lane == LANE - 1
    for row in range(height):
        for c, tile in enumerate(load(row, slice(steps, steps + 1))):
            kappa_ref[row:row + 1, c * LANE:(c + 1) * LANE] = tile
    for first in range(0, height, SUB):
        down = slice(first, first + SUB)
        kappa = [kappa_ref[down, c * LANE:(c + 1) * LANE] for c in range(width)]
        below = [kappa_ref[first + 1:first + 1 + SUB, c * LANE:(c + 1) * LANE] for c in range(width)]
        beside = from_east(kappa, at_end)
        east = [0.5 * (kappa[c] + beside[c]) for c in range(width)]
        west = from_west(east, at_start)
        for c in range(width):
            across = slice(c * LANE, (c + 1) * LANE)
            packed_ref[0, down, across] = 0.5 * (kappa[c] + below[c])
            packed_ref[1, down, across] = east[c]
            packed_ref[2, down, across] = west[c]
            packed_ref[3, down, across] = 1.0 - east[c] - west[c]
    for n, ref in enumerate((south_ref, east_ref, west_ref, keep_ref)):
        for row in range(height - 1):
            ref[row] = jnp.broadcast_to(packed_ref[n, row:row + 1, :], ref.shape[1:])
    for side, row in enumerate((HALO - 1, height - HALO)):
        inside = jnp.where(kappa_ref[row:row + 1, :] > 0.0, 1.0, 0.0)
        south_ref[height - 1 + side] = jnp.broadcast_to(inside, south_ref.shape[1:])


def sweep_kernel(whole_ref, left_ref, right_ref, south_ref, east_ref, west_ref, keep_ref, out_ref, *, begin):
    height, _, cols = whole_ref.shape
    rows, width = height - 2 * HALO, cols // LANE + 1
    count = out_ref.shape[1]
    lane = lane_index()
    at_start, at_end = lane == 0, lane == LANE - 1
    load = make_row_loader(whole_ref, left_ref, right_ref)
    state = [None] * SWEEPS

    def at(ref, row, c):
        return ref[row, :, c * LANE:(c + 1) * LANE]

    def advance(sweep, row, tiles):
        before = state[sweep]
        if before is None:
            state[sweep] = (tiles, None)
            return None
        centre, north = before
        south = [at(south_ref, row - 1, c) * (tiles[c] - centre[c]) for c in range(width)]
        state[sweep] = (tiles, south)
        if north is None:
            return None
        ahead, behind = from_east(centre, at_end), from_west(centre, at_start)
        fresh = []
        for c in range(width):
            change = south[c] - north[c]
            if row - 1 < HALO:
                change = change * at(south_ref, height - 1, c)
            if row - 1 >= HALO + rows:
                change = change * at(south_ref, height, c)
            across = at(east_ref, row - 1, c) * ahead[c] + at(west_ref, row - 1, c) * behind[c]
            fresh.append(at(keep_ref, row - 1, c) * centre[c] + across + change)
        return fresh

    waiting = [None] * (SWEEPS + 1)
    for tick in range(height + SWEEPS + 1):
        if waiting[SWEEPS] is not None:
            row, tiles = waiting[SWEEPS]
            for c in range(width - 1):
                out_ref[row - HALO, :, c * LANE:(c + 1) * LANE] = tiles[c][:count]
        for sweep in reversed(range(SWEEPS)):
            if sweep == 0:
                entry = (tick, load(tick, slice(begin, begin + SUB))) if tick < height else None
            else:
                entry = waiting[sweep]
            waiting[sweep + 1] = None
            if entry is not None:
                fresh = advance(sweep, *entry)
                if fresh is not None:
                    waiting[sweep + 1] = (entry[0] - 1, fresh)


def split_stack(value):
    high = value.astype(jnp.bfloat16).astype(jnp.float32)
    rest = value - high
    middle = rest.astype(jnp.bfloat16).astype(jnp.float32)
    low = rest - middle
    return jnp.concatenate([high, middle, high, low, middle, high], axis=0).astype(jnp.bfloat16)


def corr_kernel(corr_ref, *out_refs, groups, steps, sources):
    mine = lax.axis_index("tm")
    for at in range(groups):
        @pl.when(mine == at)
        def _(at=at):
            for (shift, begin, count), out_ref in zip(sources, out_refs):
                source = (at - shift) % groups * steps + begin
                block = corr_ref[source:source + count, at * steps:(at + 1) * steps]
                high = block.astype(jnp.bfloat16).astype(jnp.float32)
                rest = block - high
                middle = rest.astype(jnp.bfloat16).astype(jnp.float32)
                low = rest - middle
                depth = out_ref.shape[1] // 6
                pad = [jnp.zeros((depth - count, steps), jnp.float32)] if depth > count else []
                stack = []
                for part in (high, high, middle, high, middle, low):
                    stack += [part, *pad]
                out_ref[...] = jnp.concatenate(stack, axis=0).T.astype(jnp.bfloat16)


def mixed_row(row, corr_ref, field_refs):
    parts = []
    for ref in field_refs:
        part = ref[row]
        parts.append(part)
        if -part.shape[0] % SUB:
            parts.append(jnp.zeros((-part.shape[0] % SUB, part.shape[1]), jnp.float32))
    stacked = split_stack(jnp.concatenate(parts, axis=0) if len(parts) > 1 else parts[0])
    return jnp.dot(corr_ref[...], stacked, preferred_element_type=jnp.float32)


def make_mix(first):
    def kernel(*refs):
        *refs, out_ref = refs
        if first:
            corr_ref, *field_refs = refs
        else:
            acc_ref, corr_ref, *field_refs = refs
        for row in range(out_ref.shape[0]):
            total = mixed_row(row, corr_ref, field_refs)
            out_ref[row] = total if first else acc_ref[row] + total

    return kernel


def last_mix_kernel(acc_ref, corr_ref, field_ref, gram_ref, steps_ref, grads_ref, out_ref, message_ref, turn_ref, rows_ref):
    _, steps, rows, cols = steps_ref.shape
    slots = turn_ref.shape[0] // (rows * (cols // LANE))
    for row in range(rows):
        total = acc_ref[row] + mixed_row(row, corr_ref, [field_ref])
        for c in range(cols // LANE):
            base = (c * (rows // SUB) + row // SUB) * slots * SUB + row % SUB
            for begin, count in groups_of(steps):
                turn_ref[pl.ds(base + begin * SUB, count, stride=SUB), :] = total[begin:begin + count, c * LANE:(c + 1) * LANE]

    zero = jnp.zeros((SUB, LANE), jnp.float32)

    def body(step, sums):
        sums = list(sums)
        for c in range(cols // LANE):
            for r in range(0, rows, 2 * SUB):
                where = (step, pl.ds(r, 2 * SUB), pl.ds(c * LANE, LANE))
                halves = []
                for part in range(2):
                    base = (c * (rows // SUB) + r // SUB + part) * slots * SUB
                    halves.append(turn_ref[pl.ds(pl.multiple_of(base + step * SUB, SUB), SUB), :])
                mixed = jnp.concatenate(halves, axis=0)
                out_ref[where] = mixed
                half = mixed.astype(jnp.bfloat16).astype(jnp.float32)
                for n in range(NPROJ):
                    source = steps_ref if n < PAIRS else grads_ref
                    product = source[(n % PAIRS, *where)].astype(jnp.float32) * half
                    sums[n] = sums[n] + (product[:SUB] + product[SUB:])
        return tuple(sums)

    sums = lax.fori_loop(0, steps, body, (zero,) * NPROJ, unroll=2)
    rows_ref[0:NGRAM, :] = gram_ref[...]
    for n in range(NPROJ):
        rows_ref[NGRAM + n:NGRAM + n + 1, :] = jnp.sum(sums[n], axis=0, keepdims=True)
    lane, row = lane_index(), row_index()
    total = zero
    for first in range(0, NROW, SUB):
        summed = jnp.sum(rows_ref[first:first + SUB, :], axis=1, keepdims=True)
        total = total + jnp.where(lane == row + first, summed, 0.0)
    message = jnp.sum(total, axis=0, keepdims=True)
    message_ref[...] = jnp.broadcast_to(message[None], message_ref.shape)


def final_kernel(inbox_ref, mixed_ref, control_ref, steps_ref, grads_ref, out_hbm, out_ref, rows_ref, sems):
    totals = jnp.sum(inbox_ref[...], axis=0)
    lane, row = lane_index(), row_index()
    spread = jnp.broadcast_to(totals, (SUB, LANE))
    for first in range(0, NROW, SUB):
        picked = jnp.where(lane == row + first, spread, 0.0)
        rows_ref[first:first + SUB, :] = jnp.broadcast_to(jnp.sum(picked, axis=1, keepdims=True), (SUB, LANE))

    def entry(k):
        return jnp.broadcast_to(rows_ref[k:k + 1, :], (SUB, LANE))

    cross = {pair: entry(k) for pair, k in WHERE.items()}

    def square(i, j):
        return entry(NSYM + WHERE[(min(i, j), max(i, j))])

    gamma = cross[(PAIRS - 1, PAIRS - 1)] / square(PAIRS - 1, PAIRS - 1)
    pivot = [1.0 / cross[(i, i)] for i in range(PAIRS)]
    first = [None] * PAIRS
    for i in reversed(range(PAIRS)):
        rest = entry(NGRAM + i)
        for j in reversed(range(i + 1, PAIRS)):
            rest = rest - cross[(i, j)] * first[j]
        first[i] = rest * pivot[i]
    second = [None] * PAIRS
    for i in range(PAIRS):
        inner = -entry(NGRAM + PAIRS + i)
        for j in range(PAIRS):
            inner = inner + square(i, j) * first[j]
        rest = cross[(i, i)] * first[i] + gamma * inner
        for j in range(i):
            rest = rest - cross[(j, i)] * second[j]
        second[i] = rest * pivot[i]
    scaled = [gamma * value for value in first]

    _, steps, rows, cols = steps_ref.shape

    def body(step, carry):
        for c in range(0, cols, LANE):
            for r in range(0, rows, 2 * SUB):
                where = (step, pl.ds(r, 2 * SUB), pl.ds(c, LANE))
                mixed = mixed_ref[where]
                control = control_ref[where]
                update = [gamma * mixed[:SUB], gamma * mixed[SUB:]]
                for i in range(PAIRS):
                    s = steps_ref[(i, *where)].astype(jnp.float32)
                    y = grads_ref[(i, *where)].astype(jnp.float32)
                    for part, cut in enumerate((slice(0, SUB), slice(SUB, 2 * SUB))):
                        update[part] = update[part] + (second[i] * s[cut] - scaled[i] * y[cut])
                out_ref[step, pl.ds(r, SUB), pl.ds(c, LANE)] = control[:SUB] - update[0]
                out_ref[step, pl.ds(r + SUB, SUB), pl.ds(c, LANE)] = control[SUB:] - update[1]
        return carry

    copies = []
    for n, (begin, count) in enumerate(groups_of(steps)):
        lax.fori_loop(begin, begin + count, body, 0, unroll=2)
        part = pl.ds(begin, count)
        copies.append(pltpu.make_async_copy(out_ref.at[part], out_hbm.at[part], sems.at[n]))
        copies[-1].start()
    for copy in copies:
        copy.wait()


def local(gradient, control, diffusivity, land_mask, time_corr, pair_steps, pair_grads):
    steps, rows, cols = gradient.shape
    height, breadth, groups = (lax.axis_size(axis) for axis in ("lat", "lon", "tm"))
    even = [(i, j) for k in range(0, height - 1, 2) for i, j in ((k, k + 1), (k + 1, k))]
    odd = [(i, j) for k in range(1, height - 1, 2) for i, j in ((k, k + 1), (k + 1, k))]
    right = [(i, (i + 1) % breadth) for i in range(breadth)]
    left = [(j, i) for i, j in right]
    slots = slots_of(steps)
    turn = pltpu.VMEM((rows * (cols // LANE) * slots, LANE), jnp.float32)

    field, to_swap, to_next = call(
        pack_kernel,
        (f32(rows, slots, cols), f32(HALO, slots, cols), f32(HALO, slots, cols)),
        [pltpu.with_memory_space_constraint(v, pltpu.HBM) for v in (gradient, land_mask, diffusivity)],
        specs=[HBM] * 3,
        scratch=[
            pltpu.VMEM((steps, rows, cols), jnp.float32), pltpu.VMEM((rows, cols), jnp.int32),
            pltpu.VMEM((rows, cols), jnp.float32), turn, pltpu.SemaphoreType.DMA((2 + len(groups_of(steps)),)),
        ],
        name="pack",
    )
    from_swap = lax.ppermute(to_swap, "lat", even)
    from_next = lax.ppermute(to_next, "lat", odd)
    pair_shape = jax.ShapeDtypeStruct(pair_steps.shape, jnp.bfloat16)
    gram, pair_steps, pair_grads = call(
        gram_kernel, (f32(NGRAM, LANE), pair_shape, pair_shape),
        [pltpu.with_memory_space_constraint(v, pltpu.HBM) for v in (pair_steps, pair_grads)], specs=[HBM] * 2,
        scratch=[pltpu.SemaphoreType.DMA((2, 4))],
        name="gram",
    )
    tall, wide = rows + 2 * HALO, cols + LANE
    parts = groups_of(steps)
    sources = [(0, 0, steps)] + [(shift, *part) for part in parts for shift in range(1, groups)]
    own_corr, *corrs = call(
        functools.partial(corr_kernel, groups=groups, steps=steps, sources=sources),
        [jax.ShapeDtypeStruct((steps, 6 * (count + -count % SUB)), jnp.bfloat16) for _, _, count in sources],
        (time_corr,), name="corr",
    )
    side_shape = f32(slots, -(-tall // PER) * LANE)
    whole, west, east = call(
        side_kernel, (f32(tall, slots, cols), side_shape, side_shape), (from_swap, field, from_next, gram), name="sides"
    )
    from_left = lax.ppermute(east, "lon", right)
    from_right = lax.ppermute(west, "lon", left)
    extended = (whole, from_left, from_right)
    weights = call(
        functools.partial(weight_kernel, steps=steps),
        (f32(tall + 1, SUB, wide), f32(tall, SUB, wide), f32(tall, SUB, wide), f32(tall, SUB, wide)), extended,
        scratch=[pltpu.VMEM((-(-tall // SUB) * SUB + SUB, wide), jnp.float32), pltpu.VMEM((4, -(-tall // SUB) * SUB, wide), jnp.float32)],
        name="weights",
    )
    own, other = [], []
    for begin, count in parts:
        part = call(
            functools.partial(sweep_kernel, begin=begin), f32(rows, count, cols), (*extended, *weights), name="sweeps"
        )
        own.append(part)
        for shift in range(1, groups):
            pairs = [(i, (i + shift) % groups) for i in range(groups)]
            other.append(lax.ppermute(part, "tm", pairs))
    mixed = call(make_mix(True), f32(rows, steps, cols), (own_corr, *own), name="mix_own")
    for corr, part in zip(corrs[:-1], other[:-1]):
        mixed = call(make_mix(False), f32(rows, steps, cols), (mixed, corr, part), name="mix_more")
    devices = height * breadth * groups
    mixed, message = call(
        last_mix_kernel, (f32(steps, rows, cols), f32(devices, 1, LANE)),
        (mixed, corrs[-1], other[-1], gram, pair_steps, pair_grads),
        scratch=[turn, pltpu.VMEM((NROW, LANE), jnp.float32)], name="mix_last",
    )
    inbox = lax.all_to_all(
        message, ("lat", "lon", "tm"), split_axis=0, concat_axis=0, tiled=True,
        axis_index_groups=[list(reversed(range(devices)))],
    )
    return call(
        final_kernel, pltpu.HBM((steps, rows, cols), jnp.float32), (inbox, mixed, control, pair_steps, pair_grads),
        scratch=[
            pltpu.VMEM((steps, rows, cols), jnp.float32), pltpu.VMEM((NROW, LANE), jnp.float32),
            pltpu.SemaphoreType.DMA((len(parts),)),
        ],
        outs_at=HBM, name="final",
    )


def solution(mesh):
    placed = (
        P("tm", "lat", "lon"),
        P("tm", "lat", "lon"),
        P("lat", "lon"),
        P("lat", "lon"),
        P(),
        P(None, "tm", "lat", "lon"),
        P(None, "tm", "lat", "lon"),
    )
    return jax.shard_map(
        local, mesh=mesh, in_specs=placed, out_specs=P("tm", "lat", "lon"), check_vma=False
    )
```

```python
import functools
import jax
import jax.numpy as jnp
from jax import lax
from jax.experimental import pallas as pl
from jax.experimental.pallas import tpu as pltpu
from jax.sharding import PartitionSpec as P

PAIRS = 8
SWEEPS = 6
SUB = 8
LANE = 128
HALO = SWEEPS
GROUP = 8
PER = LANE // GROUP
CROSS = [(i, j) for i in range(PAIRS) for j in range(i, PAIRS)]
NSYM = len(CROSS)
WHERE = {pair: k for k, pair in enumerate(CROSS)}
NGRAM = 2 * NSYM
NPROJ = 2 * PAIRS
NROW = NGRAM + NPROJ

VMEM = pl.BlockSpec(memory_space=pltpu.VMEM)
HBM = pl.BlockSpec(memory_space=pltpu.HBM)
PARAMS = pltpu.CompilerParams(vmem_limit_bytes=12 * 1024 * 1024)


def f32(*shape):
    return jax.ShapeDtypeStruct(shape, jnp.float32)


def call(kernel, outs, args, specs=None, scratch=(), outs_at=VMEM, name=None):
    single = not isinstance(outs, (tuple, list))
    return pl.pallas_call(
        kernel,
        out_shape=outs,
        in_specs=specs or [VMEM] * len(args),
        out_specs=outs_at if single else [outs_at] * len(outs),
        scratch_shapes=list(scratch),
        compiler_params=PARAMS,
        name=name,
    )(*args)


def lane_index():
    return lax.broadcasted_iota(jnp.int32, (SUB, LANE), 1)


def row_index():
    return lax.broadcasted_iota(jnp.int32, (SUB, LANE), 0)


def gram_kernel(steps_ref, grads_ref, order_ref, out_ref):
    _, steps, rows, cols = steps_ref.shape

    def make_body(half):
        def body(step, sums):
            sums = list(sums)
            for c in range(0, cols, LANE):
                for r in range(0, rows, 2 * SUB):
                    where = (step, pl.ds(r, 2 * SUB), pl.ds(c, LANE))
                    right = [grads_ref[(i, *where)].astype(jnp.float32) for i in range(PAIRS)]
                    left = right if half else [steps_ref[(i, *where)].astype(jnp.float32) for i in range(PAIRS)]
                    for part in range(2):
                        cut = slice(part * SUB, (part + 1) * SUB)
                        for k, (i, j) in enumerate(CROSS):
                            sums[k] = sums[k] + left[i][cut] * right[j][cut]
            return tuple(sums)

        return body

    zero = jnp.zeros((SUB, LANE), jnp.float32)
    for half in range(2):
        sums = lax.fori_loop(0, steps, make_body(half), (zero,) * NSYM)
        for k in range(NSYM):
            out_ref[half * NSYM + k:half * NSYM + k + 1, :] = jnp.sum(sums[k], axis=0, keepdims=True)


def groups_of(steps):
    return [(begin, min(SUB, steps - begin)) for begin in range(0, steps, SUB)]


def slots_of(steps):
    return -(-(steps + 1) // SUB) * SUB


def halves_of(steps):
    tiles = slots_of(steps) // SUB
    order = [tiles - 1, *range(tiles - 1)]
    middle = (tiles + 1) // 2
    return [half for half in (order[:middle], order[middle:]) if half]


def pack_kernel(grad_hbm, mask_hbm, diff_hbm, field_ref, *refs):
    *message_refs, grad_ref, mask_ref, diff_ref, turn_ref, sems = refs
    steps, rows, cols = grad_ref.shape
    slots = field_ref.shape[1]
    pieces = [(begin, min(SUB, steps - begin)) for begin in range(0, steps, SUB)]
    copies = [pltpu.make_async_copy(mask_hbm, mask_ref, sems.at[0]), pltpu.make_async_copy(diff_hbm, diff_ref, sems.at[1])]
    for n, (begin, count) in enumerate(pieces):
        part = pl.ds(begin, count)
        copies.append(pltpu.make_async_copy(grad_hbm.at[part], grad_ref.at[part], sems.at[2 + n]))
    for copy in copies:
        copy.start()
    copies[0].wait()
    copies[1].wait()
    zero = jnp.zeros((SUB, LANE), jnp.float32)
    tiles = [
        (slice(r * SUB, (r + 1) * SUB), slice(c * LANE, (c + 1) * LANE), (c * (rows // SUB) + r) * slots * SUB)
        for c in range(cols // LANE) for r in range(rows // SUB)
    ]
    mask = [mask_ref[down, across].astype(jnp.float32) for down, across, _ in tiles]
    for slot in range(steps, slots):
        for down, across, base in tiles:
            value = diff_ref[down, across] if slot == steps else zero
            turn_ref[base + slot * SUB:base + (slot + 1) * SUB, :] = value
    for n, (begin, count) in enumerate(pieces):
        copies[2 + n].wait()
        for slot in range(begin, begin + count):
            for (down, across, base), keep in zip(tiles, mask):
                turn_ref[base + slot * SUB:base + (slot + 1) * SUB, :] = grad_ref[slot, down, across] * keep
    for c in range(cols // LANE):
        across = slice(c * LANE, (c + 1) * LANE)
        for row in range(rows):
            base = (c * (rows // SUB) + row // SUB) * slots * SUB + row % SUB
            for slot in range(0, slots, SUB):
                value = turn_ref[pl.ds(base + slot * SUB, SUB, stride=SUB), :]
                field_ref[row, slot:slot + SUB, across] = value
    odd = lax.rem(lax.axis_index("lat"), 2)
    near, far = (1 - odd) * (rows - HALO), odd * (rows - HALO)
    for n, half in enumerate(halves_of(steps)):
        for k, tile in enumerate(half):
            there, here = slice(k * SUB, (k + 1) * SUB), slice(tile * SUB, (tile + 1) * SUB)
            for row in range(HALO):
                message_refs[2 * n][row, there] = field_ref[near + row, here]
                message_refs[2 * n + 1][row, there] = field_ref[far + row, here]


def side_kernel(swap_ref, field_ref, next_ref, whole_ref, west_ref, east_ref, *, half):
    rows, _, cols = field_ref.shape
    slots = whole_ref.shape[1]
    odd = lax.rem(lax.axis_index("lat"), 2)
    near, far = (1 - odd) * (HALO + rows), odd * (HALO + rows)
    for row in range(HALO):
        whole_ref[near + row] = swap_ref[row]
        whole_ref[far + row] = next_ref[row]
    for k, tile in enumerate(half):
        for row in range(rows):
            whole_ref[HALO + row, k * SUB:(k + 1) * SUB] = field_ref[row, tile * SUB:(tile + 1) * SUB]
    lane = lane_index()
    for slot in range(0, slots, SUB):
        down = slice(slot, slot + SUB)
        for base in range(0, rows + 2 * HALO, PER):
            west = east = jnp.zeros((SUB, LANE), jnp.float32)
            for row in range(base, min(base + PER, rows + 2 * HALO)):
                begin = (row - base) * GROUP
                here = (lane >= begin) & (lane < begin + GROUP)
                left = whole_ref[row, down, 0:LANE]
                right = whole_ref[row, down, cols - LANE:cols]
                west = jnp.where(here, pltpu.roll(left, begin, 1) if begin else left, west)
                turn = (begin + GROUP) % LANE
                east = jnp.where(here, pltpu.roll(right, turn, 1) if turn else right, east)
            place = slice(base // PER * LANE, (base // PER + 1) * LANE)
            west_ref[down, place] = west
            east_ref[down, place] = east


def make_row_loader(whole_ref, left_ref, right_ref):
    cols = whole_ref.shape[2]
    lane = lax.broadcasted_iota(jnp.int32, (1, LANE), 1)

    def load(row, down):
        place = slice(row // PER * LANE, (row // PER + 1) * LANE)
        begin = row % PER * GROUP
        tiles = [whole_ref[row, down, c * LANE:(c + 1) * LANE] for c in range(cols // LANE)]
        east, west = right_ref[down, place], left_ref[down, place]
        east = pltpu.roll(east, LANE - begin, 1) if begin else east
        turn = (2 * LANE - GROUP - begin) % LANE
        west = pltpu.roll(west, turn, 1) if turn else west
        return tiles + [jnp.where(lane < LANE // 2, east, west)]

    return load


def from_east(tiles, at_end):
    turned = [pltpu.roll(tile, LANE - 1, 1) for tile in tiles]
    return [jnp.where(at_end, turned[(c + 1) % len(tiles)], turned[c]) for c in range(len(tiles))]


def from_west(tiles, at_start):
    turned = [pltpu.roll(tile, 1, 1) for tile in tiles]
    return [jnp.where(at_start, turned[c - 1], turned[c]) for c in range(len(tiles))]


def weight_kernel(
    whole_ref, left_ref, right_ref, south_ref, east_ref, west_ref, keep_ref, kappa_ref, packed_ref, *, slot
):
    height, _, cols = whole_ref.shape
    width = cols // LANE + 1
    load = make_row_loader(whole_ref, left_ref, right_ref)
    lane = lane_index()
    at_start, at_end = lane == 0, lane == LANE - 1
    for row in range(height):
        for c, tile in enumerate(load(row, slice(slot, slot + 1))):
            kappa_ref[row:row + 1, c * LANE:(c + 1) * LANE] = tile
    for first in range(0, height, SUB):
        down = slice(first, first + SUB)
        kappa = [kappa_ref[down, c * LANE:(c + 1) * LANE] for c in range(width)]
        below = [kappa_ref[first + 1:first + 1 + SUB, c * LANE:(c + 1) * LANE] for c in range(width)]
        beside = from_east(kappa, at_end)
        east = [0.5 * (kappa[c] + beside[c]) for c in range(width)]
        west = from_west(east, at_start)
        for c in range(width):
            across = slice(c * LANE, (c + 1) * LANE)
            packed_ref[0, down, across] = 0.5 * (kappa[c] + below[c])
            packed_ref[1, down, across] = east[c]
            packed_ref[2, down, across] = west[c]
            packed_ref[3, down, across] = 1.0 - east[c] - west[c]
    for n, ref in enumerate((south_ref, east_ref, west_ref, keep_ref)):
        for row in range(height - 1):
            ref[row] = jnp.broadcast_to(packed_ref[n, row:row + 1, :], ref.shape[1:])
    for side, row in enumerate((HALO - 1, height - HALO)):
        inside = jnp.where(kappa_ref[row:row + 1, :] > 0.0, 1.0, 0.0)
        south_ref[height - 1 + side] = jnp.broadcast_to(inside, south_ref.shape[1:])


def sweep_kernel(whole_ref, left_ref, right_ref, south_ref, east_ref, west_ref, keep_ref, *refs, begin):
    copies = []
    _, *refs = refs
    if len(refs) > 1:
        source, out_ref, target, sem = refs
        copies.append(pltpu.make_async_copy(source, target, sem))
        copies[0].start()
    else:
        (out_ref,) = refs
    height, _, cols = whole_ref.shape
    rows, width = height - 2 * HALO, cols // LANE + 1
    count = out_ref.shape[1]
    lane = lane_index()
    at_start, at_end = lane == 0, lane == LANE - 1
    load = make_row_loader(whole_ref, left_ref, right_ref)
    state = [None] * SWEEPS

    def at(ref, row, c):
        return ref[row, :, c * LANE:(c + 1) * LANE]

    def advance(sweep, row, tiles):
        before = state[sweep]
        if before is None:
            state[sweep] = (tiles, None)
            return None
        centre, north = before
        south = [at(south_ref, row - 1, c) * (tiles[c] - centre[c]) for c in range(width)]
        state[sweep] = (tiles, south)
        if north is None:
            return None
        ahead, behind = from_east(centre, at_end), from_west(centre, at_start)
        fresh = []
        for c in range(width):
            change = south[c] - north[c]
            if row - 1 < HALO:
                change = change * at(south_ref, height - 1, c)
            if row - 1 >= HALO + rows:
                change = change * at(south_ref, height, c)
            across = at(east_ref, row - 1, c) * ahead[c] + at(west_ref, row - 1, c) * behind[c]
            fresh.append(at(keep_ref, row - 1, c) * centre[c] + across + change)
        return fresh

    waiting = [None] * (SWEEPS + 1)
    for tick in range(height + SWEEPS + 1):
        if waiting[SWEEPS] is not None:
            row, tiles = waiting[SWEEPS]
            for c in range(width - 1):
                out_ref[row - HALO, :, c * LANE:(c + 1) * LANE] = tiles[c][:count]
        for sweep in reversed(range(SWEEPS)):
            if sweep == 0:
                entry = (tick, load(tick, slice(begin, begin + SUB))) if tick < height else None
            else:
                entry = waiting[sweep]
            waiting[sweep + 1] = None
            if entry is not None:
                fresh = advance(sweep, *entry)
                if fresh is not None:
                    waiting[sweep + 1] = (entry[0] - 1, fresh)
    for copy in copies:
        copy.wait()


def split_stack(value):
    high = value.astype(jnp.bfloat16).astype(jnp.float32)
    rest = value - high
    middle = rest.astype(jnp.bfloat16).astype(jnp.float32)
    low = rest - middle
    return jnp.concatenate([high, middle, high, low, middle, high], axis=0).astype(jnp.bfloat16)


def corr_kernel(corr_ref, *out_refs, groups, steps, sources):
    mine = lax.axis_index("tm")
    for at in range(groups):
        @pl.when(mine == at)
        def _(at=at):
            for pieces, out_ref in zip(sources, out_refs):
                blocks = []
                for shift, begin, count in pieces:
                    source = (at - shift) % groups * steps + begin
                    blocks.append(corr_ref[source:source + count, at * steps:(at + 1) * steps])
                    if count % SUB:
                        blocks.append(jnp.zeros((-count % SUB, steps), jnp.float32))
                block = jnp.concatenate(blocks, axis=0) if len(blocks) > 1 else blocks[0]
                high = block.astype(jnp.bfloat16).astype(jnp.float32)
                rest = block - high
                middle = rest.astype(jnp.bfloat16).astype(jnp.float32)
                low = rest - middle
                stack = jnp.concatenate([high, high, middle, high, middle, low], axis=0)
                out_ref[...] = stack.T.astype(jnp.bfloat16)


def mixed_row(row, corr_ref, field_refs):
    parts = []
    for ref in field_refs:
        part = ref[row]
        parts.append(part)
        if -part.shape[0] % SUB:
            parts.append(jnp.zeros((-part.shape[0] % SUB, part.shape[1]), jnp.float32))
    stacked = split_stack(jnp.concatenate(parts, axis=0) if len(parts) > 1 else parts[0])
    return jnp.dot(corr_ref[...], stacked, preferred_element_type=jnp.float32)


def make_mix(first):
    def kernel(*refs):
        *refs, out_ref = refs
        if first:
            corr_ref, *field_refs = refs
        else:
            acc_ref, corr_ref, *field_refs = refs
        for row in range(out_ref.shape[0]):
            total = mixed_row(row, corr_ref, field_refs)
            out_ref[row] = total if first else acc_ref[row] + total

    return kernel


def last_mix_kernel(acc_ref, corr_ref, field_ref, gram_ref, steps_ref, grads_ref, out_ref, message_ref, turn_ref, rows_ref):
    _, steps, rows, cols = steps_ref.shape
    slots = turn_ref.shape[0] // (rows * (cols // LANE))
    for row in range(rows):
        total = acc_ref[row] + mixed_row(row, corr_ref, [field_ref])
        for c in range(cols // LANE):
            base = (c * (rows // SUB) + row // SUB) * slots * SUB + row % SUB
            for begin, count in groups_of(steps):
                turn_ref[pl.ds(base + begin * SUB, count, stride=SUB), :] = total[begin:begin + count, c * LANE:(c + 1) * LANE]

    zero = jnp.zeros((SUB, LANE), jnp.float32)

    def body(step, sums):
        sums = list(sums)
        for c in range(cols // LANE):
            for r in range(0, rows, 2 * SUB):
                where = (step, pl.ds(r, 2 * SUB), pl.ds(c * LANE, LANE))
                halves = []
                for part in range(2):
                    base = (c * (rows // SUB) + r // SUB + part) * slots * SUB
                    halves.append(turn_ref[pl.ds(pl.multiple_of(base + step * SUB, SUB), SUB), :])
                mixed = jnp.concatenate(halves, axis=0)
                out_ref[where] = mixed
                half = mixed.astype(jnp.bfloat16).astype(jnp.float32)
                for n in range(NPROJ):
                    source = steps_ref if n < PAIRS else grads_ref
                    product = source[(n % PAIRS, *where)].astype(jnp.float32) * half
                    sums[n] = sums[n] + (product[:SUB] + product[SUB:])
        return tuple(sums)

    sums = lax.fori_loop(0, steps, body, (zero,) * NPROJ, unroll=2)
    rows_ref[0:NGRAM, :] = gram_ref[...]
    for n in range(NPROJ):
        rows_ref[NGRAM + n:NGRAM + n + 1, :] = jnp.sum(sums[n], axis=0, keepdims=True)
    lane, row = lane_index(), row_index()
    total = zero
    for first in range(0, NROW, SUB):
        summed = jnp.sum(rows_ref[first:first + SUB, :], axis=1, keepdims=True)
        total = total + jnp.where(lane == row + first, summed, 0.0)
    message = jnp.sum(total, axis=0, keepdims=True)
    message_ref[...] = jnp.broadcast_to(message[None], message_ref.shape)


def final_kernel(inbox_ref, mixed_ref, control_ref, steps_ref, grads_ref, out_hbm, out_ref, rows_ref, sems):
    totals = jnp.sum(inbox_ref[...], axis=0)
    lane, row = lane_index(), row_index()
    spread = jnp.broadcast_to(totals, (SUB, LANE))
    for first in range(0, NROW, SUB):
        picked = jnp.where(lane == row + first, spread, 0.0)
        rows_ref[first:first + SUB, :] = jnp.broadcast_to(jnp.sum(picked, axis=1, keepdims=True), (SUB, LANE))

    def entry(k):
        return jnp.broadcast_to(rows_ref[k:k + 1, :], (SUB, LANE))

    cross = {pair: entry(k) for pair, k in WHERE.items()}

    def square(i, j):
        return entry(NSYM + WHERE[(min(i, j), max(i, j))])

    gamma = cross[(PAIRS - 1, PAIRS - 1)] / square(PAIRS - 1, PAIRS - 1)
    pivot = [1.0 / cross[(i, i)] for i in range(PAIRS)]
    first = [None] * PAIRS
    for i in reversed(range(PAIRS)):
        rest = entry(NGRAM + i)
        for j in reversed(range(i + 1, PAIRS)):
            rest = rest - cross[(i, j)] * first[j]
        first[i] = rest * pivot[i]
    second = [None] * PAIRS
    for i in range(PAIRS):
        inner = -entry(NGRAM + PAIRS + i)
        for j in range(PAIRS):
            inner = inner + square(i, j) * first[j]
        rest = cross[(i, i)] * first[i] + gamma * inner
        for j in range(i):
            rest = rest - cross[(j, i)] * second[j]
        second[i] = rest * pivot[i]
    scaled = [gamma * value for value in first]

    _, steps, rows, cols = steps_ref.shape

    def body(step, carry):
        for c in range(0, cols, LANE):
            for r in range(0, rows, 2 * SUB):
                where = (step, pl.ds(r, 2 * SUB), pl.ds(c, LANE))
                mixed = mixed_ref[where]
                control = control_ref[where]
                update = [gamma * mixed[:SUB], gamma * mixed[SUB:]]
                for i in range(PAIRS):
                    s = steps_ref[(i, *where)].astype(jnp.float32)
                    y = grads_ref[(i, *where)].astype(jnp.float32)
                    for part, cut in enumerate((slice(0, SUB), slice(SUB, 2 * SUB))):
                        update[part] = update[part] + (second[i] * s[cut] - scaled[i] * y[cut])
                out_ref[step, pl.ds(r, SUB), pl.ds(c, LANE)] = control[:SUB] - update[0]
                out_ref[step, pl.ds(r + SUB, SUB), pl.ds(c, LANE)] = control[SUB:] - update[1]
        return carry

    copies = []
    for n, (begin, count) in enumerate(groups_of(steps)):
        lax.fori_loop(begin, begin + count, body, 0, unroll=2)
        part = pl.ds(begin, count)
        copies.append(pltpu.make_async_copy(out_ref.at[part], out_hbm.at[part], sems.at[n]))
        copies[-1].start()
    for copy in copies:
        copy.wait()


def local(gradient, control, diffusivity, land_mask, time_corr, pair_steps, pair_grads):
    steps, rows, cols = gradient.shape
    height, breadth, groups = (lax.axis_size(axis) for axis in ("lat", "lon", "tm"))
    even = [(i, j) for k in range(0, height - 1, 2) for i, j in ((k, k + 1), (k + 1, k))]
    odd = [(i, j) for k in range(1, height - 1, 2) for i, j in ((k, k + 1), (k + 1, k))]
    right = [(i, (i + 1) % breadth) for i in range(breadth)]
    left = [(j, i) for i, j in right]
    slots = slots_of(steps)
    turn = pltpu.VMEM((rows * (cols // LANE) * slots, LANE), jnp.float32)

    halves = halves_of(steps)
    field, *messages = call(
        pack_kernel,
        [f32(rows, slots, cols)] + [f32(HALO, len(half) * SUB, cols) for half in halves for _ in range(2)],
        [pltpu.with_memory_space_constraint(v, pltpu.HBM) for v in (gradient, land_mask, diffusivity)],
        specs=[HBM] * 3,
        scratch=[
            pltpu.VMEM((steps, rows, cols), jnp.float32), pltpu.VMEM((rows, cols), jnp.int32),
            pltpu.VMEM((rows, cols), jnp.float32), turn, pltpu.SemaphoreType.DMA((2 + len(groups_of(steps)),)),
        ],
        name="pack",
    )
    arrived = []
    for n in range(len(halves)):
        from_next = lax.ppermute(messages[2 * n + 1], "lat", odd)
        arrived.append((lax.ppermute(messages[2 * n], "lat", even), from_next))
    tall, wide = rows + 2 * HALO, cols + LANE
    extended = []
    for half, (from_swap, from_next) in zip(halves, arrived):
        inner = len(half) * SUB
        side_shape = f32(inner, -(-tall // PER) * LANE)
        whole, west, east = call(
            functools.partial(side_kernel, half=half), (f32(tall, inner, cols), side_shape, side_shape),
            (from_swap, field, from_next), name="sides",
        )
        extended.append((whole, lax.ppermute(east, "lon", right), lax.ppermute(west, "lon", left)))
    weights = call(
        functools.partial(weight_kernel, slot=steps % SUB),
        (f32(tall + 1, SUB, wide), f32(tall, SUB, wide), f32(tall, SUB, wide), f32(tall, SUB, wide)), extended[0],
        scratch=[pltpu.VMEM((-(-tall // SUB) * SUB + SUB, wide), jnp.float32), pltpu.VMEM((4, -(-tall // SUB) * SUB, wide), jnp.float32)],
        name="weights",
    )
    work = [(n, k, tile * SUB, min(SUB, steps - tile * SUB)) for n, half in enumerate(halves) for k, tile in enumerate(half)]
    work = [item for item in work if item[3] > 0]
    work.sort(key=lambda item: (item[0], -item[3]))
    loads = [pltpu.with_memory_space_constraint(v, pltpu.HBM) for v in (pair_steps, pair_grads)]
    pairs_at = {max(len(work) - 3 + n, 0): load for n, load in enumerate(loads)}
    own, other, sources, pairs = [], [], [], []
    for at, (n, k, begin, count) in enumerate(work):
        kernel = functools.partial(sweep_kernel, begin=k * SUB)
        order = own[-1] if own else weights[0]
        if at in pairs_at:
            load = pairs_at[at]
            part, loaded = call(
                kernel, (f32(rows, count, cols), jax.ShapeDtypeStruct(load.shape, load.dtype)), (*extended[n], *weights, order, load),
                specs=[VMEM] * 8 + [HBM], scratch=[pltpu.SemaphoreType.DMA], name="sweeps",
            )
            pairs.append(loaded)
        else:
            part = call(kernel, f32(rows, count, cols), (*extended[n], *weights, order), name="sweeps")
        own.append(part)
        for shift in range(1, groups):
            sources.append([(shift, begin, count)])
            other.append(lax.ppermute(part, "tm", [(i, (i + shift) % groups) for i in range(groups)]))
    pair_steps, pair_grads = pairs if len(pairs) == 2 else (pair_steps, pair_grads)
    sources.append([(0, begin, count) for _, _, begin, count in work])
    *corrs, own_corr = call(
        functools.partial(corr_kernel, groups=groups, steps=steps, sources=sources),
        [jax.ShapeDtypeStruct((steps, 6 * SUB * len(pieces)), jnp.bfloat16) for pieces in sources],
        (time_corr,), name="corr",
    )
    gram = call(gram_kernel, f32(NGRAM, LANE), (pair_steps, pair_grads, own[-1]), name="gram")
    mixed = call(make_mix(True), f32(rows, steps, cols), (own_corr, *own), name="mix_own")
    for corr, part in zip(corrs[:-1], other[:-1]):
        mixed = call(make_mix(False), f32(rows, steps, cols), (mixed, corr, part), name="mix_more")
    devices = height * breadth * groups
    mixed, message = call(
        last_mix_kernel, (f32(steps, rows, cols), f32(devices, 1, LANE)),
        (mixed, corrs[-1], other[-1], gram, pair_steps, pair_grads),
        scratch=[turn, pltpu.VMEM((NROW, LANE), jnp.float32)], name="mix_last",
    )
    inbox = lax.all_to_all(
        message, ("lat", "lon", "tm"), split_axis=0, concat_axis=0, tiled=True,
        axis_index_groups=[list(reversed(range(devices)))],
    )
    return call(
        final_kernel, pltpu.HBM((steps, rows, cols), jnp.float32), (inbox, mixed, control, pair_steps, pair_grads),
        scratch=[
            pltpu.VMEM((steps, rows, cols), jnp.float32), pltpu.VMEM((NROW, LANE), jnp.float32),
            pltpu.SemaphoreType.DMA((len(groups_of(steps)),)),
        ],
        outs_at=HBM, name="final",
    )


def solution(mesh):
    placed = (
        P("tm", "lat", "lon"),
        P("tm", "lat", "lon"),
        P("lat", "lon"),
        P("lat", "lon"),
        P(),
        P(None, "tm", "lat", "lon"),
        P(None, "tm", "lat", "lon"),
    )
    return jax.shard_map(
        local, mesh=mesh, in_specs=placed, out_specs=P("tm", "lat", "lon"), check_vma=False
    )
```

```python
import functools
import jax
import jax.numpy as jnp
from jax import lax
from jax.experimental import pallas as pl
from jax.experimental.pallas import tpu as pltpu
from jax.sharding import PartitionSpec as P

PAIRS = 8
SWEEPS = 6
SUB = 8
LANE = 128
HALO = SWEEPS
GROUP = 8
PER = LANE // GROUP
CROSS = [(i, j) for i in range(PAIRS) for j in range(i, PAIRS)]
NSYM = len(CROSS)
WHERE = {pair: k for k, pair in enumerate(CROSS)}
NGRAM = 2 * NSYM
NPROJ = 2 * PAIRS
NROW = NGRAM + NPROJ

VMEM = pl.BlockSpec(memory_space=pltpu.VMEM)
HBM = pl.BlockSpec(memory_space=pltpu.HBM)
PARAMS = pltpu.CompilerParams(vmem_limit_bytes=12 * 1024 * 1024)


def f32(*shape):
    return jax.ShapeDtypeStruct(shape, jnp.float32)


def call(kernel, outs, args, specs=None, scratch=(), outs_at=VMEM, name=None):
    single = not isinstance(outs, (tuple, list))
    return pl.pallas_call(
        kernel,
        out_shape=outs,
        in_specs=specs or [VMEM] * len(args),
        out_specs=outs_at if single else [outs_at] * len(outs),
        scratch_shapes=list(scratch),
        compiler_params=PARAMS,
        name=name,
    )(*args)


def lane_index():
    return lax.broadcasted_iota(jnp.int32, (SUB, LANE), 1)


def row_index():
    return lax.broadcasted_iota(jnp.int32, (SUB, LANE), 0)


def gram_kernel(steps_hbm, grads_hbm, out_ref, steps_ref, grads_ref, sems):
    _, steps, rows, cols = steps_ref.shape
    pieces = 4
    while steps % pieces:
        pieces -= 1
    count = steps // pieces
    copies = []
    for n in range(pieces):
        part = (slice(None), pl.ds(n * count, count))
        copies.append((
            pltpu.make_async_copy(steps_hbm.at[part], steps_ref.at[part], sems.at[0, n]),
            pltpu.make_async_copy(grads_hbm.at[part], grads_ref.at[part], sems.at[1, n]),
        ))
    for pair in copies:
        for copy in pair:
            copy.start()

    def make_body(half):
        def body(step, sums):
            sums = list(sums)
            for c in range(0, cols, LANE):
                for r in range(0, rows, 2 * SUB):
                    where = (step, pl.ds(r, 2 * SUB), pl.ds(c, LANE))
                    right = [grads_ref[(i, *where)].astype(jnp.float32) for i in range(PAIRS)]
                    left = right if half else [steps_ref[(i, *where)].astype(jnp.float32) for i in range(PAIRS)]
                    for part in range(2):
                        cut = slice(part * SUB, (part + 1) * SUB)
                        for k, (i, j) in enumerate(CROSS):
                            sums[k] = sums[k] + left[i][cut] * right[j][cut]
            return tuple(sums)

        return body

    zero = jnp.zeros((SUB, LANE), jnp.float32)
    sums = (zero,) * NSYM
    for n in range(pieces):
        for copy in copies[n]:
            copy.wait()
        sums = lax.fori_loop(n * count, (n + 1) * count, make_body(0), sums)
    for k in range(NSYM):
        out_ref[k:k + 1, :] = jnp.sum(sums[k], axis=0, keepdims=True)
    sums = lax.fori_loop(0, steps, make_body(1), (zero,) * NSYM)
    for k in range(NSYM):
        out_ref[NSYM + k:NSYM + k + 1, :] = jnp.sum(sums[k], axis=0, keepdims=True)


def groups_of(steps):
    return [(begin, min(SUB, steps - begin)) for begin in range(0, steps, SUB)]


def slots_of(steps):
    return -(-(steps + 1) // SUB) * SUB


def pack_kernel(grad_hbm, mask_hbm, diff_hbm, field_ref, swap_ref, next_ref, grad_ref, mask_ref, diff_ref, turn_ref, sems):
    steps, rows, cols = grad_ref.shape
    slots = field_ref.shape[1]
    pieces = [(begin, min(SUB, steps - begin)) for begin in range(0, steps, SUB)]
    copies = [pltpu.make_async_copy(mask_hbm, mask_ref, sems.at[0]), pltpu.make_async_copy(diff_hbm, diff_ref, sems.at[1])]
    for n, (begin, count) in enumerate(pieces):
        part = pl.ds(begin, count)
        copies.append(pltpu.make_async_copy(grad_hbm.at[part], grad_ref.at[part], sems.at[2 + n]))
    for copy in copies:
        copy.start()
    copies[0].wait()
    copies[1].wait()
    zero = jnp.zeros((SUB, LANE), jnp.float32)
    tiles = [
        (slice(r * SUB, (r + 1) * SUB), slice(c * LANE, (c + 1) * LANE), (c * (rows // SUB) + r) * slots * SUB)
        for c in range(cols // LANE) for r in range(rows // SUB)
    ]
    mask = [mask_ref[down, across].astype(jnp.float32) for down, across, _ in tiles]
    for slot in range(steps, slots):
        for down, across, base in tiles:
            value = diff_ref[down, across] if slot == steps else zero
            turn_ref[base + slot * SUB:base + (slot + 1) * SUB, :] = value
    for n, (begin, count) in enumerate(pieces):
        copies[2 + n].wait()
        for slot in range(begin, begin + count):
            for (down, across, base), keep in zip(tiles, mask):
                turn_ref[base + slot * SUB:base + (slot + 1) * SUB, :] = grad_ref[slot, down, across] * keep
    for c in range(cols // LANE):
        across = slice(c * LANE, (c + 1) * LANE)
        for row in range(rows):
            base = (c * (rows // SUB) + row // SUB) * slots * SUB + row % SUB
            for slot in range(0, slots, SUB):
                value = turn_ref[pl.ds(base + slot * SUB, SUB, stride=SUB), :]
                field_ref[row, slot:slot + SUB, across] = value
    odd = lax.rem(lax.axis_index("lat"), 2)
    near, far = (1 - odd) * (rows - HALO), odd * (rows - HALO)
    for row in range(HALO):
        swap_ref[row] = field_ref[near + row]
        next_ref[row] = field_ref[far + row]


def side_kernel(swap_ref, field_ref, next_ref, order_ref, whole_ref, pair_ref, beside_ref):
    rows, slots, cols = field_ref.shape
    place, count = lax.axis_index("lat"), lax.axis_size("lat")
    odd = lax.rem(place, 2)
    near, far = (1 - odd) * (HALO + rows), odd * (HALO + rows)
    has_near = jnp.full((SUB, LANE), place + 1 - 2 * odd, jnp.int32) < count
    after = jnp.full((SUB, LANE), place - 1 + 2 * odd, jnp.int32)
    has_far = (after >= 0) & (after < count)
    for row in range(HALO):
        for slot in range(0, slots, SUB):
            for c in range(0, cols, LANE):
                where = (slice(slot, slot + SUB), slice(c, c + LANE))
                whole_ref[(near + row, *where)] = jnp.where(has_near, swap_ref[(row, *where)], 0.0)
                whole_ref[(far + row, *where)] = jnp.where(has_far, next_ref[(row, *where)], 0.0)
    for row in range(rows):
        whole_ref[HALO + row] = field_ref[row]
    lane = lane_index()
    uneven = jnp.full((SUB, LANE), lax.rem(lax.axis_index("lon"), 2), jnp.int32) == 1
    for slot in range(0, slots, SUB):
        down = slice(slot, slot + SUB)
        for base in range(0, rows + 2 * HALO, PER):
            west = east = jnp.zeros((SUB, LANE), jnp.float32)
            for row in range(base, min(base + PER, rows + 2 * HALO)):
                begin = (row - base) * GROUP
                here = (lane >= begin) & (lane < begin + GROUP)
                left = whole_ref[row, down, 0:LANE]
                right = whole_ref[row, down, cols - LANE:cols]
                west = jnp.where(here, pltpu.roll(left, begin, 1) if begin else left, west)
                turn = (begin + GROUP) % LANE
                east = jnp.where(here, pltpu.roll(right, turn, 1) if turn else right, east)
            across = slice(base // PER * LANE, (base // PER + 1) * LANE)
            pair_ref[down, across] = jnp.where(uneven, west, east)
            beside_ref[down, across] = jnp.where(uneven, east, west)


def make_row_loader(whole_ref, left_ref, right_ref):
    cols = whole_ref.shape[2]
    lane = lax.broadcasted_iota(jnp.int32, (1, LANE), 1)

    def load(row, down):
        place = slice(row // PER * LANE, (row // PER + 1) * LANE)
        begin = row % PER * GROUP
        tiles = [whole_ref[row, down, c * LANE:(c + 1) * LANE] for c in range(cols // LANE)]
        east, west = right_ref[down, place], left_ref[down, place]
        east = pltpu.roll(east, LANE - begin, 1) if begin else east
        turn = (2 * LANE - GROUP - begin) % LANE
        west = pltpu.roll(west, turn, 1) if turn else west
        return tiles + [jnp.where(lane < LANE // 2, east, west)]

    return load


def from_east(tiles, at_end):
    turned = [pltpu.roll(tile, LANE - 1, 1) for tile in tiles]
    return [jnp.where(at_end, turned[(c + 1) % len(tiles)], turned[c]) for c in range(len(tiles))]


def from_west(tiles, at_start):
    turned = [pltpu.roll(tile, 1, 1) for tile in tiles]
    return [jnp.where(at_start, turned[c - 1], turned[c]) for c in range(len(tiles))]


def weight_kernel(
    whole_ref, pair_ref, beside_ref, left_ref, right_ref, south_ref, east_ref, west_ref, keep_ref, kappa_ref, packed_ref, *, steps
):
    height, _, cols = whole_ref.shape
    uneven = jnp.full(pair_ref.shape, lax.rem(lax.axis_index("lon"), 2), jnp.int32) == 1
    left_ref[...] = jnp.where(uneven, pair_ref[...], beside_ref[...])
    right_ref[...] = jnp.where(uneven, beside_ref[...], pair_ref[...])
    width = cols // LANE + 1
    load = make_row_loader(whole_ref, left_ref, right_ref)
    lane = lane_index()
    at_start, at_end = lane == 0, lane == LANE - 1
    for row in range(height):
        for c, tile in enumerate(load(row, slice(steps, steps + 1))):
            kappa_ref[row:row + 1, c * LANE:(c + 1) * LANE] = tile
    for first in range(0, height, SUB):
        down = slice(first, first + SUB)
        kappa = [kappa_ref[down, c * LANE:(c + 1) * LANE] for c in range(width)]
        below = [kappa_ref[first + 1:first + 1 + SUB, c * LANE:(c + 1) * LANE] for c in range(width)]
        beside = from_east(kappa, at_end)
        east = [0.5 * (kappa[c] + beside[c]) for c in range(width)]
        west = from_west(east, at_start)
        for c in range(width):
            across = slice(c * LANE, (c + 1) * LANE)
            packed_ref[0, down, across] = 0.5 * (kappa[c] + below[c])
            packed_ref[1, down, across] = east[c]
            packed_ref[2, down, across] = west[c]
            packed_ref[3, down, across] = 1.0 - east[c] - west[c]
    for n, ref in enumerate((south_ref, east_ref, west_ref, keep_ref)):
        for row in range(height - 1):
            ref[row] = jnp.broadcast_to(packed_ref[n, row:row + 1, :], ref.shape[1:])
    for side, row in enumerate((HALO - 1, height - HALO)):
        inside = jnp.where(kappa_ref[row:row + 1, :] > 0.0, 1.0, 0.0)
        south_ref[height - 1 + side] = jnp.broadcast_to(inside, south_ref.shape[1:])


def sweep_kernel(whole_ref, left_ref, right_ref, south_ref, east_ref, west_ref, keep_ref, out_ref, *, begin):
    height, _, cols = whole_ref.shape
    rows, width = height - 2 * HALO, cols // LANE + 1
    count = out_ref.shape[1]
    lane = lane_index()
    at_start, at_end = lane == 0, lane == LANE - 1
    load = make_row_loader(whole_ref, left_ref, right_ref)
    state = [None] * SWEEPS

    def at(ref, row, c):
        return ref[row, :, c * LANE:(c + 1) * LANE]

    def advance(sweep, row, tiles):
        before = state[sweep]
        if before is None:
            state[sweep] = (tiles, None)
            return None
        centre, north = before
        south = [at(south_ref, row - 1, c) * (tiles[c] - centre[c]) for c in range(width)]
        state[sweep] = (tiles, south)
        if north is None:
            return None
        ahead, behind = from_east(centre, at_end), from_west(centre, at_start)
        fresh = []
        for c in range(width):
            change = south[c] - north[c]
            if row - 1 < HALO:
                change = change * at(south_ref, height - 1, c)
            if row - 1 >= HALO + rows:
                change = change * at(south_ref, height, c)
            across = at(east_ref, row - 1, c) * ahead[c] + at(west_ref, row - 1, c) * behind[c]
            fresh.append(at(keep_ref, row - 1, c) * centre[c] + across + change)
        return fresh

    waiting = [None] * (SWEEPS + 1)
    for tick in range(height + SWEEPS + 1):
        if waiting[SWEEPS] is not None:
            row, tiles = waiting[SWEEPS]
            for c in range(width - 1):
                out_ref[row - HALO, :, c * LANE:(c + 1) * LANE] = tiles[c][:count]
        for sweep in reversed(range(SWEEPS)):
            if sweep == 0:
                entry = (tick, load(tick, slice(begin, begin + SUB))) if tick < height else None
            else:
                entry = waiting[sweep]
            waiting[sweep + 1] = None
            if entry is not None:
                fresh = advance(sweep, *entry)
                if fresh is not None:
                    waiting[sweep + 1] = (entry[0] - 1, fresh)


def split_stack(value):
    high = value.astype(jnp.bfloat16).astype(jnp.float32)
    rest = value - high
    middle = rest.astype(jnp.bfloat16).astype(jnp.float32)
    low = rest - middle
    return jnp.concatenate([high, middle, high, low, middle, high], axis=0).astype(jnp.bfloat16)


def corr_kernel(corr_ref, *out_refs, groups, steps, sources):
    mine = lax.axis_index("tm")
    for at in range(groups):
        @pl.when(mine == at)
        def _(at=at):
            for (shift, begin, count), out_ref in zip(sources, out_refs):
                source = (at - shift) % groups * steps + begin
                block = corr_ref[source:source + count, at * steps:(at + 1) * steps]
                high = block.astype(jnp.bfloat16).astype(jnp.float32)
                rest = block - high
                middle = rest.astype(jnp.bfloat16).astype(jnp.float32)
                low = rest - middle
                depth = out_ref.shape[1] // 6
                pad = [jnp.zeros((depth - count, steps), jnp.float32)] if depth > count else []
                stack = []
                for part in (high, high, middle, high, middle, low):
                    stack += [part, *pad]
                out_ref[...] = jnp.concatenate(stack, axis=0).T.astype(jnp.bfloat16)


def mixed_row(row, corr_ref, field_refs):
    parts = []
    for ref in field_refs:
        part = ref[row]
        parts.append(part)
        if -part.shape[0] % SUB:
            parts.append(jnp.zeros((-part.shape[0] % SUB, part.shape[1]), jnp.float32))
    stacked = split_stack(jnp.concatenate(parts, axis=0) if len(parts) > 1 else parts[0])
    return jnp.dot(corr_ref[...], stacked, preferred_element_type=jnp.float32)


def make_mix(first):
    def kernel(*refs):
        *refs, out_ref = refs
        if first:
            corr_ref, *field_refs = refs
        else:
            acc_ref, corr_ref, *field_refs = refs
        for row in range(out_ref.shape[0]):
            total = mixed_row(row, corr_ref, field_refs)
            out_ref[row] = total if first else acc_ref[row] + total

    return kernel


def last_mix_kernel(acc_ref, corr_ref, field_ref, gram_ref, steps_ref, grads_ref, out_ref, message_ref, turn_ref, rows_ref):
    _, steps, rows, cols = steps_ref.shape
    slots = turn_ref.shape[0] // (rows * (cols // LANE))
    for row in range(rows):
        total = acc_ref[row] + mixed_row(row, corr_ref, [field_ref])
        for c in range(cols // LANE):
            base = (c * (rows // SUB) + row // SUB) * slots * SUB + row % SUB
            for begin, count in groups_of(steps):
                turn_ref[pl.ds(base + begin * SUB, count, stride=SUB), :] = total[begin:begin + count, c * LANE:(c + 1) * LANE]

    zero = jnp.zeros((SUB, LANE), jnp.float32)

    def body(step, sums):
        sums = list(sums)
        for c in range(cols // LANE):
            for r in range(0, rows, 2 * SUB):
                where = (step, pl.ds(r, 2 * SUB), pl.ds(c * LANE, LANE))
                halves = []
                for part in range(2):
                    base = (c * (rows // SUB) + r // SUB + part) * slots * SUB
                    halves.append(turn_ref[pl.ds(pl.multiple_of(base + step * SUB, SUB), SUB), :])
                mixed = jnp.concatenate(halves, axis=0)
                out_ref[where] = mixed
                half = mixed.astype(jnp.bfloat16).astype(jnp.float32)
                for n in range(NPROJ):
                    source = steps_ref if n < PAIRS else grads_ref
                    product = source[(n % PAIRS, *where)].astype(jnp.float32) * half
                    sums[n] = sums[n] + (product[:SUB] + product[SUB:])
        return tuple(sums)

    sums = lax.fori_loop(0, steps, body, (zero,) * NPROJ, unroll=2)
    rows_ref[0:NGRAM, :] = gram_ref[...]
    for n in range(NPROJ):
        rows_ref[NGRAM + n:NGRAM + n + 1, :] = jnp.sum(sums[n], axis=0, keepdims=True)
    lane, row = lane_index(), row_index()
    total = zero
    for first in range(0, NROW, SUB):
        summed = jnp.sum(rows_ref[first:first + SUB, :], axis=1, keepdims=True)
        total = total + jnp.where(lane == row + first, summed, 0.0)
    message = jnp.sum(total, axis=0, keepdims=True)
    message_ref[...] = jnp.broadcast_to(message[None], message_ref.shape)


def final_kernel(inbox_ref, mixed_ref, control_ref, steps_ref, grads_ref, out_hbm, out_ref, rows_ref, sems):
    totals = jnp.sum(inbox_ref[...], axis=0)
    lane, row = lane_index(), row_index()
    spread = jnp.broadcast_to(totals, (SUB, LANE))
    for first in range(0, NROW, SUB):
        picked = jnp.where(lane == row + first, spread, 0.0)
        rows_ref[first:first + SUB, :] = jnp.broadcast_to(jnp.sum(picked, axis=1, keepdims=True), (SUB, LANE))

    def entry(k):
        return jnp.broadcast_to(rows_ref[k:k + 1, :], (SUB, LANE))

    cross = {pair: entry(k) for pair, k in WHERE.items()}

    def square(i, j):
        return entry(NSYM + WHERE[(min(i, j), max(i, j))])

    gamma = cross[(PAIRS - 1, PAIRS - 1)] / square(PAIRS - 1, PAIRS - 1)
    pivot = [1.0 / cross[(i, i)] for i in range(PAIRS)]
    first = [None] * PAIRS
    for i in reversed(range(PAIRS)):
        rest = entry(NGRAM + i)
        for j in reversed(range(i + 1, PAIRS)):
            rest = rest - cross[(i, j)] * first[j]
        first[i] = rest * pivot[i]
    second = [None] * PAIRS
    for i in range(PAIRS):
        inner = -entry(NGRAM + PAIRS + i)
        for j in range(PAIRS):
            inner = inner + square(i, j) * first[j]
        rest = cross[(i, i)] * first[i] + gamma * inner
        for j in range(i):
            rest = rest - cross[(j, i)] * second[j]
        second[i] = rest * pivot[i]
    scaled = [gamma * value for value in first]

    _, steps, rows, cols = steps_ref.shape

    def body(step, carry):
        for c in range(0, cols, LANE):
            for r in range(0, rows, 2 * SUB):
                where = (step, pl.ds(r, 2 * SUB), pl.ds(c, LANE))
                mixed = mixed_ref[where]
                control = control_ref[where]
                update = [gamma * mixed[:SUB], gamma * mixed[SUB:]]
                for i in range(PAIRS):
                    s = steps_ref[(i, *where)].astype(jnp.float32)
                    y = grads_ref[(i, *where)].astype(jnp.float32)
                    for part, cut in enumerate((slice(0, SUB), slice(SUB, 2 * SUB))):
                        update[part] = update[part] + (second[i] * s[cut] - scaled[i] * y[cut])
                out_ref[step, pl.ds(r, SUB), pl.ds(c, LANE)] = control[:SUB] - update[0]
                out_ref[step, pl.ds(r + SUB, SUB), pl.ds(c, LANE)] = control[SUB:] - update[1]
        return carry

    copies = []
    for n, (begin, count) in enumerate(groups_of(steps)):
        lax.fori_loop(begin, begin + count, body, 0, unroll=2)
        part = pl.ds(begin, count)
        copies.append(pltpu.make_async_copy(out_ref.at[part], out_hbm.at[part], sems.at[n]))
        copies[-1].start()
    for copy in copies:
        copy.wait()


def matching(firsts, count):
    partner = list(range(count))
    for first in firsts:
        partner[first], partner[(first + 1) % count] = (first + 1) % count, first
    return list(enumerate(partner))


def local(gradient, control, diffusivity, land_mask, time_corr, pair_steps, pair_grads):
    steps, rows, cols = gradient.shape
    height, breadth, groups = (lax.axis_size(axis) for axis in ("lat", "lon", "tm"))
    even = matching(range(0, height - 1, 2), height)
    odd = matching(range(1, height - 1, 2), height)
    evens = matching(range(0, breadth - 1, 2), breadth)
    odds = matching(range(1, breadth, 2), breadth)
    slots = slots_of(steps)
    turn = pltpu.VMEM((rows * (cols // LANE) * slots, LANE), jnp.float32)

    field, to_swap, to_next = call(
        pack_kernel,
        (f32(rows, slots, cols), f32(HALO, slots, cols), f32(HALO, slots, cols)),
        [pltpu.with_memory_space_constraint(v, pltpu.HBM) for v in (gradient, land_mask, diffusivity)],
        specs=[HBM] * 3,
        scratch=[
            pltpu.VMEM((steps, rows, cols), jnp.float32), pltpu.VMEM((rows, cols), jnp.int32),
            pltpu.VMEM((rows, cols), jnp.float32), turn, pltpu.SemaphoreType.DMA((2 + len(groups_of(steps)),)),
        ],
        name="pack",
    )
    from_swap = lax.ppermute(to_swap, "lat", even)
    from_next = lax.ppermute(to_next, "lat", odd)
    pair_shape = jax.ShapeDtypeStruct(pair_steps.shape, jnp.bfloat16)
    gram, pair_steps, pair_grads = call(
        gram_kernel, (f32(NGRAM, LANE), pair_shape, pair_shape),
        [pltpu.with_memory_space_constraint(v, pltpu.HBM) for v in (pair_steps, pair_grads)], specs=[HBM] * 2,
        scratch=[pltpu.SemaphoreType.DMA((2, 4))],
        name="gram",
    )
    tall, wide = rows + 2 * HALO, cols + LANE
    parts = groups_of(steps)
    sources = [(0, 0, steps)] + [(shift, *part) for part in parts for shift in range(1, groups)]
    own_corr, *corrs = call(
        functools.partial(corr_kernel, groups=groups, steps=steps, sources=sources),
        [jax.ShapeDtypeStruct((steps, 6 * (count + -count % SUB)), jnp.bfloat16) for _, _, count in sources],
        (time_corr,), name="corr",
    )
    side_shape = f32(slots, -(-tall // PER) * LANE)
    whole, to_pair, to_beside = call(
        side_kernel, (f32(tall, slots, cols), side_shape, side_shape), (from_swap, field, from_next, gram), name="sides"
    )
    from_beside = lax.ppermute(to_beside, "lon", odds)
    from_pair = lax.ppermute(to_pair, "lon", evens)
    left, right, *weights = call(
        functools.partial(weight_kernel, steps=steps),
        (side_shape, side_shape, f32(tall + 1, SUB, wide), f32(tall, SUB, wide), f32(tall, SUB, wide), f32(tall, SUB, wide)),
        (whole, from_pair, from_beside),
        scratch=[pltpu.VMEM((-(-tall // SUB) * SUB + SUB, wide), jnp.float32), pltpu.VMEM((4, -(-tall // SUB) * SUB, wide), jnp.float32)],
        name="weights",
    )
    extended = (whole, left, right)
    own, other = [], []
    for begin, count in parts:
        part = call(
            functools.partial(sweep_kernel, begin=begin), f32(rows, count, cols), (*extended, *weights), name="sweeps"
        )
        own.append(part)
        for shift in range(1, groups):
            pairs = [(i, (i + shift) % groups) for i in range(groups)]
            other.append(lax.ppermute(part, "tm", pairs))
    mixed = call(make_mix(True), f32(rows, steps, cols), (own_corr, *own), name="mix_own")
    for corr, part in zip(corrs[:-1], other[:-1]):
        mixed = call(make_mix(False), f32(rows, steps, cols), (mixed, corr, part), name="mix_more")
    devices = height * breadth * groups
    mixed, message = call(
        last_mix_kernel, (f32(steps, rows, cols), f32(devices, 1, LANE)),
        (mixed, corrs[-1], other[-1], gram, pair_steps, pair_grads),
        scratch=[turn, pltpu.VMEM((NROW, LANE), jnp.float32)], name="mix_last",
    )
    inbox = lax.all_to_all(
        message, ("lat", "lon", "tm"), split_axis=0, concat_axis=0, tiled=True,
        axis_index_groups=[list(reversed(range(devices)))],
    )
    return call(
        final_kernel, pltpu.HBM((steps, rows, cols), jnp.float32), (inbox, mixed, control, pair_steps, pair_grads),
        scratch=[
            pltpu.VMEM((steps, rows, cols), jnp.float32), pltpu.VMEM((NROW, LANE), jnp.float32),
            pltpu.SemaphoreType.DMA((len(parts),)),
        ],
        outs_at=HBM, name="final",
    )


def solution(mesh):
    placed = (
        P("tm", "lat", "lon"),
        P("tm", "lat", "lon"),
        P("lat", "lon"),
        P("lat", "lon"),
        P(),
        P(None, "tm", "lat", "lon"),
        P(None, "tm", "lat", "lon"),
    )
    return jax.shard_map(
        local, mesh=mesh, in_specs=placed, out_specs=P("tm", "lat", "lon"), check_vma=False
    )
```

```python
import functools
import jax
import jax.numpy as jnp
from jax import lax
from jax.experimental import pallas as pl
from jax.experimental.pallas import tpu as pltpu
from jax.sharding import PartitionSpec as P

PAIRS = 8
SWEEPS = 6
SUB = 8
LANE = 128
HALO = SWEEPS
GROUP = 8
PER = LANE // GROUP
CROSS = [(i, j) for i in range(PAIRS) for j in range(i, PAIRS)]
NSYM = len(CROSS)
WHERE = {pair: k for k, pair in enumerate(CROSS)}
NGRAM = 2 * NSYM
NPROJ = 2 * PAIRS
NROW = NGRAM + NPROJ

VMEM = pl.BlockSpec(memory_space=pltpu.VMEM)
HBM = pl.BlockSpec(memory_space=pltpu.HBM)
PARAMS = pltpu.CompilerParams(vmem_limit_bytes=12 * 1024 * 1024)


def f32(*shape):
    return jax.ShapeDtypeStruct(shape, jnp.float32)


def call(kernel, outs, args, specs=None, scratch=(), outs_at=VMEM, name=None):
    single = not isinstance(outs, (tuple, list))
    return pl.pallas_call(
        kernel,
        out_shape=outs,
        in_specs=specs or [VMEM] * len(args),
        out_specs=outs_at if single else [outs_at] * len(outs),
        scratch_shapes=list(scratch),
        compiler_params=PARAMS,
        name=name,
    )(*args)


def lane_index():
    return lax.broadcasted_iota(jnp.int32, (SUB, LANE), 1)


def row_index():
    return lax.broadcasted_iota(jnp.int32, (SUB, LANE), 0)


def product_body(left_ref, right_ref):
    _, _, rows, cols = left_ref.shape

    def body(step, sums):
        sums = list(sums)
        for c in range(0, cols, LANE):
            for r in range(0, rows, 2 * SUB):
                where = (step, pl.ds(r, 2 * SUB), pl.ds(c, LANE))
                right = [right_ref[(i, *where)].astype(jnp.float32) for i in range(PAIRS)]
                left = right
                if left_ref is not right_ref:
                    left = [left_ref[(i, *where)].astype(jnp.float32) for i in range(PAIRS)]
                for part in range(2):
                    cut = slice(part * SUB, (part + 1) * SUB)
                    for k, (i, j) in enumerate(CROSS):
                        sums[k] = sums[k] + left[i][cut] * right[j][cut]
        return tuple(sums)

    return body


def cross_kernel(steps_hbm, grads_hbm, out_ref, steps_ref, grads_ref, sems):
    _, steps, rows, cols = steps_ref.shape
    pieces = 4
    while steps % pieces:
        pieces -= 1
    count = steps // pieces
    copies = []
    for n in range(pieces):
        part = (slice(None), pl.ds(n * count, count))
        copies.append((
            pltpu.make_async_copy(steps_hbm.at[part], steps_ref.at[part], sems.at[0, n]),
            pltpu.make_async_copy(grads_hbm.at[part], grads_ref.at[part], sems.at[1, n]),
        ))
    for pair in copies:
        for copy in pair:
            copy.start()

    sums = (jnp.zeros((SUB, LANE), jnp.float32),) * NSYM
    for n in range(pieces):
        for copy in copies[n]:
            copy.wait()
        sums = lax.fori_loop(n * count, (n + 1) * count, product_body(steps_ref, grads_ref), sums)
    for k in range(NSYM):
        out_ref[k:k + 1, :] = jnp.sum(sums[k], axis=0, keepdims=True)


def square_kernel(grads_ref, order_ref, out_ref):
    steps = grads_ref.shape[1]
    sums = (jnp.zeros((SUB, LANE), jnp.float32),) * NSYM
    sums = lax.fori_loop(0, steps, product_body(grads_ref, grads_ref), sums)
    for k in range(NSYM):
        out_ref[k:k + 1, :] = jnp.sum(sums[k], axis=0, keepdims=True)


def groups_of(steps):
    return [(begin, min(SUB, steps - begin)) for begin in range(0, steps, SUB)]


def slots_of(steps):
    return -(-(steps + 1) // SUB) * SUB


def message_rows(steps):
    return -(-HALO * (steps + 1) // SUB) * SUB


def message_parts(row, steps):
    full = (steps + 1) // SUB * SUB
    rest = steps + 1 - full
    parts = [(slice(row * full, (row + 1) * full), slice(0, full))] if full else []
    if rest:
        start = HALO * full + row * rest
        parts.append((slice(start, start + rest), slice(full, steps + 1)))
    return parts


def pack_kernel(grad_hbm, mask_hbm, diff_hbm, field_ref, swap_ref, next_ref, grad_ref, mask_ref, diff_ref, turn_ref, sems):
    steps, rows, cols = grad_ref.shape
    slots = field_ref.shape[1]
    pieces = [(begin, min(SUB, steps - begin)) for begin in range(0, steps, SUB)]
    copies = [pltpu.make_async_copy(mask_hbm, mask_ref, sems.at[0]), pltpu.make_async_copy(diff_hbm, diff_ref, sems.at[1])]
    for n, (begin, count) in enumerate(pieces):
        part = pl.ds(begin, count)
        copies.append(pltpu.make_async_copy(grad_hbm.at[part], grad_ref.at[part], sems.at[2 + n]))
    for copy in copies:
        copy.start()
    copies[0].wait()
    copies[1].wait()
    zero = jnp.zeros((SUB, LANE), jnp.float32)
    tiles = [
        (slice(r * SUB, (r + 1) * SUB), slice(c * LANE, (c + 1) * LANE), (c * (rows // SUB) + r) * slots * SUB)
        for c in range(cols // LANE) for r in range(rows // SUB)
    ]
    mask = [mask_ref[down, across].astype(jnp.float32) for down, across, _ in tiles]
    for slot in range(steps, slots):
        for down, across, base in tiles:
            value = diff_ref[down, across] if slot == steps else zero
            turn_ref[base + slot * SUB:base + (slot + 1) * SUB, :] = value
    for n, (begin, count) in enumerate(pieces):
        copies[2 + n].wait()
        for slot in range(begin, begin + count):
            for (down, across, base), keep in zip(tiles, mask):
                turn_ref[base + slot * SUB:base + (slot + 1) * SUB, :] = grad_ref[slot, down, across] * keep
    for c in range(cols // LANE):
        across = slice(c * LANE, (c + 1) * LANE)
        for row in range(rows):
            base = (c * (rows // SUB) + row // SUB) * slots * SUB + row % SUB
            for slot in range(0, slots, SUB):
                value = turn_ref[pl.ds(base + slot * SUB, SUB, stride=SUB), :]
                field_ref[row, slot:slot + SUB, across] = value
    odd = lax.rem(lax.axis_index("lat"), 2)
    near, far = (1 - odd) * (rows - HALO), odd * (rows - HALO)
    for row in range(HALO):
        for place, there in message_parts(row, steps):
            swap_ref[place] = field_ref[near + row, there]
            next_ref[place] = field_ref[far + row, there]


def side_kernel(swap_ref, field_ref, next_ref, order_ref, whole_ref, pair_ref, beside_ref, *, steps):
    rows, slots, cols = field_ref.shape
    place, count = lax.axis_index("lat"), lax.axis_size("lat")
    odd = lax.rem(place, 2)
    near, far = (1 - odd) * (HALO + rows), odd * (HALO + rows)
    after = place - 1 + 2 * odd
    bounds = jnp.full((1, cols), place + 1 - 2 * odd, jnp.int32) < count, jnp.full((1, cols), after, jnp.int32)
    inside = bounds[0], (bounds[1] >= 0) & (bounds[1] < count)
    for row in range(HALO):
        for source, target in message_parts(row, steps):
            whole_ref[near + row, target] = jnp.where(inside[0], swap_ref[source], 0.0)
            whole_ref[far + row, target] = jnp.where(inside[1], next_ref[source], 0.0)
        if steps + 1 < slots:
            whole_ref[near + row, steps + 1:] = jnp.zeros((slots - steps - 1, cols), jnp.float32)
            whole_ref[far + row, steps + 1:] = jnp.zeros((slots - steps - 1, cols), jnp.float32)
    for row in range(rows):
        whole_ref[HALO + row] = field_ref[row]
    lane = lane_index()
    uneven = jnp.full((SUB, LANE), lax.rem(lax.axis_index("lon"), 2), jnp.int32) == 1
    for slot in range(0, slots, SUB):
        down = slice(slot, slot + SUB)
        for base in range(0, rows + 2 * HALO, PER):
            west = east = jnp.zeros((SUB, LANE), jnp.float32)
            for row in range(base, min(base + PER, rows + 2 * HALO)):
                begin = (row - base) * GROUP
                here = (lane >= begin) & (lane < begin + GROUP)
                left = whole_ref[row, down, 0:LANE]
                right = whole_ref[row, down, cols - LANE:cols]
                west = jnp.where(here, pltpu.roll(left, begin, 1) if begin else left, west)
                turn = (begin + GROUP) % LANE
                east = jnp.where(here, pltpu.roll(right, turn, 1) if turn else right, east)
            across = slice(base // PER * LANE, (base // PER + 1) * LANE)
            pair_ref[down, across] = jnp.where(uneven, west, east)
            beside_ref[down, across] = jnp.where(uneven, east, west)


def make_row_loader(whole_ref, left_ref, right_ref):
    cols = whole_ref.shape[2]
    lane = lax.broadcasted_iota(jnp.int32, (1, LANE), 1)

    def load(row, down):
        place = slice(row // PER * LANE, (row // PER + 1) * LANE)
        begin = row % PER * GROUP
        tiles = [whole_ref[row, down, c * LANE:(c + 1) * LANE] for c in range(cols // LANE)]
        east, west = right_ref[down, place], left_ref[down, place]
        east = pltpu.roll(east, LANE - begin, 1) if begin else east
        turn = (2 * LANE - GROUP - begin) % LANE
        west = pltpu.roll(west, turn, 1) if turn else west
        return tiles + [jnp.where(lane < LANE // 2, east, west)]

    return load


def from_east(tiles, at_end):
    turned = [pltpu.roll(tile, LANE - 1, 1) for tile in tiles]
    return [jnp.where(at_end, turned[(c + 1) % len(tiles)], turned[c]) for c in range(len(tiles))]


def from_west(tiles, at_start):
    turned = [pltpu.roll(tile, 1, 1) for tile in tiles]
    return [jnp.where(at_start, turned[c - 1], turned[c]) for c in range(len(tiles))]


def weight_kernel(
    whole_ref, pair_ref, beside_ref, left_ref, right_ref, south_ref, east_ref, west_ref, keep_ref, kappa_ref, packed_ref, *, steps
):
    height, _, cols = whole_ref.shape
    uneven = jnp.full(pair_ref.shape, lax.rem(lax.axis_index("lon"), 2), jnp.int32) == 1
    left_ref[...] = jnp.where(uneven, pair_ref[...], beside_ref[...])
    right_ref[...] = jnp.where(uneven, beside_ref[...], pair_ref[...])
    width = cols // LANE + 1
    load = make_row_loader(whole_ref, left_ref, right_ref)
    lane = lane_index()
    at_start, at_end = lane == 0, lane == LANE - 1
    for row in range(height):
        for c, tile in enumerate(load(row, slice(steps, steps + 1))):
            kappa_ref[row:row + 1, c * LANE:(c + 1) * LANE] = tile
    for first in range(0, height, SUB):
        down = slice(first, first + SUB)
        kappa = [kappa_ref[down, c * LANE:(c + 1) * LANE] for c in range(width)]
        below = [kappa_ref[first + 1:first + 1 + SUB, c * LANE:(c + 1) * LANE] for c in range(width)]
        beside = from_east(kappa, at_end)
        east = [0.5 * (kappa[c] + beside[c]) for c in range(width)]
        west = from_west(east, at_start)
        for c in range(width):
            across = slice(c * LANE, (c + 1) * LANE)
            packed_ref[0, down, across] = 0.5 * (kappa[c] + below[c])
            packed_ref[1, down, across] = east[c]
            packed_ref[2, down, across] = west[c]
            packed_ref[3, down, across] = 1.0 - east[c] - west[c]
    for n, ref in enumerate((south_ref, east_ref, west_ref, keep_ref)):
        for row in range(height - 1):
            ref[row] = jnp.broadcast_to(packed_ref[n, row:row + 1, :], ref.shape[1:])
    for side, row in enumerate((HALO - 1, height - HALO)):
        inside = jnp.where(kappa_ref[row:row + 1, :] > 0.0, 1.0, 0.0)
        south_ref[height - 1 + side] = jnp.broadcast_to(inside, south_ref.shape[1:])


def sweep_kernel(whole_ref, left_ref, right_ref, south_ref, east_ref, west_ref, keep_ref, out_ref, *, begin):
    height, _, cols = whole_ref.shape
    rows, width = height - 2 * HALO, cols // LANE + 1
    count = out_ref.shape[1]
    lane = lane_index()
    at_start, at_end = lane == 0, lane == LANE - 1
    load = make_row_loader(whole_ref, left_ref, right_ref)
    state = [None] * SWEEPS

    def at(ref, row, c):
        return ref[row, :, c * LANE:(c + 1) * LANE]

    def advance(sweep, row, tiles):
        before = state[sweep]
        if before is None:
            state[sweep] = (tiles, None)
            return None
        centre, north = before
        south = [at(south_ref, row - 1, c) * (tiles[c] - centre[c]) for c in range(width)]
        state[sweep] = (tiles, south)
        if north is None:
            return None
        ahead, behind = from_east(centre, at_end), from_west(centre, at_start)
        fresh = []
        for c in range(width):
            change = south[c] - north[c]
            if row - 1 < HALO:
                change = change * at(south_ref, height - 1, c)
            if row - 1 >= HALO + rows:
                change = change * at(south_ref, height, c)
            across = at(east_ref, row - 1, c) * ahead[c] + at(west_ref, row - 1, c) * behind[c]
            fresh.append(at(keep_ref, row - 1, c) * centre[c] + across + change)
        return fresh

    waiting = [None] * (SWEEPS + 1)
    for tick in range(height + SWEEPS + 1):
        if waiting[SWEEPS] is not None:
            row, tiles = waiting[SWEEPS]
            for c in range(width - 1):
                out_ref[row - HALO, :, c * LANE:(c + 1) * LANE] = tiles[c][:count]
        for sweep in reversed(range(SWEEPS)):
            if sweep == 0:
                entry = (tick, load(tick, slice(begin, begin + SUB))) if tick < height else None
            else:
                entry = waiting[sweep]
            waiting[sweep + 1] = None
            if entry is not None:
                fresh = advance(sweep, *entry)
                if fresh is not None:
                    waiting[sweep + 1] = (entry[0] - 1, fresh)


def split_stack(value):
    high = value.astype(jnp.bfloat16).astype(jnp.float32)
    rest = value - high
    middle = rest.astype(jnp.bfloat16).astype(jnp.float32)
    low = rest - middle
    return jnp.concatenate([high, middle, high, low, middle, high], axis=0).astype(jnp.bfloat16)


def corr_kernel(corr_ref, *out_refs, groups, steps, sources):
    mine = lax.axis_index("tm")
    for at in range(groups):
        @pl.when(mine == at)
        def _(at=at):
            for (shift, begin, count), out_ref in zip(sources, out_refs):
                source = (at - shift) % groups * steps + begin
                block = corr_ref[source:source + count, at * steps:(at + 1) * steps]
                high = block.astype(jnp.bfloat16).astype(jnp.float32)
                rest = block - high
                middle = rest.astype(jnp.bfloat16).astype(jnp.float32)
                low = rest - middle
                depth = out_ref.shape[1] // 6
                pad = [jnp.zeros((depth - count, steps), jnp.float32)] if depth > count else []
                stack = []
                for part in (high, high, middle, high, middle, low):
                    stack += [part, *pad]
                out_ref[...] = jnp.concatenate(stack, axis=0).T.astype(jnp.bfloat16)


def mixed_row(row, corr_ref, field_refs):
    parts = []
    for ref in field_refs:
        part = ref[row]
        parts.append(part)
        if -part.shape[0] % SUB:
            parts.append(jnp.zeros((-part.shape[0] % SUB, part.shape[1]), jnp.float32))
    stacked = split_stack(jnp.concatenate(parts, axis=0) if len(parts) > 1 else parts[0])
    return jnp.dot(corr_ref[...], stacked, preferred_element_type=jnp.float32)


def make_mix(first):
    def kernel(*refs):
        *refs, out_ref = refs
        if first:
            corr_ref, *field_refs = refs
        else:
            acc_ref, corr_ref, *field_refs = refs
        for row in range(out_ref.shape[0]):
            total = mixed_row(row, corr_ref, field_refs)
            out_ref[row] = total if first else acc_ref[row] + total

    return kernel


def last_mix_kernel(acc_ref, corr_ref, field_ref, cross_ref, square_ref, steps_ref, grads_ref, out_ref, message_ref, turn_ref, rows_ref):
    _, steps, rows, cols = steps_ref.shape
    slots = turn_ref.shape[0] // (rows * (cols // LANE))
    for row in range(rows):
        total = acc_ref[row] + mixed_row(row, corr_ref, [field_ref])
        for c in range(cols // LANE):
            base = (c * (rows // SUB) + row // SUB) * slots * SUB + row % SUB
            for begin, count in groups_of(steps):
                turn_ref[pl.ds(base + begin * SUB, count, stride=SUB), :] = total[begin:begin + count, c * LANE:(c + 1) * LANE]

    zero = jnp.zeros((SUB, LANE), jnp.float32)

    def body(step, sums):
        sums = list(sums)
        for c in range(cols // LANE):
            for r in range(0, rows, 2 * SUB):
                where = (step, pl.ds(r, 2 * SUB), pl.ds(c * LANE, LANE))
                halves = []
                for part in range(2):
                    base = (c * (rows // SUB) + r // SUB + part) * slots * SUB
                    halves.append(turn_ref[pl.ds(pl.multiple_of(base + step * SUB, SUB), SUB), :])
                mixed = jnp.concatenate(halves, axis=0)
                out_ref[where] = mixed
                half = mixed.astype(jnp.bfloat16).astype(jnp.float32)
                for n in range(NPROJ):
                    source = steps_ref if n < PAIRS else grads_ref
                    product = source[(n % PAIRS, *where)].astype(jnp.float32) * half
                    sums[n] = sums[n] + (product[:SUB] + product[SUB:])
        return tuple(sums)

    sums = lax.fori_loop(0, steps, body, (zero,) * NPROJ, unroll=2)
    rows_ref[0:NSYM, :] = cross_ref[...]
    rows_ref[NSYM:NGRAM, :] = square_ref[...]
    for n in range(NPROJ):
        rows_ref[NGRAM + n:NGRAM + n + 1, :] = jnp.sum(sums[n], axis=0, keepdims=True)
    lane, row = lane_index(), row_index()
    total = zero
    for first in range(0, NROW, SUB):
        summed = jnp.sum(rows_ref[first:first + SUB, :], axis=1, keepdims=True)
        total = total + jnp.where(lane == row + first, summed, 0.0)
    message = jnp.sum(total, axis=0, keepdims=True)
    message_ref[...] = jnp.broadcast_to(message[None], message_ref.shape)


def final_kernel(inbox_ref, mixed_ref, control_ref, steps_ref, grads_ref, out_hbm, out_ref, rows_ref, sems):
    totals = jnp.sum(inbox_ref[...], axis=0)
    lane, row = lane_index(), row_index()
    spread = jnp.broadcast_to(totals, (SUB, LANE))
    for first in range(0, NROW, SUB):
        picked = jnp.where(lane == row + first, spread, 0.0)
        rows_ref[first:first + SUB, :] = jnp.broadcast_to(jnp.sum(picked, axis=1, keepdims=True), (SUB, LANE))

    def entry(k):
        return jnp.broadcast_to(rows_ref[k:k + 1, :], (SUB, LANE))

    cross = {pair: entry(k) for pair, k in WHERE.items()}

    def square(i, j):
        return entry(NSYM + WHERE[(min(i, j), max(i, j))])

    gamma = cross[(PAIRS - 1, PAIRS - 1)] / square(PAIRS - 1, PAIRS - 1)
    pivot = [1.0 / cross[(i, i)] for i in range(PAIRS)]
    first = [None] * PAIRS
    for i in reversed(range(PAIRS)):
        rest = entry(NGRAM + i)
        for j in reversed(range(i + 1, PAIRS)):
            rest = rest - cross[(i, j)] * first[j]
        first[i] = rest * pivot[i]
    second = [None] * PAIRS
    for i in range(PAIRS):
        inner = -entry(NGRAM + PAIRS + i)
        for j in range(PAIRS):
            inner = inner + square(i, j) * first[j]
        rest = cross[(i, i)] * first[i] + gamma * inner
        for j in range(i):
            rest = rest - cross[(j, i)] * second[j]
        second[i] = rest * pivot[i]
    scaled = [gamma * value for value in first]

    _, steps, rows, cols = steps_ref.shape

    def body(step, carry):
        for c in range(0, cols, LANE):
            for r in range(0, rows, 2 * SUB):
                where = (step, pl.ds(r, 2 * SUB), pl.ds(c, LANE))
                mixed = mixed_ref[where]
                control = control_ref[where]
                update = [gamma * mixed[:SUB], gamma * mixed[SUB:]]
                for i in range(PAIRS):
                    s = steps_ref[(i, *where)].astype(jnp.float32)
                    y = grads_ref[(i, *where)].astype(jnp.float32)
                    for part, cut in enumerate((slice(0, SUB), slice(SUB, 2 * SUB))):
                        update[part] = update[part] + (second[i] * s[cut] - scaled[i] * y[cut])
                out_ref[step, pl.ds(r, SUB), pl.ds(c, LANE)] = control[:SUB] - update[0]
                out_ref[step, pl.ds(r + SUB, SUB), pl.ds(c, LANE)] = control[SUB:] - update[1]
        return carry

    copies = []
    for n, (begin, count) in enumerate(groups_of(steps)):
        lax.fori_loop(begin, begin + count, body, 0, unroll=2)
        part = pl.ds(begin, count)
        copies.append(pltpu.make_async_copy(out_ref.at[part], out_hbm.at[part], sems.at[n]))
        copies[-1].start()
    for copy in copies:
        copy.wait()


def matching(firsts, count):
    partner = list(range(count))
    for first in firsts:
        partner[first], partner[(first + 1) % count] = (first + 1) % count, first
    return list(enumerate(partner))


def local(gradient, control, diffusivity, land_mask, time_corr, pair_steps, pair_grads):
    steps, rows, cols = gradient.shape
    height, breadth, groups = (lax.axis_size(axis) for axis in ("lat", "lon", "tm"))
    even = matching(range(0, height - 1, 2), height)
    odd = matching(range(1, height - 1, 2), height)
    evens = matching(range(0, breadth - 1, 2), breadth)
    odds = matching(range(1, breadth, 2), breadth)
    slots = slots_of(steps)
    turn = pltpu.VMEM((rows * (cols // LANE) * slots, LANE), jnp.float32)

    field, to_swap, to_next = call(
        pack_kernel,
        (f32(rows, slots, cols), f32(message_rows(steps), cols), f32(message_rows(steps), cols)),
        [pltpu.with_memory_space_constraint(v, pltpu.HBM) for v in (gradient, land_mask, diffusivity)],
        specs=[HBM] * 3,
        scratch=[
            pltpu.VMEM((steps, rows, cols), jnp.float32), pltpu.VMEM((rows, cols), jnp.int32),
            pltpu.VMEM((rows, cols), jnp.float32), turn, pltpu.SemaphoreType.DMA((2 + len(groups_of(steps)),)),
        ],
        name="pack",
    )
    from_swap = lax.ppermute(to_swap, "lat", even)
    from_next = lax.ppermute(to_next, "lat", odd)
    pair_shape = jax.ShapeDtypeStruct(pair_steps.shape, jnp.bfloat16)
    cross, pair_steps, pair_grads = call(
        cross_kernel, (f32(NSYM, LANE), pair_shape, pair_shape),
        [pltpu.with_memory_space_constraint(v, pltpu.HBM) for v in (pair_steps, pair_grads)], specs=[HBM] * 2,
        scratch=[pltpu.SemaphoreType.DMA((2, 4))],
        name="cross",
    )
    tall, wide = rows + 2 * HALO, cols + LANE
    parts = groups_of(steps)
    sources = [(0, 0, steps)] + [(shift, *part) for part in parts for shift in range(1, groups)]
    own_corr, *corrs = call(
        functools.partial(corr_kernel, groups=groups, steps=steps, sources=sources),
        [jax.ShapeDtypeStruct((steps, 6 * (count + -count % SUB)), jnp.bfloat16) for _, _, count in sources],
        (time_corr,), name="corr",
    )
    side_shape = f32(slots, -(-tall // PER) * LANE)
    whole, to_pair, to_beside = call(
        functools.partial(side_kernel, steps=steps), (f32(tall, slots, cols), side_shape, side_shape), (from_swap, field, from_next, cross), name="sides"
    )
    from_beside = lax.ppermute(to_beside, "lon", odds)
    from_pair = lax.ppermute(to_pair, "lon", evens)
    left, right, *weights = call(
        functools.partial(weight_kernel, steps=steps),
        (side_shape, side_shape, f32(tall + 1, SUB, wide), f32(tall, SUB, wide), f32(tall, SUB, wide), f32(tall, SUB, wide)),
        (whole, from_pair, from_beside),
        scratch=[pltpu.VMEM((-(-tall // SUB) * SUB + SUB, wide), jnp.float32), pltpu.VMEM((4, -(-tall // SUB) * SUB, wide), jnp.float32)],
        name="weights",
    )
    extended = (whole, left, right)
    own, other = [], []
    for begin, count in parts:
        part = call(
            functools.partial(sweep_kernel, begin=begin), f32(rows, count, cols), (*extended, *weights), name="sweeps"
        )
        own.append(part)
        for shift in range(1, groups):
            pairs = [(i, (i + shift) % groups) for i in range(groups)]
            other.append(lax.ppermute(part, "tm", pairs))
    mixed = call(make_mix(True), f32(rows, steps, cols), (own_corr, *own), name="mix_own")
    square = call(square_kernel, f32(NSYM, LANE), (pair_grads, mixed), name="square")
    for corr, part in zip(corrs[:-1], other[:-1]):
        mixed = call(make_mix(False), f32(rows, steps, cols), (mixed, corr, part), name="mix_more")
    devices = height * breadth * groups
    mixed, message = call(
        last_mix_kernel, (f32(steps, rows, cols), f32(devices, 1, LANE)),
        (mixed, corrs[-1], other[-1], cross, square, pair_steps, pair_grads),
        scratch=[turn, pltpu.VMEM((NROW, LANE), jnp.float32)], name="mix_last",
    )
    inbox = lax.all_to_all(
        message, ("lat", "lon", "tm"), split_axis=0, concat_axis=0, tiled=True,
        axis_index_groups=[list(reversed(range(devices)))],
    )
    return call(
        final_kernel, pltpu.HBM((steps, rows, cols), jnp.float32), (inbox, mixed, control, pair_steps, pair_grads),
        scratch=[
            pltpu.VMEM((steps, rows, cols), jnp.float32), pltpu.VMEM((NROW, LANE), jnp.float32),
            pltpu.SemaphoreType.DMA((len(parts),)),
        ],
        outs_at=HBM, name="final",
    )


def solution(mesh):
    placed = (
        P("tm", "lat", "lon"),
        P("tm", "lat", "lon"),
        P("lat", "lon"),
        P("lat", "lon"),
        P(),
        P(None, "tm", "lat", "lon"),
        P(None, "tm", "lat", "lon"),
    )
    return jax.shard_map(
        local, mesh=mesh, in_specs=placed, out_specs=P("tm", "lat", "lon"), check_vma=False
    )
```

```python
import functools
import jax
import jax.numpy as jnp
from jax import lax
from jax.experimental import pallas as pl
from jax.experimental.pallas import tpu as pltpu
from jax.sharding import PartitionSpec as P

PAIRS = 8
SWEEPS = 6
SUB = 8
LANE = 128
HALO = SWEEPS
GROUP = 8
PER = LANE // GROUP
CROSS = [(i, j) for i in range(PAIRS) for j in range(i, PAIRS)]
NSYM = len(CROSS)
WHERE = {pair: k for k, pair in enumerate(CROSS)}
NGRAM = 2 * NSYM
NPROJ = 2 * PAIRS
NROW = NGRAM + NPROJ

VMEM = pl.BlockSpec(memory_space=pltpu.VMEM)
HBM = pl.BlockSpec(memory_space=pltpu.HBM)
PARAMS = pltpu.CompilerParams(vmem_limit_bytes=12 * 1024 * 1024)


def f32(*shape):
    return jax.ShapeDtypeStruct(shape, jnp.float32)


def call(kernel, outs, args, specs=None, scratch=(), outs_at=VMEM, name=None):
    single = not isinstance(outs, (tuple, list))
    return pl.pallas_call(
        kernel,
        out_shape=outs,
        in_specs=specs or [VMEM] * len(args),
        out_specs=outs_at if single else [outs_at] * len(outs),
        scratch_shapes=list(scratch),
        compiler_params=PARAMS,
        name=name,
    )(*args)


def lane_index():
    return lax.broadcasted_iota(jnp.int32, (SUB, LANE), 1)


def row_index():
    return lax.broadcasted_iota(jnp.int32, (SUB, LANE), 0)


def product_body(left_ref, right_ref):
    _, _, rows, cols = left_ref.shape

    def body(step, sums):
        sums = list(sums)
        for c in range(0, cols, LANE):
            for r in range(0, rows, 2 * SUB):
                where = (step, pl.ds(r, 2 * SUB), pl.ds(c, LANE))
                right = [right_ref[(i, *where)].astype(jnp.float32) for i in range(PAIRS)]
                left = right
                if left_ref is not right_ref:
                    left = [left_ref[(i, *where)].astype(jnp.float32) for i in range(PAIRS)]
                for part in range(2):
                    cut = slice(part * SUB, (part + 1) * SUB)
                    for k, (i, j) in enumerate(CROSS):
                        sums[k] = sums[k] + left[i][cut] * right[j][cut]
        return tuple(sums)

    return body


def cross_kernel(steps_hbm, grads_hbm, out_ref, steps_ref, grads_ref, sems):
    _, steps, rows, cols = steps_ref.shape
    pieces = 4
    while steps % pieces:
        pieces -= 1
    count = steps // pieces
    copies = []
    for n in range(pieces):
        part = (slice(None), pl.ds(n * count, count))
        copies.append((
            pltpu.make_async_copy(steps_hbm.at[part], steps_ref.at[part], sems.at[0, n]),
            pltpu.make_async_copy(grads_hbm.at[part], grads_ref.at[part], sems.at[1, n]),
        ))
    for pair in copies:
        for copy in pair:
            copy.start()

    sums = (jnp.zeros((SUB, LANE), jnp.float32),) * NSYM
    for n in range(pieces):
        for copy in copies[n]:
            copy.wait()
        sums = lax.fori_loop(n * count, (n + 1) * count, product_body(steps_ref, grads_ref), sums)
    for k in range(NSYM):
        out_ref[k:k + 1, :] = jnp.sum(sums[k], axis=0, keepdims=True)


def square_kernel(grads_ref, order_ref, out_ref):
    steps = grads_ref.shape[1]
    sums = (jnp.zeros((SUB, LANE), jnp.float32),) * NSYM
    sums = lax.fori_loop(0, steps, product_body(grads_ref, grads_ref), sums)
    for k in range(NSYM):
        out_ref[k:k + 1, :] = jnp.sum(sums[k], axis=0, keepdims=True)


def groups_of(steps):
    return [(begin, min(SUB, steps - begin)) for begin in range(0, steps, SUB)]


def slots_of(steps):
    return -(-(steps + 1) // SUB) * SUB


def message_rows(steps):
    return -(-HALO * (steps + 1) // SUB) * SUB


def message_parts(row, steps):
    full = (steps + 1) // SUB * SUB
    rest = steps + 1 - full
    parts = [(slice(row * full, (row + 1) * full), slice(0, full))] if full else []
    if rest:
        start = HALO * full + row * rest
        parts.append((slice(start, start + rest), slice(full, steps + 1)))
    return parts


def pack_kernel(grad_hbm, mask_hbm, diff_hbm, field_ref, swap_ref, grad_ref, mask_ref, diff_ref, turn_ref, sems):
    steps, rows, cols = grad_ref.shape
    slots = field_ref.shape[1]
    pieces = [(begin, min(SUB, steps - begin)) for begin in range(0, steps, SUB)]
    copies = [pltpu.make_async_copy(mask_hbm, mask_ref, sems.at[0]), pltpu.make_async_copy(diff_hbm, diff_ref, sems.at[1])]
    for n, (begin, count) in enumerate(pieces):
        part = pl.ds(begin, count)
        copies.append(pltpu.make_async_copy(grad_hbm.at[part], grad_ref.at[part], sems.at[2 + n]))
    for copy in copies:
        copy.start()
    copies[0].wait()
    copies[1].wait()
    zero = jnp.zeros((SUB, LANE), jnp.float32)
    tiles = [
        (slice(r * SUB, (r + 1) * SUB), slice(c * LANE, (c + 1) * LANE), (c * (rows // SUB) + r) * slots * SUB)
        for c in range(cols // LANE) for r in range(rows // SUB)
    ]
    mask = [mask_ref[down, across].astype(jnp.float32) for down, across, _ in tiles]
    for slot in range(steps, slots):
        for down, across, base in tiles:
            value = diff_ref[down, across] if slot == steps else zero
            turn_ref[base + slot * SUB:base + (slot + 1) * SUB, :] = value
    for n, (begin, count) in enumerate(pieces):
        copies[2 + n].wait()
        for slot in range(begin, begin + count):
            for (down, across, base), keep in zip(tiles, mask):
                turn_ref[base + slot * SUB:base + (slot + 1) * SUB, :] = grad_ref[slot, down, across] * keep
    for c in range(cols // LANE):
        across = slice(c * LANE, (c + 1) * LANE)
        for row in range(rows):
            base = (c * (rows // SUB) + row // SUB) * slots * SUB + row % SUB
            for slot in range(0, slots, SUB):
                value = turn_ref[pl.ds(base + slot * SUB, SUB, stride=SUB), :]
                field_ref[row, slot:slot + SUB, across] = value
    odd = lax.rem(lax.axis_index("lat"), 2)
    near = (1 - odd) * (rows - HALO)
    for row in range(HALO):
        for place, there in message_parts(row, steps):
            swap_ref[place] = field_ref[near + row, there]


def next_kernel(field_ref, next_ref, *, steps):
    far = lax.rem(lax.axis_index("lat"), 2) * (field_ref.shape[0] - HALO)
    for row in range(HALO):
        for place, there in message_parts(row, steps):
            next_ref[place] = field_ref[far + row, there]


def side_kernel(next_ref, field_ref, swap_ref, order_ref, whole_ref, pair_ref, beside_ref, *, steps):
    rows, slots, cols = field_ref.shape
    place, count = lax.axis_index("lat"), lax.axis_size("lat")
    odd = lax.rem(place, 2)
    near, far = (1 - odd) * (HALO + rows), odd * (HALO + rows)
    after = place - 1 + 2 * odd
    bounds = jnp.full((1, cols), place + 1 - 2 * odd, jnp.int32) < count, jnp.full((1, cols), after, jnp.int32)
    inside = bounds[0], (bounds[1] >= 0) & (bounds[1] < count)
    for row in range(HALO):
        for source, target in message_parts(row, steps):
            whole_ref[near + row, target] = jnp.where(inside[0], swap_ref[source], 0.0)
            whole_ref[far + row, target] = jnp.where(inside[1], next_ref[source], 0.0)
        if steps + 1 < slots:
            whole_ref[near + row, steps + 1:] = jnp.zeros((slots - steps - 1, cols), jnp.float32)
            whole_ref[far + row, steps + 1:] = jnp.zeros((slots - steps - 1, cols), jnp.float32)
    for row in range(rows):
        whole_ref[HALO + row] = field_ref[row]
    lane = lane_index()
    uneven = jnp.full((SUB, LANE), lax.rem(lax.axis_index("lon"), 2), jnp.int32) == 1
    for slot in range(0, slots, SUB):
        down = slice(slot, slot + SUB)
        for base in range(0, rows + 2 * HALO, PER):
            west = east = jnp.zeros((SUB, LANE), jnp.float32)
            for row in range(base, min(base + PER, rows + 2 * HALO)):
                begin = (row - base) * GROUP
                here = (lane >= begin) & (lane < begin + GROUP)
                left = whole_ref[row, down, 0:LANE]
                right = whole_ref[row, down, cols - LANE:cols]
                west = jnp.where(here, pltpu.roll(left, begin, 1) if begin else left, west)
                turn = (begin + GROUP) % LANE
                east = jnp.where(here, pltpu.roll(right, turn, 1) if turn else right, east)
            across = slice(base // PER * LANE, (base // PER + 1) * LANE)
            pair_ref[down, across] = jnp.where(uneven, west, east)
            beside_ref[down, across] = jnp.where(uneven, east, west)


def make_row_loader(whole_ref, left_ref, right_ref):
    cols = whole_ref.shape[2]
    lane = lax.broadcasted_iota(jnp.int32, (1, LANE), 1)

    def load(row, down):
        place = slice(row // PER * LANE, (row // PER + 1) * LANE)
        begin = row % PER * GROUP
        tiles = [whole_ref[row, down, c * LANE:(c + 1) * LANE] for c in range(cols // LANE)]
        east, west = right_ref[down, place], left_ref[down, place]
        east = pltpu.roll(east, LANE - begin, 1) if begin else east
        turn = (2 * LANE - GROUP - begin) % LANE
        west = pltpu.roll(west, turn, 1) if turn else west
        return tiles + [jnp.where(lane < LANE // 2, east, west)]

    return load


def from_east(tiles, at_end):
    turned = [pltpu.roll(tile, LANE - 1, 1) for tile in tiles]
    return [jnp.where(at_end, turned[(c + 1) % len(tiles)], turned[c]) for c in range(len(tiles))]


def from_west(tiles, at_start):
    turned = [pltpu.roll(tile, 1, 1) for tile in tiles]
    return [jnp.where(at_start, turned[c - 1], turned[c]) for c in range(len(tiles))]


def weight_kernel(
    whole_ref, pair_ref, beside_ref, left_ref, right_ref, south_ref, east_ref, west_ref, keep_ref, kappa_ref, packed_ref, *, steps
):
    height, _, cols = whole_ref.shape
    uneven = jnp.full(pair_ref.shape, lax.rem(lax.axis_index("lon"), 2), jnp.int32) == 1
    left_ref[...] = jnp.where(uneven, pair_ref[...], beside_ref[...])
    right_ref[...] = jnp.where(uneven, beside_ref[...], pair_ref[...])
    width = cols // LANE + 1
    load = make_row_loader(whole_ref, left_ref, right_ref)
    lane = lane_index()
    at_start, at_end = lane == 0, lane == LANE - 1
    for row in range(height):
        for c, tile in enumerate(load(row, slice(steps, steps + 1))):
            kappa_ref[row:row + 1, c * LANE:(c + 1) * LANE] = tile
    for first in range(0, height, SUB):
        down = slice(first, first + SUB)
        kappa = [kappa_ref[down, c * LANE:(c + 1) * LANE] for c in range(width)]
        below = [kappa_ref[first + 1:first + 1 + SUB, c * LANE:(c + 1) * LANE] for c in range(width)]
        beside = from_east(kappa, at_end)
        east = [0.5 * (kappa[c] + beside[c]) for c in range(width)]
        west = from_west(east, at_start)
        for c in range(width):
            across = slice(c * LANE, (c + 1) * LANE)
            packed_ref[0, down, across] = 0.5 * (kappa[c] + below[c])
            packed_ref[1, down, across] = east[c]
            packed_ref[2, down, across] = west[c]
            packed_ref[3, down, across] = 1.0 - east[c] - west[c]
    for n, ref in enumerate((south_ref, east_ref, west_ref, keep_ref)):
        for row in range(height - 1):
            ref[row] = jnp.broadcast_to(packed_ref[n, row:row + 1, :], ref.shape[1:])
    for side, row in enumerate((HALO - 1, height - HALO)):
        inside = jnp.where(kappa_ref[row:row + 1, :] > 0.0, 1.0, 0.0)
        south_ref[height - 1 + side] = jnp.broadcast_to(inside, south_ref.shape[1:])


def sweep_kernel(whole_ref, left_ref, right_ref, south_ref, east_ref, west_ref, keep_ref, out_ref, mid_ref, *, begin):
    height, _, cols = whole_ref.shape
    rows, width = height - 2 * HALO, cols // LANE + 1
    count = out_ref.shape[1]
    lane = lane_index()
    at_start, at_end = lane == 0, lane == LANE - 1
    load = make_row_loader(whole_ref, left_ref, right_ref)
    state = [None] * SWEEPS

    def at(ref, row, c):
        return ref[row, :, c * LANE:(c + 1) * LANE]

    def advance(sweep, row, tiles):
        before = state[sweep]
        if before is None:
            state[sweep] = (tiles, None)
            return None
        centre, north = before
        south = [at(south_ref, row - 1, c) * (tiles[c] - centre[c]) for c in range(width)]
        state[sweep] = (tiles, south)
        if north is None:
            return None
        ahead, behind = from_east(centre, at_end), from_west(centre, at_start)
        fresh = []
        for c in range(width):
            change = south[c] - north[c]
            if row - 1 < HALO:
                change = change * at(south_ref, height - 1, c)
            if row - 1 >= HALO + rows:
                change = change * at(south_ref, height, c)
            across = at(east_ref, row - 1, c) * ahead[c] + at(west_ref, row - 1, c) * behind[c]
            fresh.append(at(keep_ref, row - 1, c) * centre[c] + across + change)
        return fresh

    half = SWEEPS // 2
    for start, stop in ((0, half), (half, SWEEPS)):
        waiting = [None] * (stop + 1)
        for tick in range(start, height - start + stop - start + 1):
            if waiting[stop] is not None:
                row, tiles = waiting[stop]
                for c in range(width - 1 if stop == SWEEPS else width):
                    if stop == SWEEPS:
                        out_ref[row - HALO, :, c * LANE:(c + 1) * LANE] = tiles[c][:count]
                    else:
                        mid_ref[row, :, c * LANE:(c + 1) * LANE] = tiles[c]
            for sweep in reversed(range(start, stop)):
                entry = waiting[sweep]
                if sweep == start:
                    entry = None
                    if tick < height - start:
                        entry = (tick, [at(mid_ref, tick, c) for c in range(width)] if start else load(tick, slice(begin, begin + SUB)))
                waiting[sweep + 1] = None
                if entry is not None:
                    fresh = advance(sweep, *entry)
                    if fresh is not None:
                        waiting[sweep + 1] = (entry[0] - 1, fresh)


def split_stack(value):
    high = value.astype(jnp.bfloat16).astype(jnp.float32)
    rest = value - high
    middle = rest.astype(jnp.bfloat16).astype(jnp.float32)
    low = rest - middle
    return jnp.concatenate([high, middle, high, low, middle, high], axis=0).astype(jnp.bfloat16)


def corr_kernel(corr_ref, *out_refs, groups, steps, sources):
    mine = lax.axis_index("tm")
    for at in range(groups):
        @pl.when(mine == at)
        def _(at=at):
            for (shift, begin, count), out_ref in zip(sources, out_refs):
                source = (at - shift) % groups * steps + begin
                block = corr_ref[source:source + count, at * steps:(at + 1) * steps]
                high = block.astype(jnp.bfloat16).astype(jnp.float32)
                rest = block - high
                middle = rest.astype(jnp.bfloat16).astype(jnp.float32)
                low = rest - middle
                depth = out_ref.shape[1] // 6
                pad = [jnp.zeros((depth - count, steps), jnp.float32)] if depth > count else []
                stack = []
                for part in (high, high, middle, high, middle, low):
                    stack += [part, *pad]
                out_ref[...] = jnp.concatenate(stack, axis=0).T.astype(jnp.bfloat16)


def mixed_row(row, corr_ref, field_refs):
    parts = []
    for ref in field_refs:
        part = ref[row]
        parts.append(part)
        if -part.shape[0] % SUB:
            parts.append(jnp.zeros((-part.shape[0] % SUB, part.shape[1]), jnp.float32))
    stacked = split_stack(jnp.concatenate(parts, axis=0) if len(parts) > 1 else parts[0])
    return jnp.dot(corr_ref[...], stacked, preferred_element_type=jnp.float32)


def make_mix(first):
    def kernel(*refs):
        *refs, out_ref = refs
        if first:
            corr_ref, *field_refs = refs
        else:
            acc_ref, corr_ref, *field_refs = refs
        for row in range(out_ref.shape[0]):
            total = mixed_row(row, corr_ref, field_refs)
            out_ref[row] = total if first else acc_ref[row] + total

    return kernel


def last_mix_kernel(acc_ref, corr_ref, field_ref, cross_ref, square_ref, steps_ref, grads_ref, out_ref, message_ref, turn_ref, rows_ref):
    _, steps, rows, cols = steps_ref.shape
    slots = turn_ref.shape[0] // (rows * (cols // LANE))
    for row in range(rows):
        total = acc_ref[row] + mixed_row(row, corr_ref, [field_ref])
        for c in range(cols // LANE):
            base = (c * (rows // SUB) + row // SUB) * slots * SUB + row % SUB
            for begin, count in groups_of(steps):
                turn_ref[pl.ds(base + begin * SUB, count, stride=SUB), :] = total[begin:begin + count, c * LANE:(c + 1) * LANE]

    zero = jnp.zeros((SUB, LANE), jnp.float32)

    def body(step, sums):
        sums = list(sums)
        for c in range(cols // LANE):
            for r in range(0, rows, 2 * SUB):
                where = (step, pl.ds(r, 2 * SUB), pl.ds(c * LANE, LANE))
                halves = []
                for part in range(2):
                    base = (c * (rows // SUB) + r // SUB + part) * slots * SUB
                    halves.append(turn_ref[pl.ds(pl.multiple_of(base + step * SUB, SUB), SUB), :])
                mixed = jnp.concatenate(halves, axis=0)
                out_ref[where] = mixed
                half = mixed.astype(jnp.bfloat16).astype(jnp.float32)
                for n in range(NPROJ):
                    source = steps_ref if n < PAIRS else grads_ref
                    product = source[(n % PAIRS, *where)].astype(jnp.float32) * half
                    sums[n] = sums[n] + (product[:SUB] + product[SUB:])
        return tuple(sums)

    sums = lax.fori_loop(0, steps, body, (zero,) * NPROJ, unroll=2)
    rows_ref[0:NSYM, :] = cross_ref[...]
    rows_ref[NSYM:NGRAM, :] = square_ref[...]
    for n in range(NPROJ):
        rows_ref[NGRAM + n:NGRAM + n + 1, :] = jnp.sum(sums[n], axis=0, keepdims=True)
    lane, row = lane_index(), row_index()
    total = zero
    for first in range(0, NROW, SUB):
        summed = jnp.sum(rows_ref[first:first + SUB, :], axis=1, keepdims=True)
        total = total + jnp.where(lane == row + first, summed, 0.0)
    message = jnp.sum(total, axis=0, keepdims=True)
    message_ref[...] = jnp.broadcast_to(message[None], message_ref.shape)


def final_kernel(inbox_ref, mixed_ref, control_ref, steps_ref, grads_ref, out_hbm, out_ref, rows_ref, sems):
    totals = jnp.sum(inbox_ref[...], axis=0)
    lane, row = lane_index(), row_index()
    spread = jnp.broadcast_to(totals, (SUB, LANE))
    for first in range(0, NROW, SUB):
        picked = jnp.where(lane == row + first, spread, 0.0)
        rows_ref[first:first + SUB, :] = jnp.broadcast_to(jnp.sum(picked, axis=1, keepdims=True), (SUB, LANE))

    def entry(k):
        return jnp.broadcast_to(rows_ref[k:k + 1, :], (SUB, LANE))

    cross = {pair: entry(k) for pair, k in WHERE.items()}

    def square(i, j):
        return entry(NSYM + WHERE[(min(i, j), max(i, j))])

    gamma = cross[(PAIRS - 1, PAIRS - 1)] / square(PAIRS - 1, PAIRS - 1)
    pivot = [1.0 / cross[(i, i)] for i in range(PAIRS)]
    first = [None] * PAIRS
    for i in reversed(range(PAIRS)):
        rest = entry(NGRAM + i)
        for j in reversed(range(i + 1, PAIRS)):
            rest = rest - cross[(i, j)] * first[j]
        first[i] = rest * pivot[i]
    second = [None] * PAIRS
    for i in range(PAIRS):
        inner = -entry(NGRAM + PAIRS + i)
        for j in range(PAIRS):
            inner = inner + square(i, j) * first[j]
        rest = cross[(i, i)] * first[i] + gamma * inner
        for j in range(i):
            rest = rest - cross[(j, i)] * second[j]
        second[i] = rest * pivot[i]
    scaled = [gamma * value for value in first]

    _, steps, rows, cols = steps_ref.shape

    def body(step, carry):
        for c in range(0, cols, LANE):
            for r in range(0, rows, 2 * SUB):
                where = (step, pl.ds(r, 2 * SUB), pl.ds(c, LANE))
                mixed = mixed_ref[where]
                control = control_ref[where]
                update = [gamma * mixed[:SUB], gamma * mixed[SUB:]]
                for i in range(PAIRS):
                    s = steps_ref[(i, *where)].astype(jnp.float32)
                    y = grads_ref[(i, *where)].astype(jnp.float32)
                    for part, cut in enumerate((slice(0, SUB), slice(SUB, 2 * SUB))):
                        update[part] = update[part] + (second[i] * s[cut] - scaled[i] * y[cut])
                out_ref[step, pl.ds(r, SUB), pl.ds(c, LANE)] = control[:SUB] - update[0]
                out_ref[step, pl.ds(r + SUB, SUB), pl.ds(c, LANE)] = control[SUB:] - update[1]
        return carry

    copies = []
    for n, (begin, count) in enumerate(groups_of(steps)):
        lax.fori_loop(begin, begin + count, body, 0, unroll=2)
        part = pl.ds(begin, count)
        copies.append(pltpu.make_async_copy(out_ref.at[part], out_hbm.at[part], sems.at[n]))
        copies[-1].start()
    for copy in copies:
        copy.wait()


def matching(firsts, count):
    partner = list(range(count))
    for first in firsts:
        partner[first], partner[(first + 1) % count] = (first + 1) % count, first
    return list(enumerate(partner))


def local(gradient, control, diffusivity, land_mask, time_corr, pair_steps, pair_grads):
    steps, rows, cols = gradient.shape
    height, breadth, groups = (lax.axis_size(axis) for axis in ("lat", "lon", "tm"))
    even = matching(range(0, height - 1, 2), height)
    odd = matching(range(1, height - 1, 2), height)
    evens = matching(range(0, breadth - 1, 2), breadth)
    odds = matching(range(1, breadth, 2), breadth)
    slots = slots_of(steps)
    turn = pltpu.VMEM((rows * (cols // LANE) * slots, LANE), jnp.float32)

    field, to_swap = call(
        pack_kernel,
        (f32(rows, slots, cols), f32(message_rows(steps), cols)),
        [pltpu.with_memory_space_constraint(v, pltpu.HBM) for v in (gradient, land_mask, diffusivity)],
        specs=[HBM] * 3,
        scratch=[
            pltpu.VMEM((steps, rows, cols), jnp.float32), pltpu.VMEM((rows, cols), jnp.int32),
            pltpu.VMEM((rows, cols), jnp.float32), turn, pltpu.SemaphoreType.DMA((2 + len(groups_of(steps)),)),
        ],
        name="pack",
    )
    to_next = call(functools.partial(next_kernel, steps=steps), f32(message_rows(steps), cols), (field,), name="next")
    from_next = lax.ppermute(to_next, "lat", odd)
    from_swap = lax.ppermute(to_swap, "lat", even)
    pair_shape = jax.ShapeDtypeStruct(pair_steps.shape, jnp.bfloat16)
    cross, pair_steps, pair_grads = call(
        cross_kernel, (f32(NSYM, LANE), pair_shape, pair_shape),
        [pltpu.with_memory_space_constraint(v, pltpu.HBM) for v in (pair_steps, pair_grads)], specs=[HBM] * 2,
        scratch=[pltpu.SemaphoreType.DMA((2, 4))],
        name="cross",
    )
    tall, wide = rows + 2 * HALO, cols + LANE
    parts = groups_of(steps)
    sources = [(0, 0, steps)] + [(shift, *part) for part in parts for shift in range(1, groups)]
    own_corr, *corrs = call(
        functools.partial(corr_kernel, groups=groups, steps=steps, sources=sources),
        [jax.ShapeDtypeStruct((steps, 6 * (count + -count % SUB)), jnp.bfloat16) for _, _, count in sources],
        (time_corr,), name="corr",
    )
    side_shape = f32(slots, -(-tall // PER) * LANE)
    whole, to_pair, to_beside = call(
        functools.partial(side_kernel, steps=steps), (f32(tall, slots, cols), side_shape, side_shape), (from_next, field, from_swap, cross), name="sides"
    )
    from_beside = lax.ppermute(to_beside, "lon", odds)
    from_pair = lax.ppermute(to_pair, "lon", evens)
    left, right, *weights = call(
        functools.partial(weight_kernel, steps=steps),
        (side_shape, side_shape, f32(tall + 1, SUB, wide), f32(tall, SUB, wide), f32(tall, SUB, wide), f32(tall, SUB, wide)),
        (whole, from_pair, from_beside),
        scratch=[pltpu.VMEM((-(-tall // SUB) * SUB + SUB, wide), jnp.float32), pltpu.VMEM((4, -(-tall // SUB) * SUB, wide), jnp.float32)],
        name="weights",
    )
    extended = (whole, left, right)
    own, other = [], []
    for begin, count in parts:
        part = call(
            functools.partial(sweep_kernel, begin=begin), f32(rows, count, cols), (*extended, *weights),
            scratch=[pltpu.VMEM((tall, SUB, wide), jnp.float32)], name="sweeps",
        )
        own.append(part)
        for shift in range(1, groups):
            pairs = [(i, (i + shift) % groups) for i in range(groups)]
            other.append(lax.ppermute(part, "tm", pairs))
    mixed = call(make_mix(True), f32(rows, steps, cols), (own_corr, *own), name="mix_own")
    square = call(square_kernel, f32(NSYM, LANE), (pair_grads, mixed), name="square")
    for corr, part in zip(corrs[:-1], other[:-1]):
        mixed = call(make_mix(False), f32(rows, steps, cols), (mixed, corr, part), name="mix_more")
    devices = height * breadth * groups
    mixed, message = call(
        last_mix_kernel, (f32(steps, rows, cols), f32(devices, 1, LANE)),
        (mixed, corrs[-1], other[-1], cross, square, pair_steps, pair_grads),
        scratch=[turn, pltpu.VMEM((NROW, LANE), jnp.float32)], name="mix_last",
    )
    inbox = lax.all_to_all(
        message, ("lat", "lon", "tm"), split_axis=0, concat_axis=0, tiled=True,
        axis_index_groups=[list(reversed(range(devices)))],
    )
    return call(
        final_kernel, pltpu.HBM((steps, rows, cols), jnp.float32), (inbox, mixed, control, pair_steps, pair_grads),
        scratch=[
            pltpu.VMEM((steps, rows, cols), jnp.float32), pltpu.VMEM((NROW, LANE), jnp.float32),
            pltpu.SemaphoreType.DMA((len(parts),)),
        ],
        outs_at=HBM, name="final",
    )


def solution(mesh):
    placed = (
        P("tm", "lat", "lon"),
        P("tm", "lat", "lon"),
        P("lat", "lon"),
        P("lat", "lon"),
        P(),
        P(None, "tm", "lat", "lon"),
        P(None, "tm", "lat", "lon"),
    )
    return jax.shard_map(
        local, mesh=mesh, in_specs=placed, out_specs=P("tm", "lat", "lon"), check_vma=False
    )
```

```python
import functools
import jax
import jax.numpy as jnp
from jax import lax
from jax.experimental import pallas as pl
from jax.experimental.pallas import tpu as pltpu
from jax.sharding import PartitionSpec as P

PAIRS = 8
SWEEPS = 6
SUB = 8
LANE = 128
HALO = SWEEPS
GROUP = 8
PER = LANE // GROUP
CROSS = [(i, j) for i in range(PAIRS) for j in range(i, PAIRS)]
NSYM = len(CROSS)
WHERE = {pair: k for k, pair in enumerate(CROSS)}
NGRAM = 2 * NSYM
NPROJ = 2 * PAIRS
NROW = NGRAM + NPROJ

VMEM = pl.BlockSpec(memory_space=pltpu.VMEM)
HBM = pl.BlockSpec(memory_space=pltpu.HBM)
PARAMS = pltpu.CompilerParams(vmem_limit_bytes=12 * 1024 * 1024)


def f32(*shape):
    return jax.ShapeDtypeStruct(shape, jnp.float32)


def call(kernel, outs, args, specs=None, scratch=(), outs_at=VMEM, name=None):
    single = not isinstance(outs, (tuple, list))
    return pl.pallas_call(
        kernel,
        out_shape=outs,
        in_specs=specs or [VMEM] * len(args),
        out_specs=outs_at if single else [outs_at] * len(outs),
        scratch_shapes=list(scratch),
        compiler_params=PARAMS,
        name=name,
    )(*args)


def lane_index():
    return lax.broadcasted_iota(jnp.int32, (SUB, LANE), 1)


def row_index():
    return lax.broadcasted_iota(jnp.int32, (SUB, LANE), 0)


def product_body(left_ref, right_ref):
    _, _, rows, cols = left_ref.shape

    def body(step, sums):
        sums = list(sums)
        for c in range(0, cols, LANE):
            for r in range(0, rows, 2 * SUB):
                where = (step, pl.ds(r, 2 * SUB), pl.ds(c, LANE))
                right = [right_ref[(i, *where)].astype(jnp.float32) for i in range(PAIRS)]
                left = right
                if left_ref is not right_ref:
                    left = [left_ref[(i, *where)].astype(jnp.float32) for i in range(PAIRS)]
                for part in range(2):
                    cut = slice(part * SUB, (part + 1) * SUB)
                    for k, (i, j) in enumerate(CROSS):
                        sums[k] = sums[k] + left[i][cut] * right[j][cut]
        return tuple(sums)

    return body


def cross_kernel(steps_hbm, grads_hbm, out_ref, steps_ref, grads_ref, sems):
    _, steps, rows, cols = steps_ref.shape
    pieces = 4
    while steps % pieces:
        pieces -= 1
    count = steps // pieces
    copies = []
    for n in range(pieces):
        part = (slice(None), pl.ds(n * count, count))
        copies.append((
            pltpu.make_async_copy(steps_hbm.at[part], steps_ref.at[part], sems.at[0, n]),
            pltpu.make_async_copy(grads_hbm.at[part], grads_ref.at[part], sems.at[1, n]),
        ))
    for pair in copies:
        for copy in pair:
            copy.start()

    sums = (jnp.zeros((SUB, LANE), jnp.float32),) * NSYM
    for n in range(pieces):
        for copy in copies[n]:
            copy.wait()
        sums = lax.fori_loop(n * count, (n + 1) * count, product_body(steps_ref, grads_ref), sums)
    for k in range(NSYM):
        out_ref[k:k + 1, :] = jnp.sum(sums[k], axis=0, keepdims=True)


def square_kernel(grads_ref, order_ref, out_ref):
    steps = grads_ref.shape[1]
    sums = (jnp.zeros((SUB, LANE), jnp.float32),) * NSYM
    sums = lax.fori_loop(0, steps, product_body(grads_ref, grads_ref), sums)
    for k in range(NSYM):
        out_ref[k:k + 1, :] = jnp.sum(sums[k], axis=0, keepdims=True)


def groups_of(steps):
    return [(begin, min(SUB, steps - begin)) for begin in range(0, steps, SUB)]


def slots_of(steps):
    return -(-(steps + 1) // SUB) * SUB


def message_rows(steps):
    return -(-HALO * (steps + 1) // SUB) * SUB


def message_parts(row, steps):
    full = (steps + 1) // SUB * SUB
    rest = steps + 1 - full
    parts = [(slice(row * full, (row + 1) * full), slice(0, full))] if full else []
    if rest:
        start = HALO * full + row * rest
        parts.append((slice(start, start + rest), slice(full, steps + 1)))
    return parts


def pack_kernel(grad_hbm, mask_hbm, diff_hbm, field_ref, swap_ref, grad_ref, mask_ref, diff_ref, turn_ref, sems):
    steps, rows, cols = grad_ref.shape
    slots = field_ref.shape[1]
    pieces = [(begin, min(SUB, steps - begin)) for begin in range(0, steps, SUB)]
    copies = [pltpu.make_async_copy(mask_hbm, mask_ref, sems.at[0]), pltpu.make_async_copy(diff_hbm, diff_ref, sems.at[1])]
    for n, (begin, count) in enumerate(pieces):
        part = pl.ds(begin, count)
        copies.append(pltpu.make_async_copy(grad_hbm.at[part], grad_ref.at[part], sems.at[2 + n]))
    for copy in copies:
        copy.start()
    copies[0].wait()
    copies[1].wait()
    zero = jnp.zeros((SUB, LANE), jnp.float32)
    tiles = [
        (slice(r * SUB, (r + 1) * SUB), slice(c * LANE, (c + 1) * LANE), (c * (rows // SUB) + r) * slots * SUB)
        for c in range(cols // LANE) for r in range(rows // SUB)
    ]
    mask = [mask_ref[down, across].astype(jnp.float32) for down, across, _ in tiles]
    for slot in range(steps, slots):
        for down, across, base in tiles:
            value = diff_ref[down, across] if slot == steps else zero
            turn_ref[base + slot * SUB:base + (slot + 1) * SUB, :] = value
    for n, (begin, count) in enumerate(pieces):
        copies[2 + n].wait()
        for slot in range(begin, begin + count):
            for (down, across, base), keep in zip(tiles, mask):
                turn_ref[base + slot * SUB:base + (slot + 1) * SUB, :] = grad_ref[slot, down, across] * keep
    for c in range(cols // LANE):
        across = slice(c * LANE, (c + 1) * LANE)
        for row in range(rows):
            base = (c * (rows // SUB) + row // SUB) * slots * SUB + row % SUB
            for slot in range(0, slots, SUB):
                value = turn_ref[pl.ds(base + slot * SUB, SUB, stride=SUB), :]
                field_ref[row, slot:slot + SUB, across] = value
    odd = lax.rem(lax.axis_index("lat"), 2)
    near = (1 - odd) * (rows - HALO)
    for row in range(HALO):
        for place, there in message_parts(row, steps):
            swap_ref[place] = field_ref[near + row, there]


def next_kernel(field_ref, next_ref, *, steps):
    far = lax.rem(lax.axis_index("lat"), 2) * (field_ref.shape[0] - HALO)
    for row in range(HALO):
        for place, there in message_parts(row, steps):
            next_ref[place] = field_ref[far + row, there]


def side_kernel(next_ref, field_ref, swap_ref, order_ref, whole_ref, pair_ref, beside_ref, *, steps):
    rows, slots, cols = field_ref.shape
    place, count = lax.axis_index("lat"), lax.axis_size("lat")
    odd = lax.rem(place, 2)
    near, far = (1 - odd) * (HALO + rows), odd * (HALO + rows)
    after = place - 1 + 2 * odd
    bounds = jnp.full((1, cols), place + 1 - 2 * odd, jnp.int32) < count, jnp.full((1, cols), after, jnp.int32)
    inside = bounds[0], (bounds[1] >= 0) & (bounds[1] < count)
    for row in range(HALO):
        for source, target in message_parts(row, steps):
            whole_ref[near + row, target] = jnp.where(inside[0], swap_ref[source], 0.0)
            whole_ref[far + row, target] = jnp.where(inside[1], next_ref[source], 0.0)
        if steps + 1 < slots:
            whole_ref[near + row, steps + 1:] = jnp.zeros((slots - steps - 1, cols), jnp.float32)
            whole_ref[far + row, steps + 1:] = jnp.zeros((slots - steps - 1, cols), jnp.float32)
    for row in range(rows):
        whole_ref[HALO + row] = field_ref[row]
    lane = lane_index()
    uneven = jnp.full((SUB, LANE), lax.rem(lax.axis_index("lon"), 2), jnp.int32) == 1
    for slot in range(0, slots, SUB):
        down = slice(slot, slot + SUB)
        for base in range(0, rows + 2 * HALO, PER):
            west = east = jnp.zeros((SUB, LANE), jnp.float32)
            for row in range(base, min(base + PER, rows + 2 * HALO)):
                begin = (row - base) * GROUP
                here = (lane >= begin) & (lane < begin + GROUP)
                left = whole_ref[row, down, 0:LANE]
                right = whole_ref[row, down, cols - LANE:cols]
                west = jnp.where(here, pltpu.roll(left, begin, 1) if begin else left, west)
                turn = (begin + GROUP) % LANE
                east = jnp.where(here, pltpu.roll(right, turn, 1) if turn else right, east)
            across = slice(base // PER * LANE, (base // PER + 1) * LANE)
            pair_ref[down, across] = jnp.where(uneven, west, east)
            beside_ref[down, across] = jnp.where(uneven, east, west)


def make_row_loader(whole_ref, left_ref, right_ref):
    cols = whole_ref.shape[2]
    lane = lax.broadcasted_iota(jnp.int32, (1, LANE), 1)

    def load(row, down):
        place = slice(row // PER * LANE, (row // PER + 1) * LANE)
        begin = row % PER * GROUP
        tiles = [whole_ref[row, down, c * LANE:(c + 1) * LANE] for c in range(cols // LANE)]
        east, west = right_ref[down, place], left_ref[down, place]
        east = pltpu.roll(east, LANE - begin, 1) if begin else east
        turn = (2 * LANE - GROUP - begin) % LANE
        west = pltpu.roll(west, turn, 1) if turn else west
        return tiles + [jnp.where(lane < LANE // 2, east, west)]

    return load


def from_east(tiles, at_end):
    turned = [pltpu.roll(tile, LANE - 1, 1) for tile in tiles]
    return [jnp.where(at_end, turned[(c + 1) % len(tiles)], turned[c]) for c in range(len(tiles))]


def from_west(tiles, at_start):
    turned = [pltpu.roll(tile, 1, 1) for tile in tiles]
    return [jnp.where(at_start, turned[c - 1], turned[c]) for c in range(len(tiles))]


def weight_kernel(
    whole_ref, pair_ref, beside_ref, left_ref, right_ref, south_ref, east_ref, west_ref, keep_ref, kappa_ref, packed_ref, *, steps
):
    height, _, cols = whole_ref.shape
    uneven = jnp.full(pair_ref.shape, lax.rem(lax.axis_index("lon"), 2), jnp.int32) == 1
    left_ref[...] = jnp.where(uneven, pair_ref[...], beside_ref[...])
    right_ref[...] = jnp.where(uneven, beside_ref[...], pair_ref[...])
    width = cols // LANE + 1
    load = make_row_loader(whole_ref, left_ref, right_ref)
    lane = lane_index()
    at_start, at_end = lane == 0, lane == LANE - 1
    for row in range(height):
        for c, tile in enumerate(load(row, slice(steps, steps + 1))):
            kappa_ref[row:row + 1, c * LANE:(c + 1) * LANE] = tile
    for first in range(0, height, SUB):
        down = slice(first, first + SUB)
        kappa = [kappa_ref[down, c * LANE:(c + 1) * LANE] for c in range(width)]
        below = [kappa_ref[first + 1:first + 1 + SUB, c * LANE:(c + 1) * LANE] for c in range(width)]
        beside = from_east(kappa, at_end)
        east = [0.5 * (kappa[c] + beside[c]) for c in range(width)]
        west = from_west(east, at_start)
        for c in range(width):
            across = slice(c * LANE, (c + 1) * LANE)
            packed_ref[0, down, across] = 0.5 * (kappa[c] + below[c])
            packed_ref[1, down, across] = east[c]
            packed_ref[2, down, across] = west[c]
            packed_ref[3, down, across] = 1.0 - east[c] - west[c]
    for n, ref in enumerate((south_ref, east_ref, west_ref, keep_ref)):
        for row in range(height - 1):
            ref[row] = jnp.broadcast_to(packed_ref[n, row:row + 1, :], ref.shape[1:])
    for side, row in enumerate((HALO - 1, height - HALO)):
        inside = jnp.where(kappa_ref[row:row + 1, :] > 0.0, 1.0, 0.0)
        south_ref[height - 1 + side] = jnp.broadcast_to(inside, south_ref.shape[1:])


def sweep_kernel(whole_ref, left_ref, right_ref, south_ref, east_ref, west_ref, keep_ref, out_ref, *, begin):
    height, _, cols = whole_ref.shape
    rows, width = height - 2 * HALO, cols // LANE + 1
    count = out_ref.shape[1]
    lane = lane_index()
    at_start, at_end = lane == 0, lane == LANE - 1
    load = make_row_loader(whole_ref, left_ref, right_ref)
    state = [None] * SWEEPS

    def at(ref, row, c):
        return ref[row, :, c * LANE:(c + 1) * LANE]

    def advance(sweep, row, tiles):
        before = state[sweep]
        if before is None:
            state[sweep] = (tiles, None)
            return None
        centre, north = before
        south = [at(south_ref, row - 1, c) * (tiles[c] - centre[c]) for c in range(width)]
        state[sweep] = (tiles, south)
        if north is None:
            return None
        ahead, behind = from_east(centre, at_end), from_west(centre, at_start)
        fresh = []
        for c in range(width):
            change = south[c] - north[c]
            if row - 1 < HALO:
                change = change * at(south_ref, height - 1, c)
            if row - 1 >= HALO + rows:
                change = change * at(south_ref, height, c)
            across = at(east_ref, row - 1, c) * ahead[c] + at(west_ref, row - 1, c) * behind[c]
            fresh.append(at(keep_ref, row - 1, c) * centre[c] + across + change)
        return fresh

    waiting = [None] * (SWEEPS + 1)
    for tick in range(height + SWEEPS + 1):
        if waiting[SWEEPS] is not None:
            row, tiles = waiting[SWEEPS]
            for c in range(width - 1):
                out_ref[row - HALO, :, c * LANE:(c + 1) * LANE] = tiles[c][:count]
        for sweep in reversed(range(SWEEPS)):
            if sweep == 0:
                entry = (tick, load(tick, slice(begin, begin + SUB))) if tick < height else None
            else:
                entry = waiting[sweep]
            waiting[sweep + 1] = None
            if entry is not None:
                fresh = advance(sweep, *entry)
                if fresh is not None:
                    waiting[sweep + 1] = (entry[0] - 1, fresh)


def split_stack(value):
    high = value.astype(jnp.bfloat16).astype(jnp.float32)
    rest = value - high
    middle = rest.astype(jnp.bfloat16).astype(jnp.float32)
    low = rest - middle
    return jnp.concatenate([high, middle, high, low, middle, high], axis=0).astype(jnp.bfloat16)


def corr_kernel(corr_ref, *out_refs, groups, steps, sources):
    mine = lax.axis_index("tm")
    for at in range(groups):
        @pl.when(mine == at)
        def _(at=at):
            for (shift, begin, count), out_ref in zip(sources, out_refs):
                source = (at - shift) % groups * steps + begin
                block = corr_ref[source:source + count, at * steps:(at + 1) * steps]
                high = block.astype(jnp.bfloat16).astype(jnp.float32)
                rest = block - high
                middle = rest.astype(jnp.bfloat16).astype(jnp.float32)
                low = rest - middle
                depth = out_ref.shape[1] // 6
                pad = [jnp.zeros((depth - count, steps), jnp.float32)] if depth > count else []
                stack = []
                for part in (high, high, middle, high, middle, low):
                    stack += [part, *pad]
                out_ref[...] = jnp.concatenate(stack, axis=0).T.astype(jnp.bfloat16)


def mixed_row(row, corr_ref, field_refs):
    parts = []
    for ref in field_refs:
        part = ref[row]
        parts.append(part)
        if -part.shape[0] % SUB:
            parts.append(jnp.zeros((-part.shape[0] % SUB, part.shape[1]), jnp.float32))
    stacked = split_stack(jnp.concatenate(parts, axis=0) if len(parts) > 1 else parts[0])
    return jnp.dot(corr_ref[...], stacked, preferred_element_type=jnp.float32)


def make_mix(first):
    def kernel(*refs):
        *refs, out_ref = refs
        if first:
            corr_ref, *field_refs = refs
        else:
            acc_ref, corr_ref, *field_refs = refs
        for row in range(out_ref.shape[0]):
            total = mixed_row(row, corr_ref, field_refs)
            out_ref[row] = total if first else acc_ref[row] + total

    return kernel


def last_mix_kernel(acc_ref, corr_ref, field_ref, cross_ref, square_ref, steps_ref, grads_ref, out_ref, message_ref, turn_ref, rows_ref):
    _, steps, rows, cols = steps_ref.shape
    slots = turn_ref.shape[0] // (rows * (cols // LANE))
    for row in range(rows):
        total = acc_ref[row] + mixed_row(row, corr_ref, [field_ref])
        for c in range(cols // LANE):
            base = (c * (rows // SUB) + row // SUB) * slots * SUB + row % SUB
            for begin, count in groups_of(steps):
                turn_ref[pl.ds(base + begin * SUB, count, stride=SUB), :] = total[begin:begin + count, c * LANE:(c + 1) * LANE]

    zero = jnp.zeros((SUB, LANE), jnp.float32)

    def body(step, sums):
        sums = list(sums)
        for c in range(cols // LANE):
            for r in range(0, rows, 2 * SUB):
                where = (step, pl.ds(r, 2 * SUB), pl.ds(c * LANE, LANE))
                halves = []
                for part in range(2):
                    base = (c * (rows // SUB) + r // SUB + part) * slots * SUB
                    halves.append(turn_ref[pl.ds(pl.multiple_of(base + step * SUB, SUB), SUB), :])
                mixed = jnp.concatenate(halves, axis=0)
                out_ref[where] = mixed
                half = mixed.astype(jnp.bfloat16).astype(jnp.float32)
                for n in range(NPROJ):
                    source = steps_ref if n < PAIRS else grads_ref
                    product = source[(n % PAIRS, *where)].astype(jnp.float32) * half
                    sums[n] = sums[n] + (product[:SUB] + product[SUB:])
        return tuple(sums)

    sums = lax.fori_loop(0, steps, body, (zero,) * NPROJ, unroll=2)
    rows_ref[0:NSYM, :] = cross_ref[...]
    rows_ref[NSYM:NGRAM, :] = square_ref[...]
    for n in range(NPROJ):
        rows_ref[NGRAM + n:NGRAM + n + 1, :] = jnp.sum(sums[n], axis=0, keepdims=True)
    lane, row = lane_index(), row_index()
    total = zero
    for first in range(0, NROW, SUB):
        summed = jnp.sum(rows_ref[first:first + SUB, :], axis=1, keepdims=True)
        total = total + jnp.where(lane == row + first, summed, 0.0)
    message = jnp.sum(total, axis=0, keepdims=True)
    message_ref[...] = jnp.broadcast_to(message[None], message_ref.shape)


def final_kernel(inbox_ref, mixed_ref, control_ref, steps_ref, grads_ref, out_hbm, out_ref, rows_ref, sems):
    totals = jnp.sum(inbox_ref[...], axis=0)
    lane, row = lane_index(), row_index()
    spread = jnp.broadcast_to(totals, (SUB, LANE))
    for first in range(0, NROW, SUB):
        picked = jnp.where(lane == row + first, spread, 0.0)
        rows_ref[first:first + SUB, :] = jnp.broadcast_to(jnp.sum(picked, axis=1, keepdims=True), (SUB, LANE))

    def entry(k):
        return jnp.broadcast_to(rows_ref[k:k + 1, :], (SUB, LANE))

    cross = {pair: entry(k) for pair, k in WHERE.items()}

    def square(i, j):
        return entry(NSYM + WHERE[(min(i, j), max(i, j))])

    gamma = cross[(PAIRS - 1, PAIRS - 1)] / square(PAIRS - 1, PAIRS - 1)
    pivot = [1.0 / cross[(i, i)] for i in range(PAIRS)]
    first = [None] * PAIRS
    for i in reversed(range(PAIRS)):
        rest = entry(NGRAM + i)
        for j in reversed(range(i + 1, PAIRS)):
            rest = rest - cross[(i, j)] * first[j]
        first[i] = rest * pivot[i]
    second = [None] * PAIRS
    for i in range(PAIRS):
        inner = -entry(NGRAM + PAIRS + i)
        for j in range(PAIRS):
            inner = inner + square(i, j) * first[j]
        rest = cross[(i, i)] * first[i] + gamma * inner
        for j in range(i):
            rest = rest - cross[(j, i)] * second[j]
        second[i] = rest * pivot[i]
    scaled = [gamma * value for value in first]

    _, steps, rows, cols = steps_ref.shape

    def body(step, carry):
        for c in range(0, cols, LANE):
            for r in range(0, rows, 2 * SUB):
                where = (step, pl.ds(r, 2 * SUB), pl.ds(c, LANE))
                mixed = mixed_ref[where]
                control = control_ref[where]
                update = [gamma * mixed[:SUB], gamma * mixed[SUB:]]
                for i in range(PAIRS):
                    s = steps_ref[(i, *where)].astype(jnp.float32)
                    y = grads_ref[(i, *where)].astype(jnp.float32)
                    for part, cut in enumerate((slice(0, SUB), slice(SUB, 2 * SUB))):
                        update[part] = update[part] + (second[i] * s[cut] - scaled[i] * y[cut])
                out_ref[step, pl.ds(r, SUB), pl.ds(c, LANE)] = control[:SUB] - update[0]
                out_ref[step, pl.ds(r + SUB, SUB), pl.ds(c, LANE)] = control[SUB:] - update[1]
        return carry

    copies = []
    for n, (begin, count) in enumerate(groups_of(steps)):
        lax.fori_loop(begin, begin + count, body, 0, unroll=2)
        part = pl.ds(begin, count)
        copies.append(pltpu.make_async_copy(out_ref.at[part], out_hbm.at[part], sems.at[n]))
        copies[-1].start()
    for copy in copies:
        copy.wait()


def matching(firsts, count):
    partner = list(range(count))
    for first in firsts:
        partner[first], partner[(first + 1) % count] = (first + 1) % count, first
    return list(enumerate(partner))


def local(gradient, control, diffusivity, land_mask, time_corr, pair_steps, pair_grads):
    steps, rows, cols = gradient.shape
    height, breadth, groups = (lax.axis_size(axis) for axis in ("lat", "lon", "tm"))
    even = matching(range(0, height - 1, 2), height)
    odd = matching(range(1, height - 1, 2), height)
    evens = matching(range(0, breadth - 1, 2), breadth)
    odds = matching(range(1, breadth, 2), breadth)
    slots = slots_of(steps)
    turn = pltpu.VMEM((rows * (cols // LANE) * slots, LANE), jnp.float32)

    field, to_swap = call(
        pack_kernel,
        (f32(rows, slots, cols), f32(message_rows(steps), cols)),
        [pltpu.with_memory_space_constraint(v, pltpu.HBM) for v in (gradient, land_mask, diffusivity)],
        specs=[HBM] * 3,
        scratch=[
            pltpu.VMEM((steps, rows, cols), jnp.float32), pltpu.VMEM((rows, cols), jnp.int32),
            pltpu.VMEM((rows, cols), jnp.float32), turn, pltpu.SemaphoreType.DMA((2 + len(groups_of(steps)),)),
        ],
        name="pack",
    )
    to_next = call(functools.partial(next_kernel, steps=steps), f32(message_rows(steps), cols), (field,), name="next")
    from_next = lax.ppermute(to_next, "lat", odd)
    from_swap = lax.ppermute(to_swap, "lat", even)
    pair_shape = jax.ShapeDtypeStruct(pair_steps.shape, jnp.bfloat16)
    cross, pair_steps, pair_grads = call(
        cross_kernel, (f32(NSYM, LANE), pair_shape, pair_shape),
        [pltpu.with_memory_space_constraint(v, pltpu.HBM) for v in (pair_steps, pair_grads)], specs=[HBM] * 2,
        scratch=[pltpu.SemaphoreType.DMA((2, 4))],
        name="cross",
    )
    tall, wide = rows + 2 * HALO, cols + LANE
    parts = groups_of(steps)
    sources = [(0, 0, steps)] + [(shift, *part) for part in parts for shift in range(1, groups)]
    own_corr, *corrs = call(
        functools.partial(corr_kernel, groups=groups, steps=steps, sources=sources),
        [jax.ShapeDtypeStruct((steps, 6 * (count + -count % SUB)), jnp.bfloat16) for _, _, count in sources],
        (time_corr,), name="corr",
    )
    side_shape = f32(slots, -(-tall // PER) * LANE)
    whole, to_pair, to_beside = call(
        functools.partial(side_kernel, steps=steps), (f32(tall, slots, cols), side_shape, side_shape), (from_next, field, from_swap, cross), name="sides"
    )
    from_beside = lax.ppermute(to_beside, "lon", odds)
    from_pair = lax.ppermute(to_pair, "lon", evens)
    left, right, *weights = call(
        functools.partial(weight_kernel, steps=steps),
        (side_shape, side_shape, f32(tall + 1, SUB, wide), f32(tall, SUB, wide), f32(tall, SUB, wide), f32(tall, SUB, wide)),
        (whole, from_pair, from_beside),
        scratch=[pltpu.VMEM((-(-tall // SUB) * SUB + SUB, wide), jnp.float32), pltpu.VMEM((4, -(-tall // SUB) * SUB, wide), jnp.float32)],
        name="weights",
    )
    extended = (whole, left, right)
    own, other = [], []
    for begin, count in parts:
        part = call(
            functools.partial(sweep_kernel, begin=begin), f32(rows, count, cols), (*extended, *weights), name="sweeps"
        )
        own.append(part)
        for shift in range(1, groups):
            pairs = [(i, (i + shift) % groups) for i in range(groups)]
            other.append(lax.ppermute(part, "tm", pairs))
    mixed = call(make_mix(True), f32(rows, steps, cols), (own_corr, *own), name="mix_own")
    square = call(square_kernel, f32(NSYM, LANE), (pair_grads, mixed), name="square")
    for corr, part in zip(corrs[:-1], other[:-1]):
        mixed = call(make_mix(False), f32(rows, steps, cols), (mixed, corr, part), name="mix_more")
    devices = height * breadth * groups
    mixed, message = call(
        last_mix_kernel, (f32(steps, rows, cols), f32(devices, 1, LANE)),
        (mixed, corrs[-1], other[-1], cross, square, pair_steps, pair_grads),
        scratch=[turn, pltpu.VMEM((NROW, LANE), jnp.float32)], name="mix_last",
    )
    inbox = lax.all_to_all(
        message, ("lat", "lon", "tm"), split_axis=0, concat_axis=0, tiled=True,
        axis_index_groups=[list(reversed(range(devices)))],
    )
    return call(
        final_kernel, pltpu.HBM((steps, rows, cols), jnp.float32), (inbox, mixed, control, pair_steps, pair_grads),
        scratch=[
            pltpu.VMEM((steps, rows, cols), jnp.float32), pltpu.VMEM((NROW, LANE), jnp.float32),
            pltpu.SemaphoreType.DMA((len(parts),)),
        ],
        outs_at=HBM, name="final",
    )


def solution(mesh):
    placed = (
        P("tm", "lat", "lon"),
        P("tm", "lat", "lon"),
        P("lat", "lon"),
        P("lat", "lon"),
        P(),
        P(None, "tm", "lat", "lon"),
        P(None, "tm", "lat", "lon"),
    )
    return jax.shard_map(
        local, mesh=mesh, in_specs=placed, out_specs=P("tm", "lat", "lon"), check_vma=False
    )
```

```python
import functools
import jax
import jax.numpy as jnp
from jax import lax
from jax.experimental import pallas as pl
from jax.experimental.pallas import tpu as pltpu
from jax.sharding import PartitionSpec as P

PAIRS = 8
SWEEPS = 6
SUB = 8
LANE = 128
HALO = SWEEPS
GROUP = 8
PER = LANE // GROUP
CROSS = [(i, j) for i in range(PAIRS) for j in range(i, PAIRS)]
NSYM = len(CROSS)
WHERE = {pair: k for k, pair in enumerate(CROSS)}
NGRAM = 2 * NSYM
NPROJ = 2 * PAIRS
NROW = NGRAM + NPROJ

VMEM = pl.BlockSpec(memory_space=pltpu.VMEM)
HBM = pl.BlockSpec(memory_space=pltpu.HBM)
PARAMS = pltpu.CompilerParams(vmem_limit_bytes=12 * 1024 * 1024)


def f32(*shape):
    return jax.ShapeDtypeStruct(shape, jnp.float32)


def call(kernel, outs, args, specs=None, scratch=(), outs_at=VMEM, name=None):
    single = not isinstance(outs, (tuple, list))
    return pl.pallas_call(
        kernel,
        out_shape=outs,
        in_specs=specs or [VMEM] * len(args),
        out_specs=outs_at if single else [outs_at] * len(outs),
        scratch_shapes=list(scratch),
        compiler_params=PARAMS,
        name=name,
    )(*args)


def lane_index():
    return lax.broadcasted_iota(jnp.int32, (SUB, LANE), 1)


def row_index():
    return lax.broadcasted_iota(jnp.int32, (SUB, LANE), 0)


def product_body(left_ref, right_ref):
    _, _, rows, cols = left_ref.shape

    def body(step, sums):
        sums = list(sums)
        for c in range(0, cols, LANE):
            for r in range(0, rows, 2 * SUB):
                where = (step, pl.ds(r, 2 * SUB), pl.ds(c, LANE))
                right = [right_ref[(i, *where)].astype(jnp.float32) for i in range(PAIRS)]
                left = right
                if left_ref is not right_ref:
                    left = [left_ref[(i, *where)].astype(jnp.float32) for i in range(PAIRS)]
                for part in range(2):
                    cut = slice(part * SUB, (part + 1) * SUB)
                    for k, (i, j) in enumerate(CROSS):
                        sums[k] = sums[k] + left[i][cut] * right[j][cut]
        return tuple(sums)

    return body


def cross_kernel(steps_hbm, grads_hbm, out_ref, steps_ref, grads_ref, sems):
    _, steps, rows, cols = steps_ref.shape
    pieces = 4
    while steps % pieces:
        pieces -= 1
    count = steps // pieces
    copies = []
    for n in range(pieces):
        part = (slice(None), pl.ds(n * count, count))
        copies.append((
            pltpu.make_async_copy(steps_hbm.at[part], steps_ref.at[part], sems.at[0, n]),
            pltpu.make_async_copy(grads_hbm.at[part], grads_ref.at[part], sems.at[1, n]),
        ))
    for pair in copies:
        for copy in pair:
            copy.start()

    sums = (jnp.zeros((SUB, LANE), jnp.float32),) * NSYM
    for n in range(pieces):
        for copy in copies[n]:
            copy.wait()
        sums = lax.fori_loop(n * count, (n + 1) * count, product_body(steps_ref, grads_ref), sums)
    for k in range(NSYM):
        out_ref[k:k + 1, :] = jnp.sum(sums[k], axis=0, keepdims=True)


def square_kernel(grads_ref, order_ref, out_ref):
    steps = grads_ref.shape[1]
    sums = (jnp.zeros((SUB, LANE), jnp.float32),) * NSYM
    sums = lax.fori_loop(0, steps, product_body(grads_ref, grads_ref), sums)
    for k in range(NSYM):
        out_ref[k:k + 1, :] = jnp.sum(sums[k], axis=0, keepdims=True)


def groups_of(steps):
    return [(begin, min(SUB, steps - begin)) for begin in range(0, steps, SUB)]


def slots_of(steps):
    return -(-(steps + 1) // SUB) * SUB


def message_rows(steps):
    return -(-HALO * (steps + 1) // SUB) * SUB


def message_parts(row, steps):
    full = (steps + 1) // SUB * SUB
    rest = steps + 1 - full
    parts = [(slice(row * full, (row + 1) * full), slice(0, full))] if full else []
    if rest:
        start = HALO * full + row * rest
        parts.append((slice(start, start + rest), slice(full, steps + 1)))
    return parts


def pack_kernel(grad_hbm, mask_hbm, diff_hbm, field_ref, swap_ref, grad_ref, mask_ref, diff_ref, turn_ref, sems):
    steps, rows, cols = grad_ref.shape
    slots = field_ref.shape[1]
    pieces = [(begin, min(SUB, steps - begin)) for begin in range(0, steps, SUB)]
    copies = [pltpu.make_async_copy(mask_hbm, mask_ref, sems.at[0]), pltpu.make_async_copy(diff_hbm, diff_ref, sems.at[1])]
    for n, (begin, count) in enumerate(pieces):
        part = pl.ds(begin, count)
        copies.append(pltpu.make_async_copy(grad_hbm.at[part], grad_ref.at[part], sems.at[2 + n]))
    for copy in copies:
        copy.start()
    copies[0].wait()
    copies[1].wait()
    zero = jnp.zeros((SUB, LANE), jnp.float32)
    tiles = [
        (slice(r * SUB, (r + 1) * SUB), slice(c * LANE, (c + 1) * LANE), (c * (rows // SUB) + r) * slots * SUB)
        for c in range(cols // LANE) for r in range(rows // SUB)
    ]
    mask = [mask_ref[down, across].astype(jnp.float32) for down, across, _ in tiles]
    for slot in range(steps, slots):
        for down, across, base in tiles:
            value = diff_ref[down, across] if slot == steps else zero
            turn_ref[base + slot * SUB:base + (slot + 1) * SUB, :] = value
    for n, (begin, count) in enumerate(pieces):
        copies[2 + n].wait()
        for slot in range(begin, begin + count):
            for (down, across, base), keep in zip(tiles, mask):
                turn_ref[base + slot * SUB:base + (slot + 1) * SUB, :] = grad_ref[slot, down, across] * keep
    for c in range(cols // LANE):
        across = slice(c * LANE, (c + 1) * LANE)
        for row in range(rows):
            base = (c * (rows // SUB) + row // SUB) * slots * SUB + row % SUB
            for slot in range(0, slots, SUB):
                value = turn_ref[pl.ds(base + slot * SUB, SUB, stride=SUB), :]
                field_ref[row, slot:slot + SUB, across] = value
    odd = lax.rem(lax.axis_index("lat"), 2)
    near = (1 - odd) * (rows - HALO)
    for row in range(HALO):
        for place, there in message_parts(row, steps):
            swap_ref[place] = field_ref[near + row, there]


def next_kernel(field_ref, next_ref, *, steps):
    far = lax.rem(lax.axis_index("lat"), 2) * (field_ref.shape[0] - HALO)
    for row in range(HALO):
        for place, there in message_parts(row, steps):
            next_ref[place] = field_ref[far + row, there]


def side_kernel(next_ref, field_ref, swap_ref, order_ref, whole_ref, pair_ref, beside_ref, *, steps):
    rows, slots, cols = field_ref.shape
    place, count = lax.axis_index("lat"), lax.axis_size("lat")
    odd = lax.rem(place, 2)
    near, far = (1 - odd) * (HALO + rows), odd * (HALO + rows)
    after = place - 1 + 2 * odd
    bounds = jnp.full((1, cols), place + 1 - 2 * odd, jnp.int32) < count, jnp.full((1, cols), after, jnp.int32)
    inside = bounds[0], (bounds[1] >= 0) & (bounds[1] < count)
    for row in range(HALO):
        for source, target in message_parts(row, steps):
            whole_ref[near + row, target] = jnp.where(inside[0], swap_ref[source], 0.0)
            whole_ref[far + row, target] = jnp.where(inside[1], next_ref[source], 0.0)
        if steps + 1 < slots:
            whole_ref[near + row, steps + 1:] = jnp.zeros((slots - steps - 1, cols), jnp.float32)
            whole_ref[far + row, steps + 1:] = jnp.zeros((slots - steps - 1, cols), jnp.float32)
    for row in range(rows):
        whole_ref[HALO + row] = field_ref[row]
    lane = lane_index()
    uneven = jnp.full((SUB, LANE), lax.rem(lax.axis_index("lon"), 2), jnp.int32) == 1
    for slot in range(0, slots, SUB):
        down = slice(slot, slot + SUB)
        for base in range(0, rows + 2 * HALO, PER):
            west = east = jnp.zeros((SUB, LANE), jnp.float32)
            for row in range(base, min(base + PER, rows + 2 * HALO)):
                begin = (row - base) * GROUP
                here = (lane >= begin) & (lane < begin + GROUP)
                left = whole_ref[row, down, 0:LANE]
                right = whole_ref[row, down, cols - LANE:cols]
                west = jnp.where(here, pltpu.roll(left, begin, 1) if begin else left, west)
                turn = (begin + GROUP) % LANE
                east = jnp.where(here, pltpu.roll(right, turn, 1) if turn else right, east)
            across = slice(base // PER * LANE, (base // PER + 1) * LANE)
            pair_ref[down, across] = jnp.where(uneven, west, east)
            beside_ref[down, across] = jnp.where(uneven, east, west)


def make_row_loader(whole_ref, left_ref, right_ref):
    cols = whole_ref.shape[2]
    lane = lax.broadcasted_iota(jnp.int32, (1, LANE), 1)

    def load(row, down):
        place = slice(row // PER * LANE, (row // PER + 1) * LANE)
        begin = row % PER * GROUP
        tiles = [whole_ref[row, down, c * LANE:(c + 1) * LANE] for c in range(cols // LANE)]
        east, west = right_ref[down, place], left_ref[down, place]
        east = pltpu.roll(east, LANE - begin, 1) if begin else east
        turn = (2 * LANE - GROUP - begin) % LANE
        west = pltpu.roll(west, turn, 1) if turn else west
        return tiles + [jnp.where(lane < LANE // 2, east, west)]

    return load


def from_east(tiles, at_end):
    turned = [pltpu.roll(tile, LANE - 1, 1) for tile in tiles]
    return [jnp.where(at_end, turned[(c + 1) % len(tiles)], turned[c]) for c in range(len(tiles))]


def from_west(tiles, at_start):
    turned = [pltpu.roll(tile, 1, 1) for tile in tiles]
    return [jnp.where(at_start, turned[c - 1], turned[c]) for c in range(len(tiles))]


def weight_kernel(
    whole_ref, pair_ref, beside_ref, left_ref, right_ref, south_ref, east_ref, west_ref, keep_ref, kappa_ref, packed_ref, *, steps
):
    height, _, cols = whole_ref.shape
    uneven = jnp.full(pair_ref.shape, lax.rem(lax.axis_index("lon"), 2), jnp.int32) == 1
    left_ref[...] = jnp.where(uneven, pair_ref[...], beside_ref[...])
    right_ref[...] = jnp.where(uneven, beside_ref[...], pair_ref[...])
    width = cols // LANE + 1
    load = make_row_loader(whole_ref, left_ref, right_ref)
    lane = lane_index()
    at_start, at_end = lane == 0, lane == LANE - 1
    for row in range(height):
        for c, tile in enumerate(load(row, slice(steps, steps + 1))):
            kappa_ref[row:row + 1, c * LANE:(c + 1) * LANE] = tile
    for first in range(0, height, SUB):
        down = slice(first, first + SUB)
        kappa = [kappa_ref[down, c * LANE:(c + 1) * LANE] for c in range(width)]
        below = [kappa_ref[first + 1:first + 1 + SUB, c * LANE:(c + 1) * LANE] for c in range(width)]
        beside = from_east(kappa, at_end)
        east = [0.5 * (kappa[c] + beside[c]) for c in range(width)]
        west = from_west(east, at_start)
        for c in range(width):
            across = slice(c * LANE, (c + 1) * LANE)
            packed_ref[0, down, across] = 0.5 * (kappa[c] + below[c])
            packed_ref[1, down, across] = east[c]
            packed_ref[2, down, across] = west[c]
            packed_ref[3, down, across] = 1.0 - east[c] - west[c]
    for n, ref in enumerate((south_ref, east_ref, west_ref, keep_ref)):
        for row in range(height - 1):
            ref[row] = jnp.broadcast_to(packed_ref[n, row:row + 1, :], ref.shape[1:])
    for side, row in enumerate((HALO - 1, height - HALO)):
        inside = jnp.where(kappa_ref[row:row + 1, :] > 0.0, 1.0, 0.0)
        south_ref[height - 1 + side] = jnp.broadcast_to(inside, south_ref.shape[1:])


def sweep_kernel(whole_ref, left_ref, right_ref, south_ref, east_ref, west_ref, keep_ref, out_ref, *, begin):
    height, _, cols = whole_ref.shape
    rows, width = height - 2 * HALO, cols // LANE + 1
    count = out_ref.shape[1]
    lane = lane_index()
    at_start, at_end = lane == 0, lane == LANE - 1
    load = make_row_loader(whole_ref, left_ref, right_ref)
    state = [None] * SWEEPS

    def at(ref, row, c):
        return ref[row, :, c * LANE:(c + 1) * LANE]

    def advance(sweep, row, tiles):
        before = state[sweep]
        if before is None:
            state[sweep] = (tiles, None)
            return None
        centre, north = before
        south = [at(south_ref, row - 1, c) * (tiles[c] - centre[c]) for c in range(width)]
        state[sweep] = (tiles, south)
        if north is None:
            return None
        ahead, behind = from_east(centre, at_end), from_west(centre, at_start)
        fresh = []
        for c in range(width):
            change = south[c] - north[c]
            if row - 1 < HALO:
                change = change * at(south_ref, height - 1, c)
            if row - 1 >= HALO + rows:
                change = change * at(south_ref, height, c)
            across = at(east_ref, row - 1, c) * ahead[c] + at(west_ref, row - 1, c) * behind[c]
            fresh.append(at(keep_ref, row - 1, c) * centre[c] + across + change)
        return fresh

    waiting = [None] * (SWEEPS + 1)
    for tick in range(height + SWEEPS + 1):
        if waiting[SWEEPS] is not None:
            row, tiles = waiting[SWEEPS]
            for c in range(width - 1):
                out_ref[row - HALO, :, c * LANE:(c + 1) * LANE] = tiles[c][:count]
        for sweep in reversed(range(SWEEPS)):
            if sweep == 0:
                entry = (tick, load(tick, slice(begin, begin + SUB))) if tick < height else None
            else:
                entry = waiting[sweep]
            waiting[sweep + 1] = None
            if entry is not None:
                fresh = advance(sweep, *entry)
                if fresh is not None:
                    waiting[sweep + 1] = (entry[0] - 1, fresh)


def split_stack(value):
    high = value.astype(jnp.bfloat16).astype(jnp.float32)
    rest = value - high
    middle = rest.astype(jnp.bfloat16).astype(jnp.float32)
    low = rest - middle
    return jnp.concatenate([high, middle, high, low, middle, high], axis=0).astype(jnp.bfloat16)


def corr_kernel(corr_ref, *out_refs, groups, steps, sources):
    mine = lax.axis_index("tm")
    for at in range(groups):
        @pl.when(mine == at)
        def _(at=at):
            for (shift, begin, count), out_ref in zip(sources, out_refs):
                source = (at - shift) % groups * steps + begin
                block = corr_ref[source:source + count, at * steps:(at + 1) * steps]
                high = block.astype(jnp.bfloat16).astype(jnp.float32)
                rest = block - high
                middle = rest.astype(jnp.bfloat16).astype(jnp.float32)
                low = rest - middle
                depth = out_ref.shape[1] // 6
                pad = [jnp.zeros((depth - count, steps), jnp.float32)] if depth > count else []
                stack = []
                for part in (high, high, middle, high, middle, low):
                    stack += [part, *pad]
                out_ref[...] = jnp.concatenate(stack, axis=0).T.astype(jnp.bfloat16)


def mixed_row(row, corr_ref, field_refs):
    parts = []
    for ref in field_refs:
        part = ref[row]
        parts.append(part)
        if -part.shape[0] % SUB:
            parts.append(jnp.zeros((-part.shape[0] % SUB, part.shape[1]), jnp.float32))
    stacked = split_stack(jnp.concatenate(parts, axis=0) if len(parts) > 1 else parts[0])
    return jnp.dot(corr_ref[...], stacked, preferred_element_type=jnp.float32)


def make_mix(first):
    def kernel(*refs):
        *refs, out_ref = refs
        if first:
            corr_ref, *field_refs = refs
        else:
            acc_ref, corr_ref, *field_refs = refs
        for row in range(out_ref.shape[0]):
            total = mixed_row(row, corr_ref, field_refs)
            out_ref[row] = total if first else acc_ref[row] + total

    return kernel


def last_mix_kernel(acc_ref, corr_ref, field_ref, cross_ref, square_ref, steps_ref, grads_ref, out_ref, message_ref, turn_ref, rows_ref):
    _, steps, rows, cols = steps_ref.shape
    slots = turn_ref.shape[0] // (rows * (cols // LANE))
    for row in range(rows):
        total = acc_ref[row] + mixed_row(row, corr_ref, [field_ref])
        for c in range(cols // LANE):
            base = (c * (rows // SUB) + row // SUB) * slots * SUB + row % SUB
            for begin, count in groups_of(steps):
                turn_ref[pl.ds(base + begin * SUB, count, stride=SUB), :] = total[begin:begin + count, c * LANE:(c + 1) * LANE]

    zero = jnp.zeros((SUB, LANE), jnp.float32)

    def body(step, sums):
        sums = list(sums)
        for c in range(cols // LANE):
            for r in range(0, rows, 2 * SUB):
                where = (step, pl.ds(r, 2 * SUB), pl.ds(c * LANE, LANE))
                halves = []
                for part in range(2):
                    base = (c * (rows // SUB) + r // SUB + part) * slots * SUB
                    halves.append(turn_ref[pl.ds(pl.multiple_of(base + step * SUB, SUB), SUB), :])
                mixed = jnp.concatenate(halves, axis=0)
                out_ref[where] = mixed
                half = mixed.astype(jnp.bfloat16).astype(jnp.float32)
                for n in range(NPROJ):
                    source = steps_ref if n < PAIRS else grads_ref
                    product = source[(n % PAIRS, *where)].astype(jnp.float32) * half
                    sums[n] = sums[n] + (product[:SUB] + product[SUB:])
        return tuple(sums)

    sums = lax.fori_loop(0, steps, body, (zero,) * NPROJ, unroll=2 if steps % 4 else 4)
    rows_ref[0:NSYM, :] = cross_ref[...]
    rows_ref[NSYM:NGRAM, :] = square_ref[...]
    for n in range(NPROJ):
        rows_ref[NGRAM + n:NGRAM + n + 1, :] = jnp.sum(sums[n], axis=0, keepdims=True)
    lane, row = lane_index(), row_index()
    total = zero
    for first in range(0, NROW, SUB):
        summed = jnp.sum(rows_ref[first:first + SUB, :], axis=1, keepdims=True)
        total = total + jnp.where(lane == row + first, summed, 0.0)
    message = jnp.sum(total, axis=0, keepdims=True)
    message_ref[...] = jnp.broadcast_to(message[None], message_ref.shape)


def final_kernel(inbox_ref, mixed_ref, control_ref, steps_ref, grads_ref, out_hbm, out_ref, rows_ref, sems):
    totals = jnp.sum(inbox_ref[...], axis=0)
    lane, row = lane_index(), row_index()
    spread = jnp.broadcast_to(totals, (SUB, LANE))
    for first in range(0, NROW, SUB):
        picked = jnp.where(lane == row + first, spread, 0.0)
        rows_ref[first:first + SUB, :] = jnp.broadcast_to(jnp.sum(picked, axis=1, keepdims=True), (SUB, LANE))

    def entry(k):
        return jnp.broadcast_to(rows_ref[k:k + 1, :], (SUB, LANE))

    cross = {pair: entry(k) for pair, k in WHERE.items()}

    def square(i, j):
        return entry(NSYM + WHERE[(min(i, j), max(i, j))])

    gamma = cross[(PAIRS - 1, PAIRS - 1)] / square(PAIRS - 1, PAIRS - 1)
    pivot = [1.0 / cross[(i, i)] for i in range(PAIRS)]
    first = [None] * PAIRS
    for i in reversed(range(PAIRS)):
        rest = entry(NGRAM + i)
        for j in reversed(range(i + 1, PAIRS)):
            rest = rest - cross[(i, j)] * first[j]
        first[i] = rest * pivot[i]
    second = [None] * PAIRS
    for i in range(PAIRS):
        inner = -entry(NGRAM + PAIRS + i)
        for j in range(PAIRS):
            inner = inner + square(i, j) * first[j]
        rest = cross[(i, i)] * first[i] + gamma * inner
        for j in range(i):
            rest = rest - cross[(j, i)] * second[j]
        second[i] = rest * pivot[i]
    scaled = [gamma * value for value in first]

    _, steps, rows, cols = steps_ref.shape

    def body(step, carry):
        for c in range(0, cols, LANE):
            for r in range(0, rows, 2 * SUB):
                where = (step, pl.ds(r, 2 * SUB), pl.ds(c, LANE))
                mixed = mixed_ref[where]
                control = control_ref[where]
                update = [gamma * mixed[:SUB], gamma * mixed[SUB:]]
                for i in range(PAIRS):
                    s = steps_ref[(i, *where)].astype(jnp.float32)
                    y = grads_ref[(i, *where)].astype(jnp.float32)
                    for part, cut in enumerate((slice(0, SUB), slice(SUB, 2 * SUB))):
                        update[part] = update[part] + (second[i] * s[cut] - scaled[i] * y[cut])
                out_ref[step, pl.ds(r, SUB), pl.ds(c, LANE)] = control[:SUB] - update[0]
                out_ref[step, pl.ds(r + SUB, SUB), pl.ds(c, LANE)] = control[SUB:] - update[1]
        return carry

    copies = []
    for n, (begin, count) in enumerate(groups_of(steps)):
        lax.fori_loop(begin, begin + count, body, 0, unroll=2 if count % 4 else 4)
        part = pl.ds(begin, count)
        copies.append(pltpu.make_async_copy(out_ref.at[part], out_hbm.at[part], sems.at[n]))
        copies[-1].start()
    for copy in copies:
        copy.wait()


def matching(firsts, count):
    partner = list(range(count))
    for first in firsts:
        partner[first], partner[(first + 1) % count] = (first + 1) % count, first
    return list(enumerate(partner))


def local(gradient, control, diffusivity, land_mask, time_corr, pair_steps, pair_grads):
    steps, rows, cols = gradient.shape
    height, breadth, groups = (lax.axis_size(axis) for axis in ("lat", "lon", "tm"))
    even = matching(range(0, height - 1, 2), height)
    odd = matching(range(1, height - 1, 2), height)
    evens = matching(range(0, breadth - 1, 2), breadth)
    odds = matching(range(1, breadth, 2), breadth)
    slots = slots_of(steps)
    turn = pltpu.VMEM((rows * (cols // LANE) * slots, LANE), jnp.float32)

    field, to_swap = call(
        pack_kernel,
        (f32(rows, slots, cols), f32(message_rows(steps), cols)),
        [pltpu.with_memory_space_constraint(v, pltpu.HBM) for v in (gradient, land_mask, diffusivity)],
        specs=[HBM] * 3,
        scratch=[
            pltpu.VMEM((steps, rows, cols), jnp.float32), pltpu.VMEM((rows, cols), jnp.int32),
            pltpu.VMEM((rows, cols), jnp.float32), turn, pltpu.SemaphoreType.DMA((2 + len(groups_of(steps)),)),
        ],
        name="pack",
    )
    to_next = call(functools.partial(next_kernel, steps=steps), f32(message_rows(steps), cols), (field,), name="next")
    from_next = lax.ppermute(to_next, "lat", odd)
    from_swap = lax.ppermute(to_swap, "lat", even)
    pair_shape = jax.ShapeDtypeStruct(pair_steps.shape, jnp.bfloat16)
    cross, pair_steps, pair_grads = call(
        cross_kernel, (f32(NSYM, LANE), pair_shape, pair_shape),
        [pltpu.with_memory_space_constraint(v, pltpu.HBM) for v in (pair_steps, pair_grads)], specs=[HBM] * 2,
        scratch=[pltpu.SemaphoreType.DMA((2, 4))],
        name="cross",
    )
    tall, wide = rows + 2 * HALO, cols + LANE
    parts = groups_of(steps)
    sources = [(0, 0, steps)] + [(shift, *part) for part in parts for shift in range(1, groups)]
    own_corr, *corrs = call(
        functools.partial(corr_kernel, groups=groups, steps=steps, sources=sources),
        [jax.ShapeDtypeStruct((steps, 6 * (count + -count % SUB)), jnp.bfloat16) for _, _, count in sources],
        (time_corr,), name="corr",
    )
    side_shape = f32(slots, -(-tall // PER) * LANE)
    whole, to_pair, to_beside = call(
        functools.partial(side_kernel, steps=steps), (f32(tall, slots, cols), side_shape, side_shape), (from_next, field, from_swap, cross), name="sides"
    )
    from_beside = lax.ppermute(to_beside, "lon", odds)
    from_pair = lax.ppermute(to_pair, "lon", evens)
    left, right, *weights = call(
        functools.partial(weight_kernel, steps=steps),
        (side_shape, side_shape, f32(tall + 1, SUB, wide), f32(tall, SUB, wide), f32(tall, SUB, wide), f32(tall, SUB, wide)),
        (whole, from_pair, from_beside),
        scratch=[pltpu.VMEM((-(-tall // SUB) * SUB + SUB, wide), jnp.float32), pltpu.VMEM((4, -(-tall // SUB) * SUB, wide), jnp.float32)],
        name="weights",
    )
    extended = (whole, left, right)
    own, other = [], []
    for begin, count in parts:
        part = call(
            functools.partial(sweep_kernel, begin=begin), f32(rows, count, cols), (*extended, *weights), name="sweeps"
        )
        own.append(part)
        for shift in range(1, groups):
            pairs = [(i, (i + shift) % groups) for i in range(groups)]
            other.append(lax.ppermute(part, "tm", pairs))
    mixed = call(make_mix(True), f32(rows, steps, cols), (own_corr, *own), name="mix_own")
    square = call(square_kernel, f32(NSYM, LANE), (pair_grads, mixed), name="square")
    for corr, part in zip(corrs[:-1], other[:-1]):
        mixed = call(make_mix(False), f32(rows, steps, cols), (mixed, corr, part), name="mix_more")
    devices = height * breadth * groups
    mixed, message = call(
        last_mix_kernel, (f32(steps, rows, cols), f32(devices, 1, LANE)),
        (mixed, corrs[-1], other[-1], cross, square, pair_steps, pair_grads),
        scratch=[turn, pltpu.VMEM((NROW, LANE), jnp.float32)], name="mix_last",
    )
    inbox = lax.all_to_all(
        message, ("lat", "lon", "tm"), split_axis=0, concat_axis=0, tiled=True,
        axis_index_groups=[list(reversed(range(devices)))],
    )
    return call(
        final_kernel, pltpu.HBM((steps, rows, cols), jnp.float32), (inbox, mixed, control, pair_steps, pair_grads),
        scratch=[
            pltpu.VMEM((steps, rows, cols), jnp.float32), pltpu.VMEM((NROW, LANE), jnp.float32),
            pltpu.SemaphoreType.DMA((len(parts),)),
        ],
        outs_at=HBM, name="final",
    )


def solution(mesh):
    placed = (
        P("tm", "lat", "lon"),
        P("tm", "lat", "lon"),
        P("lat", "lon"),
        P("lat", "lon"),
        P(),
        P(None, "tm", "lat", "lon"),
        P(None, "tm", "lat", "lon"),
    )
    return jax.shard_map(
        local, mesh=mesh, in_specs=placed, out_specs=P("tm", "lat", "lon"), check_vma=False
    )
```

```python
import functools
import jax
import jax.numpy as jnp
from jax import lax
from jax.experimental import pallas as pl
from jax.experimental.pallas import tpu as pltpu
from jax.sharding import PartitionSpec as P

PAIRS = 8
SWEEPS = 6
SUB = 8
LANE = 128
HALO = SWEEPS
GROUP = 8
PER = LANE // GROUP
CROSS = [(i, j) for i in range(PAIRS) for j in range(i, PAIRS)]
NSYM = len(CROSS)
WHERE = {pair: k for k, pair in enumerate(CROSS)}
NGRAM = 2 * NSYM
NPROJ = 2 * PAIRS
NROW = NGRAM + NPROJ

VMEM = pl.BlockSpec(memory_space=pltpu.VMEM)
HBM = pl.BlockSpec(memory_space=pltpu.HBM)
PARAMS = pltpu.CompilerParams(vmem_limit_bytes=12 * 1024 * 1024)


def f32(*shape):
    return jax.ShapeDtypeStruct(shape, jnp.float32)


def call(kernel, outs, args, specs=None, scratch=(), outs_at=VMEM, name=None):
    single = not isinstance(outs, (tuple, list))
    return pl.pallas_call(
        kernel,
        out_shape=outs,
        in_specs=specs or [VMEM] * len(args),
        out_specs=outs_at if single else [outs_at] * len(outs),
        scratch_shapes=list(scratch),
        compiler_params=PARAMS,
        name=name,
    )(*args)


def lane_index():
    return lax.broadcasted_iota(jnp.int32, (SUB, LANE), 1)


def row_index():
    return lax.broadcasted_iota(jnp.int32, (SUB, LANE), 0)


def product_body(left_ref, right_ref):
    _, _, rows, cols = left_ref.shape

    def body(step, sums):
        sums = list(sums)
        for c in range(0, cols, LANE):
            for r in range(0, rows, 2 * SUB):
                where = (step, pl.ds(r, 2 * SUB), pl.ds(c, LANE))
                right = [right_ref[(i, *where)].astype(jnp.float32) for i in range(PAIRS)]
                left = right
                if left_ref is not right_ref:
                    left = [left_ref[(i, *where)].astype(jnp.float32) for i in range(PAIRS)]
                for part in range(2):
                    cut = slice(part * SUB, (part + 1) * SUB)
                    for k, (i, j) in enumerate(CROSS):
                        sums[k] = sums[k] + left[i][cut] * right[j][cut]
        return tuple(sums)

    return body


def cross_kernel(steps_hbm, grads_hbm, out_ref, steps_ref, grads_ref, sems):
    _, steps, rows, cols = steps_ref.shape
    pieces = 4
    while steps % pieces:
        pieces -= 1
    count = steps // pieces
    copies = []
    for n in range(pieces):
        part = (slice(None), pl.ds(n * count, count))
        copies.append((
            pltpu.make_async_copy(steps_hbm.at[part], steps_ref.at[part], sems.at[0, n]),
            pltpu.make_async_copy(grads_hbm.at[part], grads_ref.at[part], sems.at[1, n]),
        ))
    for pair in copies:
        for copy in pair:
            copy.start()

    sums = (jnp.zeros((SUB, LANE), jnp.float32),) * NSYM
    for n in range(pieces):
        for copy in copies[n]:
            copy.wait()
        sums = lax.fori_loop(n * count, (n + 1) * count, product_body(steps_ref, grads_ref), sums)
    for k in range(NSYM):
        out_ref[k:k + 1, :] = jnp.sum(sums[k], axis=0, keepdims=True)


def square_kernel(grads_ref, order_ref, out_ref):
    steps = grads_ref.shape[1]
    sums = (jnp.zeros((SUB, LANE), jnp.float32),) * NSYM
    sums = lax.fori_loop(0, steps, product_body(grads_ref, grads_ref), sums)
    for k in range(NSYM):
        out_ref[k:k + 1, :] = jnp.sum(sums[k], axis=0, keepdims=True)


def groups_of(steps):
    return [(begin, min(SUB, steps - begin)) for begin in range(0, steps, SUB)]


def slots_of(steps):
    return -(-(steps + 1) // SUB) * SUB


def message_rows(steps):
    return -(-HALO * (steps + 1) // SUB) * SUB


def message_parts(row, steps):
    full = (steps + 1) // SUB * SUB
    rest = steps + 1 - full
    parts = [(slice(row * full, (row + 1) * full), slice(0, full))] if full else []
    if rest:
        start = HALO * full + row * rest
        parts.append((slice(start, start + rest), slice(full, steps + 1)))
    return parts


def pack_kernel(grad_hbm, mask_hbm, diff_hbm, field_ref, swap_ref, grad_ref, mask_ref, diff_ref, turn_ref, sems):
    steps, rows, cols = grad_ref.shape
    slots = field_ref.shape[1]
    pieces = [(begin, min(SUB, steps - begin)) for begin in range(0, steps, SUB)]
    copies = [pltpu.make_async_copy(mask_hbm, mask_ref, sems.at[0]), pltpu.make_async_copy(diff_hbm, diff_ref, sems.at[1])]
    for n, (begin, count) in enumerate(pieces):
        part = pl.ds(begin, count)
        copies.append(pltpu.make_async_copy(grad_hbm.at[part], grad_ref.at[part], sems.at[2 + n]))
    for copy in copies:
        copy.start()
    copies[0].wait()
    copies[1].wait()
    zero = jnp.zeros((SUB, LANE), jnp.float32)
    tiles = [
        (slice(r * SUB, (r + 1) * SUB), slice(c * LANE, (c + 1) * LANE), (c * (rows // SUB) + r) * slots * SUB)
        for c in range(cols // LANE) for r in range(rows // SUB)
    ]
    mask = [mask_ref[down, across].astype(jnp.float32) for down, across, _ in tiles]
    for slot in range(steps, slots):
        for down, across, base in tiles:
            value = diff_ref[down, across] if slot == steps else zero
            turn_ref[base + slot * SUB:base + (slot + 1) * SUB, :] = value
    for n, (begin, count) in enumerate(pieces):
        copies[2 + n].wait()
        for slot in range(begin, begin + count):
            for (down, across, base), keep in zip(tiles, mask):
                turn_ref[base + slot * SUB:base + (slot + 1) * SUB, :] = grad_ref[slot, down, across] * keep
    for c in range(cols // LANE):
        across = slice(c * LANE, (c + 1) * LANE)
        for row in range(rows):
            base = (c * (rows // SUB) + row // SUB) * slots * SUB + row % SUB
            for slot in range(0, slots, SUB):
                value = turn_ref[pl.ds(base + slot * SUB, SUB, stride=SUB), :]
                field_ref[row, slot:slot + SUB, across] = value
    odd = lax.rem(lax.axis_index("lat"), 2)
    near = (1 - odd) * (rows - HALO)
    for row in range(HALO):
        for place, there in message_parts(row, steps):
            swap_ref[place] = field_ref[near + row, there]


def next_kernel(field_ref, next_ref, *, steps):
    far = lax.rem(lax.axis_index("lat"), 2) * (field_ref.shape[0] - HALO)
    for row in range(HALO):
        for place, there in message_parts(row, steps):
            next_ref[place] = field_ref[far + row, there]


def own_side_kernel(field_ref, order_ref, west_ref, east_ref):
    rows, slots, cols = field_ref.shape
    lane = lane_index()
    for slot in range(0, slots, SUB):
        down = slice(slot, slot + SUB)
        for base in range(0, rows + 2 * HALO, PER):
            west = east = jnp.zeros((SUB, LANE), jnp.float32)
            for row in range(max(base, HALO), min(base + PER, rows + HALO)):
                begin = (row - base) * GROUP
                here = (lane >= begin) & (lane < begin + GROUP)
                left = field_ref[row - HALO, down, 0:LANE]
                right = field_ref[row - HALO, down, cols - LANE:cols]
                west = jnp.where(here, pltpu.roll(left, begin, 1) if begin else left, west)
                turn = (begin + GROUP) % LANE
                east = jnp.where(here, pltpu.roll(right, turn, 1) if turn else right, east)
            across = slice(base // PER * LANE, (base // PER + 1) * LANE)
            west_ref[down, across] = west
            east_ref[down, across] = east


def side_kernel(next_ref, field_ref, swap_ref, own_west_ref, own_east_ref, whole_ref, pair_ref, beside_ref, *, steps):
    rows, slots, cols = field_ref.shape
    place, count = lax.axis_index("lat"), lax.axis_size("lat")
    odd = lax.rem(place, 2)
    near, far = (1 - odd) * (HALO + rows), odd * (HALO + rows)
    after = place - 1 + 2 * odd
    bounds = jnp.full((1, cols), place + 1 - 2 * odd, jnp.int32) < count, jnp.full((1, cols), after, jnp.int32)
    inside = bounds[0], (bounds[1] >= 0) & (bounds[1] < count)
    for row in range(HALO):
        for source, target in message_parts(row, steps):
            whole_ref[near + row, target] = jnp.where(inside[0], swap_ref[source], 0.0)
            whole_ref[far + row, target] = jnp.where(inside[1], next_ref[source], 0.0)
        if steps + 1 < slots:
            whole_ref[near + row, steps + 1:] = jnp.zeros((slots - steps - 1, cols), jnp.float32)
            whole_ref[far + row, steps + 1:] = jnp.zeros((slots - steps - 1, cols), jnp.float32)
    for row in range(rows):
        whole_ref[HALO + row] = field_ref[row]
    lane = lane_index()
    uneven = jnp.full((SUB, LANE), lax.rem(lax.axis_index("lon"), 2), jnp.int32) == 1
    for slot in range(0, slots, SUB):
        down = slice(slot, slot + SUB)
        for base in range(0, rows + 2 * HALO, PER):
            across = slice(base // PER * LANE, (base // PER + 1) * LANE)
            west, east = own_west_ref[down, across], own_east_ref[down, across]
            for row in range(base, min(base + PER, rows + 2 * HALO)):
                if HALO <= row < HALO + rows:
                    continue
                begin = (row - base) * GROUP
                here = (lane >= begin) & (lane < begin + GROUP)
                left = whole_ref[row, down, 0:LANE]
                right = whole_ref[row, down, cols - LANE:cols]
                west = jnp.where(here, pltpu.roll(left, begin, 1) if begin else left, west)
                turn = (begin + GROUP) % LANE
                east = jnp.where(here, pltpu.roll(right, turn, 1) if turn else right, east)
            pair_ref[down, across] = jnp.where(uneven, west, east)
            beside_ref[down, across] = jnp.where(uneven, east, west)


def make_row_loader(whole_ref, left_ref, right_ref):
    cols = whole_ref.shape[2]
    lane = lax.broadcasted_iota(jnp.int32, (1, LANE), 1)

    def load(row, down):
        place = slice(row // PER * LANE, (row // PER + 1) * LANE)
        begin = row % PER * GROUP
        tiles = [whole_ref[row, down, c * LANE:(c + 1) * LANE] for c in range(cols // LANE)]
        east, west = right_ref[down, place], left_ref[down, place]
        east = pltpu.roll(east, LANE - begin, 1) if begin else east
        turn = (2 * LANE - GROUP - begin) % LANE
        west = pltpu.roll(west, turn, 1) if turn else west
        return tiles + [jnp.where(lane < LANE // 2, east, west)]

    return load


def from_east(tiles, at_end):
    turned = [pltpu.roll(tile, LANE - 1, 1) for tile in tiles]
    return [jnp.where(at_end, turned[(c + 1) % len(tiles)], turned[c]) for c in range(len(tiles))]


def from_west(tiles, at_start):
    turned = [pltpu.roll(tile, 1, 1) for tile in tiles]
    return [jnp.where(at_start, turned[c - 1], turned[c]) for c in range(len(tiles))]


def weight_kernel(
    whole_ref, pair_ref, beside_ref, left_ref, right_ref, south_ref, east_ref, west_ref, keep_ref, kappa_ref, packed_ref, *, steps
):
    height, _, cols = whole_ref.shape
    uneven = jnp.full(pair_ref.shape, lax.rem(lax.axis_index("lon"), 2), jnp.int32) == 1
    left_ref[...] = jnp.where(uneven, pair_ref[...], beside_ref[...])
    right_ref[...] = jnp.where(uneven, beside_ref[...], pair_ref[...])
    width = cols // LANE + 1
    load = make_row_loader(whole_ref, left_ref, right_ref)
    lane = lane_index()
    at_start, at_end = lane == 0, lane == LANE - 1
    for row in range(height):
        for c, tile in enumerate(load(row, slice(steps, steps + 1))):
            kappa_ref[row:row + 1, c * LANE:(c + 1) * LANE] = tile
    for first in range(0, height, SUB):
        down = slice(first, first + SUB)
        kappa = [kappa_ref[down, c * LANE:(c + 1) * LANE] for c in range(width)]
        below = [kappa_ref[first + 1:first + 1 + SUB, c * LANE:(c + 1) * LANE] for c in range(width)]
        beside = from_east(kappa, at_end)
        east = [0.5 * (kappa[c] + beside[c]) for c in range(width)]
        west = from_west(east, at_start)
        for c in range(width):
            across = slice(c * LANE, (c + 1) * LANE)
            packed_ref[0, down, across] = 0.5 * (kappa[c] + below[c])
            packed_ref[1, down, across] = east[c]
            packed_ref[2, down, across] = west[c]
            packed_ref[3, down, across] = 1.0 - east[c] - west[c]
    for n, ref in enumerate((south_ref, east_ref, west_ref, keep_ref)):
        for row in range(height - 1):
            ref[row] = jnp.broadcast_to(packed_ref[n, row:row + 1, :], ref.shape[1:])
    for side, row in enumerate((HALO - 1, height - HALO)):
        inside = jnp.where(kappa_ref[row:row + 1, :] > 0.0, 1.0, 0.0)
        south_ref[height - 1 + side] = jnp.broadcast_to(inside, south_ref.shape[1:])


def sweep_kernel(whole_ref, left_ref, right_ref, south_ref, east_ref, west_ref, keep_ref, out_ref, *, begin):
    height, _, cols = whole_ref.shape
    rows, width = height - 2 * HALO, cols // LANE + 1
    count = out_ref.shape[1]
    lane = lane_index()
    at_start, at_end = lane == 0, lane == LANE - 1
    load = make_row_loader(whole_ref, left_ref, right_ref)
    state = [None] * SWEEPS

    def at(ref, row, c):
        return ref[row, :, c * LANE:(c + 1) * LANE]

    def advance(sweep, row, tiles):
        before = state[sweep]
        if before is None:
            state[sweep] = (tiles, None)
            return None
        centre, north = before
        south = [at(south_ref, row - 1, c) * (tiles[c] - centre[c]) for c in range(width)]
        state[sweep] = (tiles, south)
        if north is None:
            return None
        ahead, behind = from_east(centre, at_end), from_west(centre, at_start)
        fresh = []
        for c in range(width):
            change = south[c] - north[c]
            if row - 1 < HALO:
                change = change * at(south_ref, height - 1, c)
            if row - 1 >= HALO + rows:
                change = change * at(south_ref, height, c)
            across = at(east_ref, row - 1, c) * ahead[c] + at(west_ref, row - 1, c) * behind[c]
            fresh.append(at(keep_ref, row - 1, c) * centre[c] + across + change)
        return fresh

    waiting = [None] * (SWEEPS + 1)
    for tick in range(height + SWEEPS + 1):
        if waiting[SWEEPS] is not None:
            row, tiles = waiting[SWEEPS]
            for c in range(width - 1):
                out_ref[row - HALO, :, c * LANE:(c + 1) * LANE] = tiles[c][:count]
        for sweep in reversed(range(SWEEPS)):
            if sweep == 0:
                entry = (tick, load(tick, slice(begin, begin + SUB))) if tick < height else None
            else:
                entry = waiting[sweep]
            waiting[sweep + 1] = None
            if entry is not None:
                fresh = advance(sweep, *entry)
                if fresh is not None:
                    waiting[sweep + 1] = (entry[0] - 1, fresh)


def split_stack(value):
    high = value.astype(jnp.bfloat16).astype(jnp.float32)
    rest = value - high
    middle = rest.astype(jnp.bfloat16).astype(jnp.float32)
    low = rest - middle
    return jnp.concatenate([high, middle, high, low, middle, high], axis=0).astype(jnp.bfloat16)


def corr_kernel(corr_ref, *out_refs, groups, steps, sources):
    mine = lax.axis_index("tm")
    for at in range(groups):
        @pl.when(mine == at)
        def _(at=at):
            for (shift, begin, count), out_ref in zip(sources, out_refs):
                source = (at - shift) % groups * steps + begin
                block = corr_ref[source:source + count, at * steps:(at + 1) * steps]
                high = block.astype(jnp.bfloat16).astype(jnp.float32)
                rest = block - high
                middle = rest.astype(jnp.bfloat16).astype(jnp.float32)
                low = rest - middle
                depth = out_ref.shape[1] // 6
                pad = [jnp.zeros((depth - count, steps), jnp.float32)] if depth > count else []
                stack = []
                for part in (high, high, middle, high, middle, low):
                    stack += [part, *pad]
                out_ref[...] = jnp.concatenate(stack, axis=0).T.astype(jnp.bfloat16)


def mixed_row(row, corr_ref, field_refs):
    parts = []
    for ref in field_refs:
        part = ref[row]
        parts.append(part)
        if -part.shape[0] % SUB:
            parts.append(jnp.zeros((-part.shape[0] % SUB, part.shape[1]), jnp.float32))
    stacked = split_stack(jnp.concatenate(parts, axis=0) if len(parts) > 1 else parts[0])
    return jnp.dot(corr_ref[...], stacked, preferred_element_type=jnp.float32)


def make_mix(first):
    def kernel(*refs):
        *refs, out_ref = refs
        if first:
            corr_ref, *field_refs = refs
        else:
            acc_ref, corr_ref, *field_refs = refs
        for row in range(out_ref.shape[0]):
            total = mixed_row(row, corr_ref, field_refs)
            out_ref[row] = total if first else acc_ref[row] + total

    return kernel


def last_mix_kernel(acc_ref, corr_ref, field_ref, cross_ref, square_ref, steps_ref, grads_ref, out_ref, message_ref, turn_ref, rows_ref):
    _, steps, rows, cols = steps_ref.shape
    slots = turn_ref.shape[0] // (rows * (cols // LANE))
    for row in range(rows):
        total = acc_ref[row] + mixed_row(row, corr_ref, [field_ref])
        for c in range(cols // LANE):
            base = (c * (rows // SUB) + row // SUB) * slots * SUB + row % SUB
            for begin, count in groups_of(steps):
                turn_ref[pl.ds(base + begin * SUB, count, stride=SUB), :] = total[begin:begin + count, c * LANE:(c + 1) * LANE]

    zero = jnp.zeros((SUB, LANE), jnp.float32)

    def body(step, sums):
        sums = list(sums)
        for c in range(cols // LANE):
            for r in range(0, rows, 2 * SUB):
                where = (step, pl.ds(r, 2 * SUB), pl.ds(c * LANE, LANE))
                halves = []
                for part in range(2):
                    base = (c * (rows // SUB) + r // SUB + part) * slots * SUB
                    halves.append(turn_ref[pl.ds(pl.multiple_of(base + step * SUB, SUB), SUB), :])
                mixed = jnp.concatenate(halves, axis=0)
                out_ref[where] = mixed
                half = mixed.astype(jnp.bfloat16).astype(jnp.float32)
                for n in range(NPROJ):
                    source = steps_ref if n < PAIRS else grads_ref
                    product = source[(n % PAIRS, *where)].astype(jnp.float32) * half
                    sums[n] = sums[n] + (product[:SUB] + product[SUB:])
        return tuple(sums)

    sums = lax.fori_loop(0, steps, body, (zero,) * NPROJ, unroll=2 if steps % 4 else 4)
    rows_ref[0:NSYM, :] = cross_ref[...]
    rows_ref[NSYM:NGRAM, :] = square_ref[...]
    for n in range(NPROJ):
        rows_ref[NGRAM + n:NGRAM + n + 1, :] = jnp.sum(sums[n], axis=0, keepdims=True)
    lane, row = lane_index(), row_index()
    total = zero
    for first in range(0, NROW, SUB):
        summed = jnp.sum(rows_ref[first:first + SUB, :], axis=1, keepdims=True)
        total = total + jnp.where(lane == row + first, summed, 0.0)
    message = jnp.sum(total, axis=0, keepdims=True)
    message_ref[...] = jnp.broadcast_to(message[None], message_ref.shape)


def final_kernel(inbox_ref, mixed_ref, control_ref, steps_ref, grads_ref, out_hbm, out_ref, rows_ref, sems):
    totals = jnp.sum(inbox_ref[...], axis=0)
    lane, row = lane_index(), row_index()
    spread = jnp.broadcast_to(totals, (SUB, LANE))
    for first in range(0, NROW, SUB):
        picked = jnp.where(lane == row + first, spread, 0.0)
        rows_ref[first:first + SUB, :] = jnp.broadcast_to(jnp.sum(picked, axis=1, keepdims=True), (SUB, LANE))

    def entry(k):
        return jnp.broadcast_to(rows_ref[k:k + 1, :], (SUB, LANE))

    cross = {pair: entry(k) for pair, k in WHERE.items()}

    def square(i, j):
        return entry(NSYM + WHERE[(min(i, j), max(i, j))])

    gamma = cross[(PAIRS - 1, PAIRS - 1)] / square(PAIRS - 1, PAIRS - 1)
    pivot = [1.0 / cross[(i, i)] for i in range(PAIRS)]
    first = [None] * PAIRS
    for i in reversed(range(PAIRS)):
        rest = entry(NGRAM + i)
        for j in reversed(range(i + 1, PAIRS)):
            rest = rest - cross[(i, j)] * first[j]
        first[i] = rest * pivot[i]
    second = [None] * PAIRS
    for i in range(PAIRS):
        inner = -entry(NGRAM + PAIRS + i)
        for j in range(PAIRS):
            inner = inner + square(i, j) * first[j]
        rest = cross[(i, i)] * first[i] + gamma * inner
        for j in range(i):
            rest = rest - cross[(j, i)] * second[j]
        second[i] = rest * pivot[i]
    scaled = [gamma * value for value in first]

    _, steps, rows, cols = steps_ref.shape

    def body(step, carry):
        for c in range(0, cols, LANE):
            for r in range(0, rows, 2 * SUB):
                where = (step, pl.ds(r, 2 * SUB), pl.ds(c, LANE))
                mixed = mixed_ref[where]
                control = control_ref[where]
                update = [gamma * mixed[:SUB], gamma * mixed[SUB:]]
                for i in range(PAIRS):
                    s = steps_ref[(i, *where)].astype(jnp.float32)
                    y = grads_ref[(i, *where)].astype(jnp.float32)
                    for part, cut in enumerate((slice(0, SUB), slice(SUB, 2 * SUB))):
                        update[part] = update[part] + (second[i] * s[cut] - scaled[i] * y[cut])
                out_ref[step, pl.ds(r, SUB), pl.ds(c, LANE)] = control[:SUB] - update[0]
                out_ref[step, pl.ds(r + SUB, SUB), pl.ds(c, LANE)] = control[SUB:] - update[1]
        return carry

    copies = []
    for n, (begin, count) in enumerate(groups_of(steps)):
        lax.fori_loop(begin, begin + count, body, 0, unroll=2 if count % 4 else 4)
        part = pl.ds(begin, count)
        copies.append(pltpu.make_async_copy(out_ref.at[part], out_hbm.at[part], sems.at[n]))
        copies[-1].start()
    for copy in copies:
        copy.wait()


def matching(firsts, count):
    partner = list(range(count))
    for first in firsts:
        partner[first], partner[(first + 1) % count] = (first + 1) % count, first
    return list(enumerate(partner))


def local(gradient, control, diffusivity, land_mask, time_corr, pair_steps, pair_grads):
    steps, rows, cols = gradient.shape
    height, breadth, groups = (lax.axis_size(axis) for axis in ("lat", "lon", "tm"))
    even = matching(range(0, height - 1, 2), height)
    odd = matching(range(1, height - 1, 2), height)
    evens = matching(range(0, breadth - 1, 2), breadth)
    odds = matching(range(1, breadth, 2), breadth)
    slots = slots_of(steps)
    turn = pltpu.VMEM((rows * (cols // LANE) * slots, LANE), jnp.float32)

    field, to_swap = call(
        pack_kernel,
        (f32(rows, slots, cols), f32(message_rows(steps), cols)),
        [pltpu.with_memory_space_constraint(v, pltpu.HBM) for v in (gradient, land_mask, diffusivity)],
        specs=[HBM] * 3,
        scratch=[
            pltpu.VMEM((steps, rows, cols), jnp.float32), pltpu.VMEM((rows, cols), jnp.int32),
            pltpu.VMEM((rows, cols), jnp.float32), turn, pltpu.SemaphoreType.DMA((2 + len(groups_of(steps)),)),
        ],
        name="pack",
    )
    to_next = call(functools.partial(next_kernel, steps=steps), f32(message_rows(steps), cols), (field,), name="next")
    from_next = lax.ppermute(to_next, "lat", odd)
    from_swap = lax.ppermute(to_swap, "lat", even)
    pair_shape = jax.ShapeDtypeStruct(pair_steps.shape, jnp.bfloat16)
    cross, pair_steps, pair_grads = call(
        cross_kernel, (f32(NSYM, LANE), pair_shape, pair_shape),
        [pltpu.with_memory_space_constraint(v, pltpu.HBM) for v in (pair_steps, pair_grads)], specs=[HBM] * 2,
        scratch=[pltpu.SemaphoreType.DMA((2, 4))],
        name="cross",
    )
    tall, wide = rows + 2 * HALO, cols + LANE
    parts = groups_of(steps)
    sources = [(0, 0, steps)] + [(shift, *part) for part in parts for shift in range(1, groups)]
    own_corr, *corrs = call(
        functools.partial(corr_kernel, groups=groups, steps=steps, sources=sources),
        [jax.ShapeDtypeStruct((steps, 6 * (count + -count % SUB)), jnp.bfloat16) for _, _, count in sources],
        (time_corr,), name="corr",
    )
    side_shape = f32(slots, -(-tall // PER) * LANE)
    own_west, own_east = call(own_side_kernel, (side_shape, side_shape), (field, cross), name="own_sides")
    whole, to_pair, to_beside = call(
        functools.partial(side_kernel, steps=steps), (f32(tall, slots, cols), side_shape, side_shape), (from_next, field, from_swap, own_west, own_east), name="sides"
    )
    from_beside = lax.ppermute(to_beside, "lon", odds)
    from_pair = lax.ppermute(to_pair, "lon", evens)
    left, right, *weights = call(
        functools.partial(weight_kernel, steps=steps),
        (side_shape, side_shape, f32(tall + 1, SUB, wide), f32(tall, SUB, wide), f32(tall, SUB, wide), f32(tall, SUB, wide)),
        (whole, from_pair, from_beside),
        scratch=[pltpu.VMEM((-(-tall // SUB) * SUB + SUB, wide), jnp.float32), pltpu.VMEM((4, -(-tall // SUB) * SUB, wide), jnp.float32)],
        name="weights",
    )
    extended = (whole, left, right)
    own, other = [], []
    for begin, count in parts:
        part = call(
            functools.partial(sweep_kernel, begin=begin), f32(rows, count, cols), (*extended, *weights), name="sweeps"
        )
        own.append(part)
        for shift in range(1, groups):
            pairs = [(i, (i + shift) % groups) for i in range(groups)]
            other.append(lax.ppermute(part, "tm", pairs))
    mixed = call(make_mix(True), f32(rows, steps, cols), (own_corr, *own), name="mix_own")
    square = call(square_kernel, f32(NSYM, LANE), (pair_grads, mixed), name="square")
    for corr, part in zip(corrs[:-1], other[:-1]):
        mixed = call(make_mix(False), f32(rows, steps, cols), (mixed, corr, part), name="mix_more")
    devices = height * breadth * groups
    mixed, message = call(
        last_mix_kernel, (f32(steps, rows, cols), f32(devices, 1, LANE)),
        (mixed, corrs[-1], other[-1], cross, square, pair_steps, pair_grads),
        scratch=[turn, pltpu.VMEM((NROW, LANE), jnp.float32)], name="mix_last",
    )
    inbox = lax.all_to_all(
        message, ("lat", "lon", "tm"), split_axis=0, concat_axis=0, tiled=True,
        axis_index_groups=[list(reversed(range(devices)))],
    )
    return call(
        final_kernel, pltpu.HBM((steps, rows, cols), jnp.float32), (inbox, mixed, control, pair_steps, pair_grads),
        scratch=[
            pltpu.VMEM((steps, rows, cols), jnp.float32), pltpu.VMEM((NROW, LANE), jnp.float32),
            pltpu.SemaphoreType.DMA((len(parts),)),
        ],
        outs_at=HBM, name="final",
    )


def solution(mesh):
    placed = (
        P("tm", "lat", "lon"),
        P("tm", "lat", "lon"),
        P("lat", "lon"),
        P("lat", "lon"),
        P(),
        P(None, "tm", "lat", "lon"),
        P(None, "tm", "lat", "lon"),
    )
    return jax.shard_map(
        local, mesh=mesh, in_specs=placed, out_specs=P("tm", "lat", "lon"), check_vma=False
    )
```
